256 devices in a mesh: wide: 16 (over z, core), sum: 16 (over x, y).
Axes of the slice: x: 4, y: 4, z: 8, core: 2. Of those that a mesh axis runs over, the one named last changes fastest.
Arguments:
- field_pos: float32 [3, 98304], P(None, ('wide', 'sum')), may hold values from -6 to 6
- field_vel: float32 [3, 98304], P(None, ('wide', 'sum')), may hold values from -6 to 6
- field_acc: float32 [3, 98304], P(None, ('wide', 'sum')), may hold values from -6 to 6
- field_jerk: float32 [3, 98304], P(None, ('wide', 'sum')), may hold values from -6 to 6
- masses: float32 [98304], P(('wide', 'sum')), may hold values from 2.5431316e-06 to 4.0690105e-05
- levels: int32 [98304], P(('wide', 'sum')), may hold values from 0 to 3
- active_index: int32 [256, 64], P(('wide', 'sum')), may hold values from 0 to 383, as said below
- active_count: int32 [256], P(('wide', 'sum')), may hold values from 1 to 64, as said below
Outputs:
- new_pos: float32 [3, 16384], P(None, ('wide', 'sum'))
- new_vel: float32 [3, 16384], P(None, ('wide', 'sum'))
- new_acc: float32 [3, 16384], P(None, ('wide', 'sum'))
- new_jerk: float32 [3, 16384], P(None, ('wide', 'sum'))
The draws below stay inside these ranges and needn't reach their ends.
Inputs may be any that keep to these rules, and one draw needn't show every extreme that they name: `active_index`: in each owner's row the 64 entries are distinct local indices of that owner's field stars. `active_count`: some owner has all 64 slots live.
All inputs are finite; a program needn't handle non-finite values.
Results may differ from the reference program's by a relative error of at most 0.0003.
Values sent between devices are 32-bit elements; how exact they have to be, the bound alone decides.
A program may use at most 64 MiB of HBM per device.

```python
import math
import jax
import jax.numpy as jnp
from jax import lax

F_DEV = 384
A_CAP = 64
LEVELS = 4
OWNERS = 256
NF = 98304
SLOTS = 16384


def draw_active_index(key, part):
    key = jax.random.fold_in(key, 11)
    keys = jax.random.split(key, OWNERS)

    def one_row(row_key):
        return jax.random.permutation(row_key, F_DEV)[:A_CAP]
    return jax.vmap(one_row)(keys).astype(jnp.int32)


def draw_active_count(key, part):
    key = jax.random.fold_in(key, 23)
    first, second = jax.random.split(key)
    counts = jax.random.randint(first, (OWNERS,), max(1, A_CAP // 8), A_CAP + 1)
    chosen = jax.random.randint(second, (), 0, OWNERS)
    return jnp.where(jnp.arange(OWNERS) == chosen, A_CAP, counts).astype(jnp.int32)


def set_ends(entries, stream_key, least, high):
    longest = entries.shape.index(max(entries.shape))
    spots = []
    for shift in (0, 1):
        where = [jax.random.randint(jax.random.fold_in(stream_key, axis), (), 0, length) for axis, length in enumerate(entries.shape)]
        where[longest] = (where[longest] + shift) % entries.shape[longest]
        spots.append(tuple(where))
    return entries.at[spots[0]].set(least).at[spots[1]].set(high)


def block_levels(rng, shape, cuts, least, largest):
    gain, own = 1.0, jax.random.fold_in(rng, 6)
    for dim, shards_of in cuts:
        heights = jnp.exp(jax.random.uniform(jax.random.fold_in(own, dim), (shards_of,), jnp.float32, least / len(cuts), largest / len(cuts)))
        gain = gain * jnp.repeat(heights, shape[dim] // shards_of).reshape([-1 if axis == dim else 1 for axis in range(len(shape))])
    return gain


def bell_draw(key, extent, width, bound, cuts=(), held_as=jnp.bfloat16):
    result = width * jax.random.normal(key, extent, jnp.float32)
    if cuts:
        result = result * block_levels(key, extent, cuts, -0.22, 0.18)
    return jnp.clip(result, -bound, bound).astype(held_as)


def setup_inputs(seed: int = 0) -> dict:
    seeds = jax.random.split(jax.random.key(seed), 9)
    return {
        "field_pos": bell_draw(seeds[0], (3, NF), 1.0, 6.0, ((1, 256),), jnp.float32),
        "field_vel": bell_draw(seeds[1], (3, NF), 0.5, 6.0, ((1, 256),), jnp.float32),
        "field_acc": bell_draw(seeds[2], (3, NF), 1.0, 6.0, ((1, 256),), jnp.float32),
        "field_jerk": bell_draw(seeds[3], (3, NF), 1.0, 6.0, ((1, 256),), jnp.float32),
        "masses": jnp.clip(jnp.exp(math.log(4.069010537932627e-05) - 2.7725887 * jax.random.uniform(seeds[4], (NF,), jnp.float32) ** block_levels(seeds[4], (NF,), ((0, 256),), -0.2, 0.2)), 2.543131586207892e-06, 4.069010537932627e-05),
        "levels": set_ends(jax.random.randint(seeds[5], (NF,), 0, LEVELS), jax.random.fold_in(seeds[5], 1), 0, LEVELS - 1).astype(jnp.int32),
        "active_index": draw_active_index(jax.random.fold_in(seeds[8], 71), 0),
        "active_count": draw_active_count(jax.random.fold_in(seeds[8], 71), 0),
    }


SOFT2 = 0.0025
STEP0 = 0.5

def predict(field_pos, field_vel, field_acc, field_jerk, levels):
    step_size = STEP0 * jnp.exp2(-levels.astype(jnp.float32))
    pred_pos = field_pos + step_size * (field_vel + step_size * (field_acc / 2 + step_size * field_jerk / 6))
    pred_vel = field_vel + step_size * (field_acc + step_size * field_jerk / 2)
    return (step_size, pred_pos, pred_vel)

def pair_terms(actives, fpos, fvel, fmass):
    offsets = [fpos[c][None, :] - actives[c][:, None] for c in range(3)]
    motions = [fvel[c][None, :] - actives[c + 3][:, None] for c in range(3)]
    dist2 = offsets[0] * offsets[0] + offsets[1] * offsets[1] + offsets[2] * offsets[2] + SOFT2
    inverse = lax.rsqrt(dist2)
    weight = fmass[None, :] * inverse * inverse * inverse
    along = 3.0 * (offsets[0] * motions[0] + offsets[1] * motions[1] + offsets[2] * motions[2]) / dist2
    accel = [lax.optimization_barrier(jnp.sum(weight * offsets[c], axis=1)) for c in range(3)]
    jerks = [lax.optimization_barrier(jnp.sum(weight * (motions[c] - along * offsets[c]), axis=1)) for c in range(3)]
    return jnp.stack(accel + jerks, 0)

def correct(x_old, v_old, a_old, j_old, step, acc_new, jerk_new):
    vel_new = v_old + (a_old + acc_new) * step / 2 + (j_old - jerk_new) * step * step / 12
    pos_new = x_old + (v_old + vel_new) * step / 2 + (a_old - acc_new) * step * step / 12
    return (pos_new, vel_new)

def reference(field_pos, field_vel, field_acc, field_jerk, masses, levels, active_index, active_count):
    step_size, pred_pos, pred_vel = predict(field_pos, field_vel, field_acc, field_jerk, levels)
    owner_ids = jnp.arange(OWNERS, dtype=jnp.int32)[:, None] * F_DEV + active_index
    star_ids = owner_ids.reshape(-1).astype(jnp.int32)
    actives = jnp.concatenate([pred_pos[:, star_ids], pred_vel[:, star_ids]], 0)
    field_blocks = (pred_pos.reshape(3, OWNERS, F_DEV).transpose(1, 0, 2), pred_vel.reshape(3, OWNERS, F_DEV).transpose(1, 0, 2), masses.reshape(OWNERS, F_DEV))

    def per_owner(block):

        def add_block(total, pieces):
            return (total + pair_terms(block, pieces[0], pieces[1], pieces[2]), None)
        total, unused = lax.scan(add_block, jnp.zeros((6, A_CAP), jnp.float32), field_blocks)
        return total
    forces = lax.map(per_owner, actives.reshape(6, OWNERS, A_CAP).transpose(1, 0, 2))
    forces = forces.transpose(1, 0, 2).reshape(6, SLOTS)
    acc_new = forces[:3]
    jerk_new = forces[3:]
    step = step_size[star_ids]
    pos_new, vel_new = correct(field_pos[:, star_ids], field_vel[:, star_ids], field_acc[:, star_ids], field_jerk[:, star_ids], step, acc_new, jerk_new)
    live = (jnp.arange(A_CAP, dtype=jnp.int32)[None, :] < active_count[:, None]).reshape(1, SLOTS)
    zeros = jnp.zeros((3, SLOTS), jnp.float32)
    return (jnp.where(live, pos_new, zeros), jnp.where(live, vel_new, zeros), jnp.where(live, acc_new, zeros), jnp.where(live, jerk_new, zeros))
```

```python
import functools

import jax
import jax.numpy as jnp
from jax import lax
from jax.experimental import pallas as pl
from jax.experimental.pallas import tpu as pltpu
from jax.sharding import PartitionSpec as P

SOFT2 = 0.0025
STEP0 = 0.5
MESH = pl.DeviceIdType.MESH
F32 = jnp.float32
BF16 = jnp.bfloat16
LANES = 128
TILE = 256
STARS = 16
SOURCES = 32
VMEM_LIMIT = 63 * 1024 * 1024


def step_of(levels):
    low = jnp.where(levels == 0, STEP0, STEP0 / 2)
    high = jnp.where(levels == 2, STEP0 / 4, STEP0 / 8)
    return jnp.where(levels < 2, low, high).astype(F32)


def predict(pos, vel, acc, jerk, step):
    pred_pos = pos + step * (vel + step * (acc / 2 + step * jerk / 6))
    pred_vel = vel + step * (acc + step * jerk / 2)
    return pred_pos, pred_vel


def pieces(value):
    first = value.astype(BF16).astype(F32)
    rest = value - first
    second = rest.astype(BF16).astype(F32)
    third = (rest - second).astype(BF16).astype(F32)
    return first, second, third


def source_rows(tile):
    weight = tile[6:7]
    none = jnp.zeros_like(weight)
    sources = jnp.concatenate([weight * tile[0:3], weight, weight * tile[3:6], none], 0)
    return jnp.concatenate(list(pieces(sources)) + [jnp.zeros_like(tile)], 0)


def kernel(
    lines, planes, pos_hbm, vel_hbm, acc_hbm, jerk_hbm, mass_hbm, level_hbm, index_hbm, result,
    pos, vel, acc, jerk, mass, level, index, stage, fields, actives, arrived, partial,
    spread, moments, slot_state, sums, high_low,
    load_sem, field_send, field_recv, active_send, active_recv, part_send, part_recv,
):
    group = 2 * planes
    stars, slots = pos.shape[1], index.shape[1]
    tiles = group * slots // TILE
    share = TILE // slots
    wide, s = lax.axis_index("wide"), lax.axis_index("sum")
    z, core = wide // 2, wide % 2
    me = core * planes + s

    def line_peer(k):
        return (z + 1 + k) % lines

    def plane_peer(k):
        return (me + 1 + k) % group

    def line_id(other):
        return (other * 2 + core, s)

    def plane_id(other):
        return (z * 2 + other // planes, other % planes)

    loads = [
        pltpu.make_async_copy(source, target, load_sem.at[i])
        for i, (source, target) in enumerate(
            zip((pos_hbm, vel_hbm, acc_hbm, jerk_hbm, mass_hbm, level_hbm, index_hbm), (pos, vel, acc, jerk, mass, level, index))
        )
    ]
    for load in loads:
        load.start()

    barrier = pltpu.get_barrier_semaphore()

    def greet_line(k, carry):
        pl.semaphore_signal(barrier, inc=1, device_id=line_id(line_peer(k)), device_id_type=MESH)
        return carry

    def greet_plane(k, carry):
        pl.semaphore_signal(barrier, inc=1, device_id=plane_id(plane_peer(k)), device_id_type=MESH)
        return carry

    lax.fori_loop(0, group - 1, greet_plane, 0)
    lax.fori_loop(0, lines - 1, greet_line, 0)
    for load in loads:
        load.wait()

    step = step_of(level[...].reshape(1, stars))
    pred_pos, pred_vel = predict(pos[...], vel[...], acc[...], jerk[...], step)
    fields[z, 0:3, :] = pred_pos
    fields[z, 3:6, :] = pred_vel
    fields[z, 6:7, :] = mass[...].reshape(1, stars)
    fields[z, 7:8, :] = jnp.zeros_like(step)

    stage[0:3, :] = pos[...]
    stage[3:6, :] = vel[...]
    stage[6:9, :] = acc[...]
    stage[9:12, :] = jerk[...]
    stage[12:13, :] = step
    stage[13:16, :] = jnp.zeros((3, stars), F32)
    chosen = lax.broadcasted_iota(jnp.int32, (stars, slots), 0) == index[...]
    chosen = chosen.astype(F32).astype(BF16)
    picked = [jnp.dot(part.astype(BF16), chosen, preferred_element_type=F32) for part in pieces(stage[...])]
    picked = (picked[0] + picked[1]) + picked[2]
    result[8:24, :] = picked
    slot_pos, slot_vel = predict(picked[0:3], picked[3:6], picked[6:9], picked[9:12], picked[12:13])
    actives[me] = jnp.zeros((8, LANES), F32)
    actives[me, 0:3, 0:slots] = slot_pos
    actives[me, 3:6, 0:slots] = slot_vel

    pl.semaphore_wait(barrier, lines - 1 + group - 1)

    def line_copy(block, other, k):
        return pltpu.make_async_remote_copy(
            src_ref=fields.at[block], dst_ref=fields.at[block],
            send_sem=field_send.at[k], recv_sem=field_recv.at[block],
            device_id=line_id(other), device_id_type=MESH,
        )

    def plane_copy(block, other, k):
        return pltpu.make_async_remote_copy(
            src_ref=actives.at[block], dst_ref=actives.at[block],
            send_sem=active_send.at[k], recv_sem=active_recv.at[block],
            device_id=plane_id(other), device_id_type=MESH,
        )

    def part_copy(pair, slot, other):
        return pltpu.make_async_remote_copy(
            src_ref=partial.at[pair], dst_ref=arrived.at[slot],
            send_sem=part_send.at[other], recv_sem=part_recv.at[slot],
            device_id=plane_id(other), device_id_type=MESH,
        )

    def send_line(k, carry):
        line_copy(z, line_peer(k), k).start()
        return carry

    def send_plane(k, carry):
        plane_copy(me, plane_peer(k), k).start()
        return carry

    lax.fori_loop(0, group - 1, send_plane, 0)
    lax.fori_loop(0, lines - 1, send_line, 0)

    def take_stars(k, block):
        tile = fields[block]
        turned = jnp.concatenate([tile] + [jnp.zeros_like(tile)] * 15, 0).T
        for c in range(6):
            spread[c, k * stars:(k + 1) * stars, :] = jnp.broadcast_to(turned[:, c:c + 1], (stars, LANES))
        moments[:, k * stars:(k + 1) * stars] = source_rows(tile).astype(BF16)

    take_stars(0, z)

    def get_plane(k, carry):
        plane_copy(plane_peer(k), plane_peer(k), k).wait_recv()
        return carry

    lax.fori_loop(0, group - 1, get_plane, 0)

    lane = lax.broadcasted_iota(jnp.int32, (8, LANES), 1)

    def take_slots(i, carry):
        for pair in range(share // 2):
            o = i * share + 2 * pair
            at = pl.ds(pl.multiple_of(i * TILE + pair * LANES, LANES), LANES)
            slot_state[:, at] = jnp.where(lane < slots, actives[o], pltpu.roll(actives[o + 1], slots, 1))
        return carry

    lax.fori_loop(0, tiles, take_slots, 0)

    row = lax.broadcasted_iota(jnp.int32, (8, TILE), 0)
    blocks = 2 * stars // TILE
    rounds = lines // 2

    def weigh(at, state, buffer):
        for sub in range(0, TILE, STARS):
            star = [spread[c, at + sub:at + sub + STARS, :] for c in range(6)]
            star = [jnp.concatenate([value] * (TILE // LANES), 1) for value in star]
            r = [star[c] - state[c] for c in range(3)]
            u = [star[c + 3] - state[c + 3] for c in range(3)]
            q = r[0] * r[0] + r[1] * r[1] + (r[2] * r[2] + SOFT2)
            ru = r[0] * u[0] + r[1] * u[1] + r[2] * u[2]
            inverse = lax.rsqrt(q)
            inverse2 = inverse * inverse
            w = inverse2 * inverse
            sw = (w * inverse2) * ru
            for kind, value in enumerate((w, sw)):
                high = value.astype(BF16)
                high_low[buffer, 2 * kind, sub:sub + STARS, :] = high
                high_low[buffer, 2 * kind + 1, sub:sub + STARS, :] = (value - high.astype(F32)).astype(BF16)

    def gain(at, buffer):
        source = moments[:, at:at + TILE]
        parts = [jnp.dot(source, high_low[buffer, p], preferred_element_type=F32) for p in range(4)]
        return parts[0] + parts[1], parts[2] + parts[3]

    def finish(i):
        by_w, by_s = sums[i, 0], sums[i, 1]
        by_w = by_w[0:8] + by_w[8:16] + by_w[16:24]
        by_s = by_s[0:8] + by_s[8:16] + by_s[16:24]
        terms = by_w + pltpu.roll(jnp.where(row < 4, -3.0 * by_s, 0.0), 4, 0)
        for pair in range(share // 2):
            place = i * (share // 2) + pair
            partial[place] = terms[:, pair * LANES:(pair + 1) * LANES]
            for half in range(2):
                owner = 2 * place + half

                @pl.when(owner != me)
                def _():
                    part_copy(place, me, owner).start()

    def tile_of(j):
        return (me // share + 1 + j) % tiles

    sums[...] = jnp.zeros_like(sums)
    high_low[...] = jnp.zeros_like(high_low)
    for n in range(rounds):
        for k in (2 * n, 2 * n + 1):
            if k:
                block = (z + k) % lines
                line_copy(block, block, 0).wait_recv()
                take_stars(k, block)
        start = n * 2 * stars
        last = start + (blocks - 1) * TILE

        def add(i, terms):
            sums[i, 0] += terms[0]
            sums[i, 1] += terms[1]

        def slot_tile(j, carry, n=n, start=start, last=last, add=add):
            i = tile_of(j)
            before = jnp.where(j > 0, tile_of(j + tiles - 1), tiles)
            cols = pl.ds(pl.multiple_of(i * TILE, TILE), TILE)
            state = [jnp.broadcast_to(slot_state[c:c + 1, cols], (STARS, TILE)) for c in range(6)]
            for b in range(blocks):
                weigh(start + b * TILE, state, b)
                if b == 0:
                    add(before, gain(last, blocks - 1))
                else:
                    add(i, gain(start + (b - 1) * TILE, b - 1))
            if n == rounds - 1:

                @pl.when(j > 0)
                def _():
                    finish(before)

            return carry

        lax.fori_loop(0, tiles, slot_tile, 0)
        add(tile_of(tiles - 1), gain(last, blocks - 1))
        if n == rounds - 1:
            finish(tile_of(tiles - 1))

    arrived[me] = partial[me // 2]

    def end_line(k, carry):
        line_copy(z, line_peer(k), k).wait_send()
        return carry

    def end_plane(k, carry):
        other = plane_peer(k)
        plane_copy(me, other, k).wait_send()
        part_copy(other // 2, me, other).wait_send()
        part_copy(other // 2, other, other).wait_recv()
        return carry

    lax.fori_loop(0, lines - 1, end_line, 0)
    lax.fori_loop(0, group - 1, end_plane, 0)
    terms = jnp.sum(arrived[...], axis=0)
    terms = jnp.where(me % 2 == 0, terms, pltpu.roll(terms, slots, 1))
    result[0:8, :] = terms[:, 0:slots]


def correct_kernel(result, count, pos_hbm, vel_hbm, acc_hbm, jerk_hbm, pos, vel, acc, jerk, store_sem):
    terms, picked = result[0:8, :], result[8:24, :]
    x0, v0, a0, j0, h = picked[0:3], picked[3:6], picked[6:9], picked[9:12], picked[12:13]
    slot_pos, slot_vel = predict(x0, v0, a0, j0, h)
    new_acc = terms[0:3] - slot_pos * terms[3:4]
    new_jerk = terms[4:7] - slot_vel * terms[3:4] - slot_pos * terms[7:8]
    new_vel = v0 + (a0 + new_acc) * h / 2 + (j0 - new_jerk) * h * h / 12
    new_pos = x0 + (v0 + new_vel) * h / 2 + (a0 - new_acc) * h * h / 12
    live = lax.broadcasted_iota(jnp.int32, new_acc.shape, 1) < count[0]
    stores = []
    for i, (value, held, target) in enumerate(
        ((new_acc, acc, acc_hbm), (new_jerk, jerk, jerk_hbm), (new_vel, vel, vel_hbm), (new_pos, pos, pos_hbm))
    ):
        held[...] = jnp.where(live, value, 0.0)
        stores.append(pltpu.make_async_copy(held, target, store_sem.at[i]))
        stores[-1].start()
    for store in stores:
        store.wait()


def body(lines, planes, pos, vel, acc, jerk, masses, levels, index, count):
    stars, slots, group = pos.shape[1], index.shape[1], 2 * planes
    hbm = pl.BlockSpec(memory_space=pl.ANY)
    tiles = group * slots // TILE
    result = pl.pallas_call(
        functools.partial(kernel, lines, planes),
        out_shape=jax.ShapeDtypeStruct((24, slots), F32),
        in_specs=[hbm] * 7,
        out_specs=pl.BlockSpec(memory_space=pltpu.VMEM),
        scratch_shapes=[
            pltpu.VMEM((3, stars), F32),
            pltpu.VMEM((3, stars), F32),
            pltpu.VMEM((3, stars), F32),
            pltpu.VMEM((3, stars), F32),
            pltpu.VMEM((stars,), F32),
            pltpu.VMEM((stars,), jnp.int32),
            pltpu.VMEM((1, slots), jnp.int32),
            pltpu.VMEM((16, stars), F32),
            pltpu.VMEM((lines, 8, stars), F32),
            pltpu.VMEM((group, 8, LANES), F32),
            pltpu.VMEM((group, 8, LANES), F32),
            pltpu.VMEM((group // 2, 8, LANES), F32),
            pltpu.VMEM((6, lines * stars, LANES), F32),
            pltpu.VMEM((SOURCES, lines * stars), BF16),
            pltpu.VMEM((8, group * slots), F32),
            pltpu.VMEM((tiles + 1, 2, SOURCES, TILE), F32),
            pltpu.VMEM((2 * stars // TILE, 4, TILE, TILE), BF16),
            pltpu.SemaphoreType.DMA((7,)),
            pltpu.SemaphoreType.DMA((lines,)),
            pltpu.SemaphoreType.DMA((lines,)),
            pltpu.SemaphoreType.DMA((group,)),
            pltpu.SemaphoreType.DMA((group,)),
            pltpu.SemaphoreType.DMA((group,)),
            pltpu.SemaphoreType.DMA((group,)),
        ],
        compiler_params=pltpu.CompilerParams(collective_id=0, has_side_effects=True, vmem_limit_bytes=VMEM_LIMIT),
        name="forces",
    )(pos, vel, acc, jerk, masses, levels, index)
    three = jax.ShapeDtypeStruct((3, slots), F32)
    return pl.pallas_call(
        correct_kernel,
        out_shape=(three,) * 4,
        in_specs=[pl.BlockSpec(memory_space=pltpu.VMEM), pl.BlockSpec(memory_space=pltpu.SMEM)],
        out_specs=(hbm,) * 4,
        scratch_shapes=[pltpu.VMEM((3, slots), F32)] * 4 + [pltpu.SemaphoreType.DMA((4,))],
        compiler_params=pltpu.CompilerParams(vmem_limit_bytes=VMEM_LIMIT),
        name="correct",
    )(result, count)


def solution(mesh):
    lines, planes = mesh.shape["wide"] // 2, mesh.shape["sum"]
    both = ("wide", "sum")
    in_specs = (P(None, both),) * 4 + (P(both), P(both), P(both, None), P(both))
    return jax.shard_map(
        functools.partial(body, lines, planes), mesh=mesh, in_specs=in_specs,
        out_specs=(P(None, both),) * 4, check_vma=False,
    )
```

```python
import functools

import jax
import jax.numpy as jnp
from jax import lax
from jax.experimental import pallas as pl
from jax.experimental.pallas import tpu as pltpu
from jax.sharding import PartitionSpec as P

SOFT2 = 0.0025
STEP0 = 0.5
MESH = pl.DeviceIdType.MESH
F32 = jnp.float32
BF16 = jnp.bfloat16
LANES = 128
TILE = 256
KDIM = 128
ROWS = 16
VMEM_LIMIT = 63 * 1024 * 1024


def step_of(levels):
    low = jnp.where(levels == 0, STEP0, STEP0 / 2)
    high = jnp.where(levels == 2, STEP0 / 4, STEP0 / 8)
    return jnp.where(levels < 2, low, high).astype(F32)


def predict(pos, vel, acc, jerk, step):
    pred_pos = pos + step * (vel + step * (acc / 2 + step * jerk / 6))
    pred_vel = vel + step * (acc + step * jerk / 2)
    return pred_pos, pred_vel


def pieces(value):
    first = value.astype(BF16).astype(F32)
    rest = value - first
    second = rest.astype(BF16).astype(F32)
    third = (rest - second).astype(BF16).astype(F32)
    return first, second, third


def split_state(tile):
    row = lax.broadcasted_iota(jnp.int32, tile.shape, 0)
    state = jnp.where(row < 6, tile, 0.0)
    grid = jnp.floor(state * 16.0 + 0.5) * 0.0625
    rest = state - grid
    near = rest.astype(BF16).astype(F32)
    far = (rest - near).astype(BF16).astype(F32)
    return grid, near, far


def own_cross(grid, near, far):
    small = near + far
    gp, gv, sp, sv = grid[0:3], grid[3:6], small[0:3], small[3:6]
    cross = jnp.sum(gp * gv, axis=0, keepdims=True)
    rest = jnp.sum(gp * sv + sp * gv + sp * sv, axis=0, keepdims=True)
    return list(pieces(cross)[:2] + pieces(rest))


def slot_rows(tile):
    width = tile.shape[1]
    grid, near, far = split_state(tile)
    none = jnp.zeros((3, width), F32)
    own = jnp.concatenate(own_cross(grid, near, far) + [none], 0)
    other = jnp.concatenate([jnp.ones((5, width), F32), none], 0)
    pad = jnp.zeros((KDIM - 88, width), F32)
    return jnp.concatenate([grid] * 3 + [near] * 3 + [far] * 3 + [own, other, pad], 0)


def star_rows(tile):
    width = tile.shape[1]
    grid, near, far = split_state(tile)
    none = jnp.zeros((3, width), F32)
    crossed = [jnp.concatenate([-part[3:6], -part[0:3], part[6:8]], 0) for part in (grid, near, far)]
    other = jnp.concatenate([jnp.ones((5, width), F32), none], 0)
    own = jnp.concatenate(own_cross(grid, near, far) + [none], 0)
    pad = jnp.zeros((KDIM - 88, width), F32)
    return jnp.concatenate(crossed * 3 + [other, own, pad], 0)


def source_rows(tile):
    weight = tile[6:7]
    none = jnp.zeros_like(weight)
    sources = jnp.concatenate([weight * tile[0:3], weight, weight * tile[3:6], none], 0)
    return jnp.concatenate(list(pieces(sources)) + [jnp.zeros((LANES - 24, tile.shape[1]), F32)], 0)


def kernel(
    lines, planes, pos_hbm, vel_hbm, acc_hbm, jerk_hbm, mass_hbm, level_hbm, index_hbm, result,
    pos, vel, acc, jerk, mass, level, index, stage, fields, actives, arrived, partial,
    spread, left, place_rows, along, moments, cross, high_low, sums,
    load_sem, ready, field_send, field_recv, active_send, active_recv, part_send, part_recv,
):
    group = 2 * planes
    stars, slots = pos.shape[1], index.shape[1]
    tiles = group * slots // TILE
    share = TILE // slots
    wide, s = lax.axis_index("wide"), lax.axis_index("sum")
    z, core = wide // 2, wide % 2
    me = core * planes + s

    def line_peer(k):
        other, bit = z, 1
        while bit < lines:
            other = other + (k // bit) % 2 * bit * (1 - 2 * ((z // bit) % 2))
            bit *= 2
        return other

    def plane_peer(k):
        return (me + 1 + k) % group

    def line_id(other):
        return (other * 2 + core, s)

    def plane_id(other):
        return (z * 2 + other // planes, other % planes)

    loads = [
        pltpu.make_async_copy(source, target, load_sem.at[i])
        for i, (source, target) in enumerate(
            zip((pos_hbm, vel_hbm, acc_hbm, jerk_hbm, mass_hbm, level_hbm, index_hbm), (pos, vel, acc, jerk, mass, level, index))
        )
    ]
    for load in loads:
        load.start()

    barrier = pltpu.get_barrier_semaphore()

    def greet_line(other, carry):
        pl.semaphore_signal(barrier, inc=1, device_id=line_id(other), device_id_type=MESH)
        return carry

    def greet_plane(k, carry):
        pl.semaphore_signal(barrier, inc=1, device_id=plane_id(plane_peer(k)), device_id_type=MESH)
        return carry

    lax.fori_loop(0, group - 1, greet_plane, 0)
    lax.fori_loop(z + 1, lines, greet_line, 0)
    for load in loads:
        load.wait()

    step = step_of(level[...].reshape(1, stars))
    pred_pos, pred_vel = predict(pos[...], vel[...], acc[...], jerk[...], step)
    fields[z, 0:3, :] = pred_pos
    fields[z, 3:6, :] = pred_vel
    fields[z, 6:7, :] = mass[...].reshape(1, stars)
    fields[z, 7:8, :] = jnp.zeros_like(step)

    stage[0:3, :] = pos[...]
    stage[3:6, :] = vel[...]
    stage[6:9, :] = acc[...]
    stage[9:12, :] = jerk[...]
    stage[12:13, :] = step
    stage[13:16, :] = jnp.zeros((3, stars), F32)
    chosen = lax.broadcasted_iota(jnp.int32, (stars, slots), 0) == index[...]
    chosen = chosen.astype(F32).astype(BF16)
    picked = [jnp.dot(part.astype(BF16), chosen, preferred_element_type=F32) for part in pieces(stage[...])]
    picked = (picked[0] + picked[1]) + picked[2]
    result[8:24, :] = picked
    slot_pos, slot_vel = predict(picked[0:3], picked[3:6], picked[6:9], picked[9:12], picked[12:13])
    actives[me] = jnp.zeros((8, LANES), F32)
    actives[me, 0:3, 0:slots] = slot_pos
    actives[me, 3:6, 0:slots] = slot_vel

    pl.semaphore_wait(barrier, group - 1 + z)

    def line_copy(block, other):
        return pltpu.make_async_remote_copy(
            src_ref=fields.at[block], dst_ref=fields.at[block],
            send_sem=field_send.at[other], recv_sem=field_recv.at[block],
            device_id=line_id(other), device_id_type=MESH,
        )

    def plane_copy(block, other, k):
        return pltpu.make_async_remote_copy(
            src_ref=actives.at[block], dst_ref=actives.at[block],
            send_sem=active_send.at[k], recv_sem=active_recv.at[block],
            device_id=plane_id(other), device_id_type=MESH,
        )

    def part_copy(pair, slot, other):
        return pltpu.make_async_remote_copy(
            src_ref=partial.at[pair], dst_ref=arrived.at[slot],
            send_sem=part_send.at[other], recv_sem=part_recv.at[slot],
            device_id=plane_id(other), device_id_type=MESH,
        )

    def send_lower(other, carry):
        pl.semaphore_signal(ready.at[z], inc=1, device_id=line_id(other), device_id_type=MESH)
        line_copy(z, other).start()
        return carry

    def send_higher(other, carry):
        pl.semaphore_wait(ready.at[other], 1)
        line_copy(z, other).start()
        return carry

    def send_plane(k, carry):
        plane_copy(me, plane_peer(k), k).start()
        return carry

    lax.fori_loop(0, group - 1, send_plane, 0)
    lax.fori_loop(0, z, send_lower, 0)

    def take_stars(k, block):
        tile = fields[block]
        at = pl.ds(pl.multiple_of(k * stars, LANES), stars)
        place_rows[:, at] = tile
        along[:, at] = star_rows(tile).astype(BF16)
        turned = source_rows(tile).T.astype(BF16)
        for sub in range(0, stars, LANES):
            first = k * stars + sub
            tall = first // TILE * 2 * TILE + first % TILE
            for part in range(2):
                moments[pl.ds(pl.multiple_of(tall + part * TILE, LANES), LANES), :] = turned[sub:sub + LANES]

    take_stars(0, z)

    def get_plane(k, carry):
        plane_copy(plane_peer(k), plane_peer(k), k).wait_recv()
        return carry

    lax.fori_loop(0, group - 1, get_plane, 0)

    lane = lax.broadcasted_iota(jnp.int32, (8, LANES), 1)

    def take_slots(pair, carry):
        tile = jnp.where(lane < slots, actives[2 * pair], pltpu.roll(actives[2 * pair + 1], slots, 1))
        at = pl.ds(pl.multiple_of(pair * LANES, LANES), LANES)
        left[at, :] = slot_rows(tile).T.astype(BF16)
        turned = jnp.concatenate([tile] + [jnp.zeros_like(tile)] * 15, 0).T
        for c in range(3):
            spread[c, at, :] = jnp.broadcast_to(turned[:, c:c + 1], (LANES, LANES))
        return carry

    lax.fori_loop(0, group // 2, take_slots, 0)

    @pl.when(z % 2 == 0)
    def _():
        send_higher(z + 1, 0)

    line_copy(line_peer(1), line_peer(1)).wait_recv()
    take_stars(1, line_peer(1))

    blocks = 2 * stars // TILE
    rounds = lines // 2

    def stars_of(n, b):
        return pl.ds(pl.multiple_of((n * blocks + b) * TILE, TILE), TILE)

    def get_cross(n, i, b):
        rows = pl.ds(pl.multiple_of(i * TILE, TILE), TILE)
        cross[b] = jnp.dot(left[rows, :], along[:, stars_of(n, b)], preferred_element_type=F32)

    def weigh(n, i, b, side):
        state = [jnp.broadcast_to(place_rows[c:c + 1, stars_of(n, b)], (ROWS, TILE)) for c in range(3)]
        high_at = slice(2 * b * TILE, (2 * b + 1) * TILE)
        low_at = slice((2 * b + 1) * TILE, (2 * b + 2) * TILE)
        for sub in range(0, TILE, ROWS):
            rows = pl.ds(pl.multiple_of(i * TILE + sub, ROWS), ROWS)
            slot = [jnp.concatenate([spread[c, rows, :]] * (TILE // LANES), 1) for c in range(3)]
            r = [state[c] - slot[c] for c in range(3)]
            q = r[0] * r[0] + r[1] * r[1] + (r[2] * r[2] + SOFT2)
            inverse = lax.rsqrt(q)
            inverse2 = inverse * inverse
            w = inverse2 * inverse
            sw = (w * inverse2) * cross[b, sub:sub + ROWS, :]
            for kind, value in enumerate((w, sw)):
                high = value.astype(BF16)
                high_low[side, kind, sub:sub + ROWS, high_at] = high
                high_low[side, kind, sub:sub + ROWS, low_at] = (value - high.astype(F32)).astype(BF16)

    def gain(n, side, kind):
        source = moments[pl.ds(pl.multiple_of(n * 2 * blocks * TILE, TILE), 2 * blocks * TILE), :]
        return jnp.dot(high_low[side, kind], source, preferred_element_type=F32)

    def add(i, by_w, by_s):
        lane = lax.broadcasted_iota(jnp.int32, (TILE, LANES), 1) % 8
        sums[i] += by_w + pltpu.roll(jnp.where(lane < 4, -3.0 * by_s, 0.0), 4, 1)

    def finish(i):
        turned = sums[i].T
        terms = turned[0:8] + turned[8:16] + turned[16:24]
        for pair in range(share // 2):
            place = i * (share // 2) + pair
            partial[place] = terms[:, pair * LANES:(pair + 1) * LANES]
            for half in range(2):
                owner = 2 * place + half

                @pl.when(owner != me)
                def _():
                    part_copy(place, me, owner).start()

    def tile_of(j):
        return (me // share + 1 + j) % tiles

    sums[...] = jnp.zeros_like(sums)

    def pair_round(n, final):
        get_cross(n, tile_of(0), 0)

        def two_tiles(pair, carry):
            for side in range(2):
                j = 2 * pair + side
                i, after = tile_of(j), tile_of(j + 1)
                before = tile_of(j + tiles - 1) if side else jnp.where(j > 0, tile_of(j + tiles - 1), tiles)
                found = []
                for b in range(blocks):
                    if b < blocks - 1:
                        get_cross(n, i, b + 1)
                    else:
                        get_cross(n, after, 0)
                    weigh(n, i, b, side)
                    if b < 2:
                        found.append(gain(n, 1 - side, b))
                add(before, *found)
                if final and side:
                    finish(before)
                elif final:

                    @pl.when(j > 0)
                    def _():
                        finish(before)

            return carry

        lax.fori_loop(0, tiles // 2, two_tiles, 0)
        add(tile_of(tiles - 1), gain(n, 1, 0), gain(n, 1, 1))
        if final:
            finish(tile_of(tiles - 1))

    def early_round(n, carry):
        pair_round(n, False)

        @pl.when(n == 0)
        def _():
            lax.fori_loop(z + 2 - z % 2, lines, send_higher, 0)

        for k in (2 * n + 2, 2 * n + 3):
            block = line_peer(k)
            line_copy(block, block).wait_recv()
            take_stars(k, block)
        return carry

    lax.fori_loop(0, rounds - 1, early_round, 0)
    pair_round(rounds - 1, True)

    arrived[me] = partial[me // 2]

    def end_line(k, carry):
        line_copy(z, line_peer(k + 1)).wait_send()
        return carry

    def end_plane(k, carry):
        other = plane_peer(k)
        plane_copy(me, other, k).wait_send()
        part_copy(other // 2, me, other).wait_send()
        part_copy(other // 2, other, other).wait_recv()
        return carry

    lax.fori_loop(0, lines - 1, end_line, 0)
    lax.fori_loop(0, group - 1, end_plane, 0)
    terms = jnp.sum(arrived[...], axis=0)
    terms = jnp.where(me % 2 == 0, terms, pltpu.roll(terms, slots, 1))
    result[0:8, :] = terms[:, 0:slots]


def correct_kernel(result, count, pos_hbm, vel_hbm, acc_hbm, jerk_hbm, pos, vel, acc, jerk, store_sem):
    terms, picked = result[0:8, :], result[8:24, :]
    x0, v0, a0, j0, h = picked[0:3], picked[3:6], picked[6:9], picked[9:12], picked[12:13]
    slot_pos, slot_vel = predict(x0, v0, a0, j0, h)
    new_acc = terms[0:3] - slot_pos * terms[3:4]
    new_jerk = terms[4:7] - slot_vel * terms[3:4] - slot_pos * terms[7:8]
    new_vel = v0 + (a0 + new_acc) * h / 2 + (j0 - new_jerk) * h * h / 12
    new_pos = x0 + (v0 + new_vel) * h / 2 + (a0 - new_acc) * h * h / 12
    live = lax.broadcasted_iota(jnp.int32, new_acc.shape, 1) < count[0]
    stores = []
    for i, (value, held, target) in enumerate(
        ((new_acc, acc, acc_hbm), (new_jerk, jerk, jerk_hbm), (new_vel, vel, vel_hbm), (new_pos, pos, pos_hbm))
    ):
        held[...] = jnp.where(live, value, 0.0)
        stores.append(pltpu.make_async_copy(held, target, store_sem.at[i]))
        stores[-1].start()
    for store in stores:
        store.wait()


def body(lines, planes, pos, vel, acc, jerk, masses, levels, index, count):
    stars, slots, group = pos.shape[1], index.shape[1], 2 * planes
    hbm = pl.BlockSpec(memory_space=pl.ANY)
    tiles, blocks = group * slots // TILE, 2 * stars // TILE
    result = pl.pallas_call(
        functools.partial(kernel, lines, planes),
        out_shape=jax.ShapeDtypeStruct((24, slots), F32),
        in_specs=[hbm] * 7,
        out_specs=pl.BlockSpec(memory_space=pltpu.VMEM),
        scratch_shapes=[
            pltpu.VMEM((3, stars), F32),
            pltpu.VMEM((3, stars), F32),
            pltpu.VMEM((3, stars), F32),
            pltpu.VMEM((3, stars), F32),
            pltpu.VMEM((stars,), F32),
            pltpu.VMEM((stars,), jnp.int32),
            pltpu.VMEM((1, slots), jnp.int32),
            pltpu.VMEM((16, stars), F32),
            pltpu.VMEM((lines, 8, stars), F32),
            pltpu.VMEM((group, 8, LANES), F32),
            pltpu.VMEM((group, 8, LANES), F32),
            pltpu.VMEM((group // 2, 8, LANES), F32),
            pltpu.VMEM((3, group * slots, LANES), F32),
            pltpu.VMEM((group * slots, KDIM), BF16),
            pltpu.VMEM((8, lines * stars), F32),
            pltpu.VMEM((KDIM, lines * stars), BF16),
            pltpu.VMEM((2 * lines * stars, LANES), BF16),
            pltpu.VMEM((blocks, TILE, TILE), F32),
            pltpu.VMEM((2, 2, TILE, 2 * blocks * TILE), BF16),
            pltpu.VMEM((tiles + 1, TILE, LANES), F32),
            pltpu.SemaphoreType.DMA((7,)),
            pltpu.SemaphoreType.REGULAR((lines,)),
            pltpu.SemaphoreType.DMA((lines,)),
            pltpu.SemaphoreType.DMA((lines,)),
            pltpu.SemaphoreType.DMA((group,)),
            pltpu.SemaphoreType.DMA((group,)),
            pltpu.SemaphoreType.DMA((group,)),
            pltpu.SemaphoreType.DMA((group,)),
        ],
        compiler_params=pltpu.CompilerParams(collective_id=0, has_side_effects=True, vmem_limit_bytes=VMEM_LIMIT),
        name="forces",
    )(pos, vel, acc, jerk, masses, levels, index)
    three = jax.ShapeDtypeStruct((3, slots), F32)
    return pl.pallas_call(
        correct_kernel,
        out_shape=(three,) * 4,
        in_specs=[pl.BlockSpec(memory_space=pltpu.VMEM), pl.BlockSpec(memory_space=pltpu.SMEM)],
        out_specs=(hbm,) * 4,
        scratch_shapes=[pltpu.VMEM((3, slots), F32)] * 4 + [pltpu.SemaphoreType.DMA((4,))],
        compiler_params=pltpu.CompilerParams(vmem_limit_bytes=VMEM_LIMIT),
        name="correct",
    )(result, count)


def solution(mesh):
    lines, planes = mesh.shape["wide"] // 2, mesh.shape["sum"]
    both = ("wide", "sum")
    in_specs = (P(None, both),) * 4 + (P(both), P(both), P(both, None), P(both))
    return jax.shard_map(
        functools.partial(body, lines, planes), mesh=mesh, in_specs=in_specs,
        out_specs=(P(None, both),) * 4, check_vma=False,
    )
```

```python
import functools

import jax
import jax.numpy as jnp
from jax import lax
from jax.experimental import pallas as pl
from jax.experimental.pallas import tpu as pltpu
from jax.sharding import PartitionSpec as P

SOFT2 = 0.0025
STEP0 = 0.5
MESH = pl.DeviceIdType.MESH
F32 = jnp.float32
BF16 = jnp.bfloat16
LANES = 128
TILE = 256
KDIM = 128
ROWS = 16
SOURCES = 32
VMEM_LIMIT = 63 * 1024 * 1024


def step_of(levels):
    low = jnp.where(levels == 0, STEP0, STEP0 / 2)
    high = jnp.where(levels == 2, STEP0 / 4, STEP0 / 8)
    return jnp.where(levels < 2, low, high).astype(F32)


def predict(pos, vel, acc, jerk, step):
    pred_pos = pos + step * (vel + step * (acc / 2 + step * jerk / 6))
    pred_vel = vel + step * (acc + step * jerk / 2)
    return pred_pos, pred_vel


def pieces(value):
    first = value.astype(BF16).astype(F32)
    rest = value - first
    second = rest.astype(BF16).astype(F32)
    third = (rest - second).astype(BF16).astype(F32)
    return first, second, third


def split_state(tile):
    row = lax.broadcasted_iota(jnp.int32, tile.shape, 0)
    state = jnp.where(row < 6, tile, 0.0)
    grid = jnp.floor(state * 16.0 + 0.5) * 0.0625
    rest = state - grid
    near = rest.astype(BF16).astype(F32)
    far = (rest - near).astype(BF16).astype(F32)
    return grid, near, far


def own_cross(grid, near, far):
    small = near + far
    gp, gv, sp, sv = grid[0:3], grid[3:6], small[0:3], small[3:6]
    cross = jnp.sum(gp * gv, axis=0, keepdims=True)
    rest = jnp.sum(gp * sv + sp * gv + sp * sv, axis=0, keepdims=True)
    return list(pieces(cross)[:2] + pieces(rest))


def slot_rows(tile):
    width = tile.shape[1]
    grid, near, far = split_state(tile)
    none = jnp.zeros((3, width), F32)
    own = jnp.concatenate(own_cross(grid, near, far) + [none], 0)
    other = jnp.concatenate([jnp.ones((5, width), F32), none], 0)
    pad = jnp.zeros((KDIM - 88, width), F32)
    return jnp.concatenate([grid] * 3 + [near] * 3 + [far] * 3 + [own, other, pad], 0)


def star_rows(tile):
    width = tile.shape[1]
    grid, near, far = split_state(tile)
    none = jnp.zeros((3, width), F32)
    crossed = [jnp.concatenate([-part[3:6], -part[0:3], part[6:8]], 0) for part in (grid, near, far)]
    other = jnp.concatenate([jnp.ones((5, width), F32), none], 0)
    own = jnp.concatenate(own_cross(grid, near, far) + [none], 0)
    pad = jnp.zeros((KDIM - 88, width), F32)
    return jnp.concatenate(crossed * 3 + [other, own, pad], 0)


def source_rows(tile):
    weight = tile[6:7]
    none = jnp.zeros_like(weight)
    sources = jnp.concatenate([weight * tile[0:3], weight, weight * tile[3:6], none], 0)
    return jnp.concatenate(list(pieces(sources)) + [jnp.zeros((SOURCES - 24, tile.shape[1]), F32)], 0)


def kernel(
    lines, planes, pos_hbm, vel_hbm, acc_hbm, jerk_hbm, mass_hbm, level_hbm, index_hbm, result,
    pos, vel, acc, jerk, mass, level, index, stage, fields, actives, arrived, partial,
    spread, left, place_rows, along, moments, cross, high_low, sums,
    load_sem, ready, field_send, field_recv, active_send, active_recv, part_send, part_recv,
):
    group = 2 * planes
    stars, slots = pos.shape[1], index.shape[1]
    tiles = group * slots // TILE
    share = TILE // slots
    wide, s = lax.axis_index("wide"), lax.axis_index("sum")
    z, core = wide // 2, wide % 2
    me = core * planes + s

    def line_peer(k):
        other, bit = z, 1
        while bit < lines:
            other = other + (k // bit) % 2 * bit * (1 - 2 * ((z // bit) % 2))
            bit *= 2
        return other

    def plane_peer(k):
        return (me + 1 + k) % group

    def line_id(other):
        return (other * 2 + core, s)

    def plane_id(other):
        return (z * 2 + other // planes, other % planes)

    loads = [
        pltpu.make_async_copy(source, target, load_sem.at[i])
        for i, (source, target) in enumerate(
            zip((pos_hbm, vel_hbm, acc_hbm, jerk_hbm, mass_hbm, level_hbm, index_hbm), (pos, vel, acc, jerk, mass, level, index))
        )
    ]
    for load in loads:
        load.start()

    barrier = pltpu.get_barrier_semaphore()

    def greet_line(other, carry):
        pl.semaphore_signal(barrier, inc=1, device_id=line_id(other), device_id_type=MESH)
        return carry

    def greet_plane(k, carry):
        pl.semaphore_signal(barrier, inc=1, device_id=plane_id(plane_peer(k)), device_id_type=MESH)
        return carry

    lax.fori_loop(0, group - 1, greet_plane, 0)
    lax.fori_loop(z + 1, lines, greet_line, 0)
    for load in loads:
        load.wait()

    step = step_of(level[...].reshape(1, stars))
    pred_pos, pred_vel = predict(pos[...], vel[...], acc[...], jerk[...], step)
    fields[z, 0:3, :] = pred_pos
    fields[z, 3:6, :] = pred_vel
    fields[z, 6:7, :] = mass[...].reshape(1, stars)
    fields[z, 7:8, :] = jnp.zeros_like(step)

    stage[0:3, :] = pos[...]
    stage[3:6, :] = vel[...]
    stage[6:9, :] = acc[...]
    stage[9:12, :] = jerk[...]
    stage[12:13, :] = step
    stage[13:16, :] = jnp.zeros((3, stars), F32)
    chosen = lax.broadcasted_iota(jnp.int32, (stars, slots), 0) == index[...]
    chosen = chosen.astype(F32).astype(BF16)
    picked = [jnp.dot(part.astype(BF16), chosen, preferred_element_type=F32) for part in pieces(stage[...])]
    picked = (picked[0] + picked[1]) + picked[2]
    result[8:24, :] = picked
    slot_pos, slot_vel = predict(picked[0:3], picked[3:6], picked[6:9], picked[9:12], picked[12:13])
    actives[me] = jnp.zeros((8, LANES), F32)
    actives[me, 0:3, 0:slots] = slot_pos
    actives[me, 3:6, 0:slots] = slot_vel

    pl.semaphore_wait(barrier, group - 1 + z)

    def line_copy(block, other):
        return pltpu.make_async_remote_copy(
            src_ref=fields.at[block], dst_ref=fields.at[block],
            send_sem=field_send.at[other], recv_sem=field_recv.at[block],
            device_id=line_id(other), device_id_type=MESH,
        )

    def plane_copy(block, other, k):
        return pltpu.make_async_remote_copy(
            src_ref=actives.at[block], dst_ref=actives.at[block],
            send_sem=active_send.at[k], recv_sem=active_recv.at[block],
            device_id=plane_id(other), device_id_type=MESH,
        )

    def part_copy(pair, slot, other):
        return pltpu.make_async_remote_copy(
            src_ref=partial.at[pair], dst_ref=arrived.at[slot],
            send_sem=part_send.at[other], recv_sem=part_recv.at[slot],
            device_id=plane_id(other), device_id_type=MESH,
        )

    def send_lower(other, carry):
        pl.semaphore_signal(ready.at[z], inc=1, device_id=line_id(other), device_id_type=MESH)
        line_copy(z, other).start()
        return carry

    def send_higher(other, carry):
        pl.semaphore_wait(ready.at[other], 1)
        line_copy(z, other).start()
        return carry

    def send_plane(k, carry):
        plane_copy(me, plane_peer(k), k).start()
        return carry

    lax.fori_loop(0, group - 1, send_plane, 0)
    lax.fori_loop(0, z, send_lower, 0)

    def take_stars(k, block):
        tile = fields[block]
        at = pl.ds(pl.multiple_of(k * stars, LANES), stars)
        left[at, :] = star_rows(tile).T.astype(BF16)
        turned = jnp.concatenate([tile] + [jnp.zeros_like(tile)] * 15, 0).T
        for c in range(3):
            spread[c, at, :] = jnp.broadcast_to(turned[:, c:c + 1], (stars, LANES))
        moments[:, at] = source_rows(tile).astype(BF16)

    take_stars(0, z)

    def get_plane(k, carry):
        plane_copy(plane_peer(k), plane_peer(k), k).wait_recv()
        return carry

    lax.fori_loop(0, group - 1, get_plane, 0)

    lane = lax.broadcasted_iota(jnp.int32, (8, LANES), 1)

    def take_slots(pair, carry):
        tile = jnp.where(lane < slots, actives[2 * pair], pltpu.roll(actives[2 * pair + 1], slots, 1))
        at = pl.ds(pl.multiple_of(pair * LANES, LANES), LANES)
        place_rows[:, at] = tile
        along[:, at] = slot_rows(tile).astype(BF16)
        return carry

    lax.fori_loop(0, group // 2, take_slots, 0)

    @pl.when(z % 2 == 0)
    def _():
        send_higher(z + 1, 0)

    line_copy(line_peer(1), line_peer(1)).wait_recv()
    take_stars(1, line_peer(1))

    blocks = 2 * stars // TILE
    rounds = lines // 2

    def stars_of(n, b):
        return pl.ds(pl.multiple_of((n * blocks + b) * TILE, TILE), TILE)

    def slots_of(i):
        return pl.ds(pl.multiple_of(i * TILE, TILE), TILE)

    def get_cross(n, i, b):
        cross[b] = jnp.dot(left[stars_of(n, b), :], along[:, slots_of(i)], preferred_element_type=F32)

    def weigh(n, i, b):
        state = [jnp.broadcast_to(place_rows[c:c + 1, slots_of(i)], (ROWS, TILE)) for c in range(3)]
        for sub in range(0, TILE, ROWS):
            rows = pl.ds(pl.multiple_of((n * blocks + b) * TILE + sub, ROWS), ROWS)
            star = [jnp.concatenate([spread[c, rows, :]] * (TILE // LANES), 1) for c in range(3)]
            r = [star[c] - state[c] for c in range(3)]
            q = r[0] * r[0] + r[1] * r[1] + (r[2] * r[2] + SOFT2)
            inverse = lax.rsqrt(q)
            inverse2 = inverse * inverse
            w = inverse2 * inverse
            sw = (w * inverse2) * cross[b, sub:sub + ROWS, :]
            for kind, value in enumerate((w, sw)):
                high = value.astype(BF16)
                high_low[b, kind, sub:sub + ROWS, :] = high
                high_low[b, kind, TILE + sub:TILE + sub + ROWS, :] = (value - high.astype(F32)).astype(BF16)

    def gain(n, i, b):
        source = moments[:, stars_of(n, b)]
        source = jnp.concatenate([source, source], 1)
        for kind in range(2):
            sums[i, kind] += jnp.dot(source, high_low[b, kind], preferred_element_type=F32)

    def finish(i):
        by_w, by_s = sums[i, 0], sums[i, 1]
        by_w = by_w[0:8] + by_w[8:16] + by_w[16:24]
        by_s = by_s[0:8] + by_s[8:16] + by_s[16:24]
        row = lax.broadcasted_iota(jnp.int32, by_s.shape, 0)
        terms = by_w + pltpu.roll(jnp.where(row < 4, -3.0 * by_s, 0.0), 4, 0)
        for pair in range(share // 2):
            place = i * (share // 2) + pair
            partial[place] = terms[:, pair * LANES:(pair + 1) * LANES]
            for half in range(2):
                owner = 2 * place + half

                @pl.when(owner != me)
                def _():
                    part_copy(place, me, owner).start()

    def tile_of(j):
        return (me // share + 1 + j) % tiles

    sums[...] = jnp.zeros_like(sums)

    def pair_round(n, final):
        get_cross(n, tile_of(0), 0)

        def slot_tile(j, carry):
            i = tile_of(j)
            before = jnp.where(j > 0, tile_of(j + tiles - 1), tiles)
            for b in range(blocks):
                if b < blocks - 1:
                    get_cross(n, i, b + 1)
                else:
                    get_cross(n, tile_of(j + 1), 0)
                weigh(n, i, b)
                if b == 0:
                    gain(n, before, blocks - 1)
                else:
                    gain(n, i, b - 1)
            if final:

                @pl.when(j > 0)
                def _():
                    finish(before)

            else:

                @pl.when((n == 0) & (j == 1) & (z // 2 % 2 == 0))
                def _():
                    lax.fori_loop(z // 4 * 4 + 2, z // 4 * 4 + 4, send_higher, 0)

            return carry

        lax.fori_loop(0, tiles, slot_tile, 0)
        gain(n, tile_of(tiles - 1), blocks - 1)
        if final:
            finish(tile_of(tiles - 1))

    def early_round(n, carry):
        pair_round(n, False)

        @pl.when(n == 0)
        def _():
            lax.fori_loop(z // 4 * 4 + 4, lines, send_higher, 0)

        for k in (2 * n + 2, 2 * n + 3):
            block = line_peer(k)
            line_copy(block, block).wait_recv()
            take_stars(k, block)
        return carry

    lax.fori_loop(0, rounds - 1, early_round, 0)
    pair_round(rounds - 1, True)

    arrived[me] = partial[me // 2]

    def end_line(k, carry):
        line_copy(z, line_peer(k + 1)).wait_send()
        return carry

    def end_plane(k, carry):
        other = plane_peer(k)
        plane_copy(me, other, k).wait_send()
        part_copy(other // 2, me, other).wait_send()
        part_copy(other // 2, other, other).wait_recv()
        return carry

    lax.fori_loop(0, lines - 1, end_line, 0)
    lax.fori_loop(0, group - 1, end_plane, 0)
    terms = jnp.sum(arrived[...], axis=0)
    terms = jnp.where(me % 2 == 0, terms, pltpu.roll(terms, slots, 1))
    result[0:8, :] = terms[:, 0:slots]


def correct_kernel(result, count, pos_hbm, vel_hbm, acc_hbm, jerk_hbm, pos, vel, acc, jerk, store_sem):
    terms, picked = result[0:8, :], result[8:24, :]
    x0, v0, a0, j0, h = picked[0:3], picked[3:6], picked[6:9], picked[9:12], picked[12:13]
    slot_pos, slot_vel = predict(x0, v0, a0, j0, h)
    new_acc = terms[0:3] - slot_pos * terms[3:4]
    new_jerk = terms[4:7] - slot_vel * terms[3:4] - slot_pos * terms[7:8]
    new_vel = v0 + (a0 + new_acc) * h / 2 + (j0 - new_jerk) * h * h / 12
    new_pos = x0 + (v0 + new_vel) * h / 2 + (a0 - new_acc) * h * h / 12
    live = lax.broadcasted_iota(jnp.int32, new_acc.shape, 1) < count[0]
    stores = []
    for i, (value, held, target) in enumerate(
        ((new_acc, acc, acc_hbm), (new_jerk, jerk, jerk_hbm), (new_vel, vel, vel_hbm), (new_pos, pos, pos_hbm))
    ):
        held[...] = jnp.where(live, value, 0.0)
        stores.append(pltpu.make_async_copy(held, target, store_sem.at[i]))
        stores[-1].start()
    for store in stores:
        store.wait()


def body(lines, planes, pos, vel, acc, jerk, masses, levels, index, count):
    stars, slots, group = pos.shape[1], index.shape[1], 2 * planes
    hbm = pl.BlockSpec(memory_space=pl.ANY)
    tiles, blocks = group * slots // TILE, 2 * stars // TILE
    result = pl.pallas_call(
        functools.partial(kernel, lines, planes),
        out_shape=jax.ShapeDtypeStruct((24, slots), F32),
        in_specs=[hbm] * 7,
        out_specs=pl.BlockSpec(memory_space=pltpu.VMEM),
        scratch_shapes=[
            pltpu.VMEM((3, stars), F32),
            pltpu.VMEM((3, stars), F32),
            pltpu.VMEM((3, stars), F32),
            pltpu.VMEM((3, stars), F32),
            pltpu.VMEM((stars,), F32),
            pltpu.VMEM((stars,), jnp.int32),
            pltpu.VMEM((1, slots), jnp.int32),
            pltpu.VMEM((16, stars), F32),
            pltpu.VMEM((lines, 8, stars), F32),
            pltpu.VMEM((group, 8, LANES), F32),
            pltpu.VMEM((group, 8, LANES), F32),
            pltpu.VMEM((group // 2, 8, LANES), F32),
            pltpu.VMEM((3, lines * stars, LANES), F32),
            pltpu.VMEM((lines * stars, KDIM), BF16),
            pltpu.VMEM((8, group * slots), F32),
            pltpu.VMEM((KDIM, group * slots), BF16),
            pltpu.VMEM((SOURCES, lines * stars), BF16),
            pltpu.VMEM((blocks, TILE, TILE), F32),
            pltpu.VMEM((blocks, 2, 2 * TILE, TILE), BF16),
            pltpu.VMEM((tiles + 1, 2, SOURCES, TILE), F32),
            pltpu.SemaphoreType.DMA((7,)),
            pltpu.SemaphoreType.REGULAR((lines,)),
            pltpu.SemaphoreType.DMA((lines,)),
            pltpu.SemaphoreType.DMA((lines,)),
            pltpu.SemaphoreType.DMA((group,)),
            pltpu.SemaphoreType.DMA((group,)),
            pltpu.SemaphoreType.DMA((group,)),
            pltpu.SemaphoreType.DMA((group,)),
        ],
        compiler_params=pltpu.CompilerParams(collective_id=0, has_side_effects=True, vmem_limit_bytes=VMEM_LIMIT),
        name="forces",
    )(pos, vel, acc, jerk, masses, levels, index)
    three = jax.ShapeDtypeStruct((3, slots), F32)
    return pl.pallas_call(
        correct_kernel,
        out_shape=(three,) * 4,
        in_specs=[pl.BlockSpec(memory_space=pltpu.VMEM), pl.BlockSpec(memory_space=pltpu.SMEM)],
        out_specs=(hbm,) * 4,
        scratch_shapes=[pltpu.VMEM((3, slots), F32)] * 4 + [pltpu.SemaphoreType.DMA((4,))],
        compiler_params=pltpu.CompilerParams(vmem_limit_bytes=VMEM_LIMIT),
        name="correct",
    )(result, count)


def solution(mesh):
    lines, planes = mesh.shape["wide"] // 2, mesh.shape["sum"]
    both = ("wide", "sum")
    in_specs = (P(None, both),) * 4 + (P(both), P(both), P(both, None), P(both))
    return jax.shard_map(
        functools.partial(body, lines, planes), mesh=mesh, in_specs=in_specs,
        out_specs=(P(None, both),) * 4, check_vma=False,
    )
```

```python
import functools

import jax
import jax.numpy as jnp
from jax import lax
from jax.experimental import pallas as pl
from jax.experimental.pallas import tpu as pltpu
from jax.sharding import PartitionSpec as P

SOFT2 = 0.0025
STEP0 = 0.5
MESH = pl.DeviceIdType.MESH
F32 = jnp.float32
BF16 = jnp.bfloat16
LANES = 128
TILE = 256
KDIM = 128
ROWS = 16
SOURCES = 32
VMEM_LIMIT = 63 * 1024 * 1024


def step_of(levels):
    low = jnp.where(levels == 0, STEP0, STEP0 / 2)
    high = jnp.where(levels == 2, STEP0 / 4, STEP0 / 8)
    return jnp.where(levels < 2, low, high).astype(F32)


def predict(pos, vel, acc, jerk, step):
    pred_pos = pos + step * (vel + step * (acc / 2 + step * jerk / 6))
    pred_vel = vel + step * (acc + step * jerk / 2)
    return pred_pos, pred_vel


def pieces(value):
    first = value.astype(BF16).astype(F32)
    rest = value - first
    second = rest.astype(BF16).astype(F32)
    third = (rest - second).astype(BF16).astype(F32)
    return first, second, third


def split_state(tile):
    row = lax.broadcasted_iota(jnp.int32, tile.shape, 0)
    state = jnp.where(row < 6, tile, 0.0)
    grid = jnp.floor(state * 16.0 + 0.5) * 0.0625
    rest = state - grid
    near = rest.astype(BF16).astype(F32)
    far = (rest - near).astype(BF16).astype(F32)
    return grid, near, far


def own_cross(grid, near, far):
    small = near + far
    gp, gv, sp, sv = grid[0:3], grid[3:6], small[0:3], small[3:6]
    cross = jnp.sum(gp * gv, axis=0, keepdims=True)
    rest = jnp.sum(gp * sv + sp * gv + sp * sv, axis=0, keepdims=True)
    return list(pieces(cross)[:2] + pieces(rest))


def slot_rows(tile):
    width = tile.shape[1]
    grid, near, far = split_state(tile)
    none = jnp.zeros((3, width), F32)
    own = jnp.concatenate(own_cross(grid, near, far) + [none], 0)
    other = jnp.concatenate([jnp.ones((5, width), F32), none], 0)
    pad = jnp.zeros((KDIM - 88, width), F32)
    return jnp.concatenate([grid] * 3 + [near] * 3 + [far] * 3 + [own, other, pad], 0)


def star_rows(tile):
    width = tile.shape[1]
    grid, near, far = split_state(tile)
    none = jnp.zeros((3, width), F32)
    crossed = [jnp.concatenate([-part[3:6], -part[0:3], part[6:8]], 0) for part in (grid, near, far)]
    other = jnp.concatenate([jnp.ones((5, width), F32), none], 0)
    own = jnp.concatenate(own_cross(grid, near, far) + [none], 0)
    pad = jnp.zeros((KDIM - 88, width), F32)
    return jnp.concatenate(crossed * 3 + [other, own, pad], 0)


def source_rows(tile):
    weight = tile[6:7]
    none = jnp.zeros_like(weight)
    sources = jnp.concatenate([weight * tile[0:3], weight, weight * tile[3:6], none], 0)
    return jnp.concatenate(list(pieces(sources)) + [jnp.zeros((SOURCES - 24, tile.shape[1]), F32)], 0)


def kernel(
    lines, planes, pos_hbm, vel_hbm, acc_hbm, jerk_hbm, mass_hbm, level_hbm, index_hbm, result,
    pos, vel, acc, jerk, mass, level, index, stage, fields, actives, arrived, partial,
    spread, left, place_rows, along, moments, cross, high_low, sums,
    load_sem, ready, field_send, field_recv, active_send, active_recv, part_send, part_recv,
):
    group = 2 * planes
    stars, slots = pos.shape[1], index.shape[1]
    tiles = group * slots // TILE
    share = TILE // slots
    wide, s = lax.axis_index("wide"), lax.axis_index("sum")
    z, core = wide // 2, wide % 2
    me = core * planes + s

    def line_peer(k):
        other, bit = z, 1
        while bit < lines:
            other = other + (k // bit) % 2 * bit * (1 - 2 * ((z // bit) % 2))
            bit *= 2
        return other

    def plane_peer(k):
        return (me + 1 + k) % group

    def line_id(other):
        return (other * 2 + core, s)

    def plane_id(other):
        return (z * 2 + other // planes, other % planes)

    loads = [
        pltpu.make_async_copy(source, target, load_sem.at[i])
        for i, (source, target) in enumerate(
            zip((pos_hbm, vel_hbm, acc_hbm, jerk_hbm, mass_hbm, level_hbm, index_hbm), (pos, vel, acc, jerk, mass, level, index))
        )
    ]
    for load in loads:
        load.start()

    barrier = pltpu.get_barrier_semaphore()

    def greet_line(other, carry):
        pl.semaphore_signal(barrier, inc=1, device_id=line_id(other), device_id_type=MESH)
        return carry

    def greet_plane(k, carry):
        pl.semaphore_signal(barrier, inc=1, device_id=plane_id(plane_peer(k)), device_id_type=MESH)
        return carry

    lax.fori_loop(0, group - 1, greet_plane, 0)
    mate = line_peer(1)
    greet_line(mate, 0)
    lax.fori_loop(z // 2 * 2 + 2, lines, greet_line, 0)
    for load in loads:
        load.wait()

    step = step_of(level[...].reshape(1, stars))
    pred_pos, pred_vel = predict(pos[...], vel[...], acc[...], jerk[...], step)
    fields[z, 0:3, :] = pred_pos
    fields[z, 3:6, :] = pred_vel
    fields[z, 6:7, :] = mass[...].reshape(1, stars)
    fields[z, 7:8, :] = jnp.zeros_like(step)

    stage[0:3, :] = pos[...]
    stage[3:6, :] = vel[...]
    stage[6:9, :] = acc[...]
    stage[9:12, :] = jerk[...]
    stage[12:13, :] = step
    stage[13:16, :] = jnp.zeros((3, stars), F32)
    chosen = lax.broadcasted_iota(jnp.int32, (stars, slots), 0) == index[...]
    chosen = chosen.astype(F32).astype(BF16)
    picked = [jnp.dot(part.astype(BF16), chosen, preferred_element_type=F32) for part in pieces(stage[...])]
    picked = (picked[0] + picked[1]) + picked[2]
    result[8:24, :] = picked
    slot_pos, slot_vel = predict(picked[0:3], picked[3:6], picked[6:9], picked[9:12], picked[12:13])
    actives[me] = jnp.zeros((8, LANES), F32)
    actives[me, 0:3, 0:slots] = slot_pos
    actives[me, 3:6, 0:slots] = slot_vel

    pl.semaphore_wait(barrier, group + z // 2 * 2)

    def line_copy(block, other):
        return pltpu.make_async_remote_copy(
            src_ref=fields.at[block], dst_ref=fields.at[block],
            send_sem=field_send.at[other], recv_sem=field_recv.at[block],
            device_id=line_id(other), device_id_type=MESH,
        )

    def plane_copy(block, other, k):
        return pltpu.make_async_remote_copy(
            src_ref=actives.at[block], dst_ref=actives.at[block],
            send_sem=active_send.at[k], recv_sem=active_recv.at[block],
            device_id=plane_id(other), device_id_type=MESH,
        )

    def part_copy(pair, slot, other):
        return pltpu.make_async_remote_copy(
            src_ref=partial.at[pair], dst_ref=arrived.at[slot],
            send_sem=part_send.at[other], recv_sem=part_recv.at[slot],
            device_id=plane_id(other), device_id_type=MESH,
        )

    def send_lower(other, carry):
        pl.semaphore_signal(ready.at[z], inc=1, device_id=line_id(other), device_id_type=MESH)
        line_copy(z, other).start()
        return carry

    def send_higher(other, carry):
        pl.semaphore_wait(ready.at[other], 1)
        line_copy(z, other).start()
        return carry

    def send_plane(k, carry):
        plane_copy(me, plane_peer(k), k).start()
        return carry

    lax.fori_loop(0, group - 1, send_plane, 0)
    line_copy(z, mate).start()
    lax.fori_loop(0, z // 2 * 2, send_lower, 0)

    def take_stars(k, block):
        tile = fields[block]
        at = pl.ds(pl.multiple_of(k * stars, LANES), stars)
        left[at, :] = star_rows(tile).T.astype(BF16)
        turned = jnp.concatenate([tile] + [jnp.zeros_like(tile)] * 15, 0).T
        for c in range(3):
            spread[c, at, :] = jnp.broadcast_to(turned[:, c:c + 1], (stars, LANES))
        moments[:, at] = source_rows(tile).astype(BF16)

    take_stars(0, z)

    def get_plane(k, carry):
        plane_copy(plane_peer(k), plane_peer(k), k).wait_recv()
        return carry

    lax.fori_loop(0, group - 1, get_plane, 0)

    lane = lax.broadcasted_iota(jnp.int32, (8, LANES), 1)

    def take_slots(pair, carry):
        tile = jnp.where(lane < slots, actives[2 * pair], pltpu.roll(actives[2 * pair + 1], slots, 1))
        at = pl.ds(pl.multiple_of(pair * LANES, LANES), LANES)
        place_rows[:, at] = tile
        along[:, at] = slot_rows(tile).astype(BF16)
        return carry

    lax.fori_loop(0, group // 2, take_slots, 0)

    line_copy(mate, mate).wait_recv()
    take_stars(1, mate)

    blocks = 2 * stars // TILE
    rounds = lines // 2

    def stars_of(n, b):
        return pl.ds(pl.multiple_of((n * blocks + b) * TILE, TILE), TILE)

    def slots_of(i):
        return pl.ds(pl.multiple_of(i * TILE, TILE), TILE)

    def get_cross(n, i, b, part):
        half = slice(part * TILE // 2, (part + 1) * TILE // 2)
        rows = pl.ds(pl.multiple_of((n * blocks + b) * TILE + part * TILE // 2, TILE // 2), TILE // 2)
        cross[b, half, :] = jnp.dot(left[rows, :], along[:, slots_of(i)], preferred_element_type=F32)

    def weigh(n, i, b, beside):
        state = [jnp.broadcast_to(place_rows[c:c + 1, slots_of(i)], (ROWS, TILE)) for c in range(3)]
        for sub in range(0, TILE, ROWS):
            rows = pl.ds(pl.multiple_of((n * blocks + b) * TILE + sub, ROWS), ROWS)
            star = [jnp.concatenate([spread[c, rows, :]] * (TILE // LANES), 1) for c in range(3)]
            r = [star[c] - state[c] for c in range(3)]
            q = r[0] * r[0] + r[1] * r[1] + (r[2] * r[2] + SOFT2)
            inverse = lax.rsqrt(q)
            inverse2 = inverse * inverse
            w = inverse2 * inverse
            sw = (w * inverse2) * cross[b, sub:sub + ROWS, :]
            for kind, value in enumerate((w, sw)):
                high = value.astype(BF16)
                high_low[b, kind, sub:sub + ROWS, :] = high
                high_low[b, kind, TILE + sub:TILE + sub + ROWS, :] = (value - high.astype(F32)).astype(BF16)
            if sub // ROWS in beside:
                beside[sub // ROWS]()

    def gain(n, i, b, kind, part):
        piece = high_low[b, kind, part * TILE:(part + 1) * TILE, :]
        sums[i, kind] += jnp.dot(moments[:, stars_of(n, b)], piece, preferred_element_type=F32)

    def finish(i):
        by_w, by_s = sums[i, 0], sums[i, 1]
        by_w = by_w[0:8] + by_w[8:16] + by_w[16:24]
        by_s = by_s[0:8] + by_s[8:16] + by_s[16:24]
        row = lax.broadcasted_iota(jnp.int32, by_s.shape, 0)
        terms = by_w + pltpu.roll(jnp.where(row < 4, -3.0 * by_s, 0.0), 4, 0)
        for pair in range(share // 2):
            place = i * (share // 2) + pair
            partial[place] = terms[:, pair * LANES:(pair + 1) * LANES]
            for half in range(2):
                owner = 2 * place + half

                @pl.when(owner != me)
                def _():
                    part_copy(place, me, owner).start()

    def tile_of(j):
        return (me // share + 1 + j) % tiles

    sums[...] = jnp.zeros_like(sums)

    def pair_round(n, final):
        for part in range(2):
            get_cross(n, tile_of(0), 0, part)

        def slot_tile(j, carry):
            i = tile_of(j)
            before = jnp.where(j > 0, tile_of(j + tiles - 1), tiles)
            for b in range(blocks):
                done = (before, blocks - 1) if b == 0 else (i, b - 1)
                soon = (i, b + 1) if b < blocks - 1 else (tile_of(j + 1), 0)
                beside = {}
                for part in range(2):
                    beside[8 * part + 3] = functools.partial(get_cross, n, *soon, part)
                    for kind in range(2):
                        beside[8 * part + 4 * kind + 1] = functools.partial(gain, n, *done, kind, part)
                weigh(n, i, b, beside)
            if final:

                @pl.when(j > 0)
                def _():
                    finish(before)

            else:

                @pl.when((n == 0) & (j == 1) & (z // 2 % 2 == 0))
                def _():
                    lax.fori_loop(z // 4 * 4 + 2, z // 4 * 4 + 4, send_higher, 0)

            return carry

        lax.fori_loop(0, tiles, slot_tile, 0, unroll=1 if final else 2)
        for kind in range(2):
            for part in range(2):
                gain(n, tile_of(tiles - 1), blocks - 1, kind, part)
        if final:
            finish(tile_of(tiles - 1))

    def early_round(n, carry):
        pair_round(n, False)

        @pl.when(n == 0)
        def _():
            lax.fori_loop(z // 4 * 4 + 4, lines, send_higher, 0)

        for k in (2 * n + 2, 2 * n + 3):
            block = line_peer(k)
            line_copy(block, block).wait_recv()
            take_stars(k, block)
        return carry

    lax.fori_loop(0, rounds - 1, early_round, 0)
    pair_round(rounds - 1, True)

    arrived[me] = partial[me // 2]

    def end_line(k, carry):
        line_copy(z, line_peer(k + 1)).wait_send()
        return carry

    def end_plane(k, carry):
        other = plane_peer(k)
        plane_copy(me, other, k).wait_send()
        part_copy(other // 2, me, other).wait_send()
        part_copy(other // 2, other, other).wait_recv()
        return carry

    lax.fori_loop(0, lines - 1, end_line, 0)
    lax.fori_loop(0, group - 1, end_plane, 0)
    terms = jnp.sum(arrived[...], axis=0)
    terms = jnp.where(me % 2 == 0, terms, pltpu.roll(terms, slots, 1))
    result[0:8, :] = terms[:, 0:slots]


def correct_kernel(result, count, pos_hbm, vel_hbm, acc_hbm, jerk_hbm, pos, vel, acc, jerk, store_sem):
    terms, picked = result[0:8, :], result[8:24, :]
    x0, v0, a0, j0, h = picked[0:3], picked[3:6], picked[6:9], picked[9:12], picked[12:13]
    slot_pos, slot_vel = predict(x0, v0, a0, j0, h)
    new_acc = terms[0:3] - slot_pos * terms[3:4]
    new_jerk = terms[4:7] - slot_vel * terms[3:4] - slot_pos * terms[7:8]
    new_vel = v0 + (a0 + new_acc) * h / 2 + (j0 - new_jerk) * h * h / 12
    new_pos = x0 + (v0 + new_vel) * h / 2 + (a0 - new_acc) * h * h / 12
    live = lax.broadcasted_iota(jnp.int32, new_acc.shape, 1) < count[0]
    stores = []
    for i, (value, held, target) in enumerate(
        ((new_acc, acc, acc_hbm), (new_jerk, jerk, jerk_hbm), (new_vel, vel, vel_hbm), (new_pos, pos, pos_hbm))
    ):
        held[...] = jnp.where(live, value, 0.0)
        stores.append(pltpu.make_async_copy(held, target, store_sem.at[i]))
        stores[-1].start()
    for store in stores:
        store.wait()


def body(lines, planes, pos, vel, acc, jerk, masses, levels, index, count):
    stars, slots, group = pos.shape[1], index.shape[1], 2 * planes
    hbm = pl.BlockSpec(memory_space=pl.ANY)
    tiles, blocks = group * slots // TILE, 2 * stars // TILE
    result = pl.pallas_call(
        functools.partial(kernel, lines, planes),
        out_shape=jax.ShapeDtypeStruct((24, slots), F32),
        in_specs=[hbm] * 7,
        out_specs=pl.BlockSpec(memory_space=pltpu.VMEM),
        scratch_shapes=[
            pltpu.VMEM((3, stars), F32),
            pltpu.VMEM((3, stars), F32),
            pltpu.VMEM((3, stars), F32),
            pltpu.VMEM((3, stars), F32),
            pltpu.VMEM((stars,), F32),
            pltpu.VMEM((stars,), jnp.int32),
            pltpu.VMEM((1, slots), jnp.int32),
            pltpu.VMEM((16, stars), F32),
            pltpu.VMEM((lines, 8, stars), F32),
            pltpu.VMEM((group, 8, LANES), F32),
            pltpu.VMEM((group, 8, LANES), F32),
            pltpu.VMEM((group // 2, 8, LANES), F32),
            pltpu.VMEM((3, lines * stars, LANES), F32),
            pltpu.VMEM((lines * stars, KDIM), BF16),
            pltpu.VMEM((8, group * slots), F32),
            pltpu.VMEM((KDIM, group * slots), BF16),
            pltpu.VMEM((SOURCES, lines * stars), BF16),
            pltpu.VMEM((blocks, TILE, TILE), F32),
            pltpu.VMEM((blocks, 2, 2 * TILE, TILE), BF16),
            pltpu.VMEM((tiles + 1, 2, SOURCES, TILE), F32),
            pltpu.SemaphoreType.DMA((7,)),
            pltpu.SemaphoreType.REGULAR((lines,)),
            pltpu.SemaphoreType.DMA((lines,)),
            pltpu.SemaphoreType.DMA((lines,)),
            pltpu.SemaphoreType.DMA((group,)),
            pltpu.SemaphoreType.DMA((group,)),
            pltpu.SemaphoreType.DMA((group,)),
            pltpu.SemaphoreType.DMA((group,)),
        ],
        compiler_params=pltpu.CompilerParams(collective_id=0, has_side_effects=True, vmem_limit_bytes=VMEM_LIMIT),
        name="forces",
    )(pos, vel, acc, jerk, masses, levels, index)
    three = jax.ShapeDtypeStruct((3, slots), F32)
    return pl.pallas_call(
        correct_kernel,
        out_shape=(three,) * 4,
        in_specs=[pl.BlockSpec(memory_space=pltpu.VMEM), pl.BlockSpec(memory_space=pltpu.SMEM)],
        out_specs=(hbm,) * 4,
        scratch_shapes=[pltpu.VMEM((3, slots), F32)] * 4 + [pltpu.SemaphoreType.DMA((4,))],
        compiler_params=pltpu.CompilerParams(vmem_limit_bytes=VMEM_LIMIT),
        name="correct",
    )(result, count)


def solution(mesh):
    lines, planes = mesh.shape["wide"] // 2, mesh.shape["sum"]
    both = ("wide", "sum")
    in_specs = (P(None, both),) * 4 + (P(both), P(both), P(both, None), P(both))
    return jax.shard_map(
        functools.partial(body, lines, planes), mesh=mesh, in_specs=in_specs,
        out_specs=(P(None, both),) * 4, check_vma=False,
    )
```

```python
import functools

import jax
import jax.numpy as jnp
from jax import lax
from jax.experimental import pallas as pl
from jax.experimental.pallas import tpu as pltpu
from jax.sharding import PartitionSpec as P

SOFT2 = 0.0025
STEP0 = 0.5
MESH = pl.DeviceIdType.MESH
F32 = jnp.float32
BF16 = jnp.bfloat16
LANES = 128
TILE = 256
KDIM = 128
STATE_ROW = 88
ROWS = 16
SOURCES = 32
VMEM_LIMIT = 63 * 1024 * 1024


def step_of(levels):
    low = jnp.where(levels == 0, STEP0, STEP0 / 2)
    high = jnp.where(levels == 2, STEP0 / 4, STEP0 / 8)
    return jnp.where(levels < 2, low, high).astype(F32)


def predict(pos, vel, acc, jerk, step):
    pred_pos = pos + step * (vel + step * (acc / 2 + step * jerk / 6))
    pred_vel = vel + step * (acc + step * jerk / 2)
    return pred_pos, pred_vel


def pieces(value):
    first = value.astype(BF16).astype(F32)
    rest = value - first
    second = rest.astype(BF16).astype(F32)
    third = (rest - second).astype(BF16).astype(F32)
    return first, second, third


def split_state(tile):
    row = lax.broadcasted_iota(jnp.int32, tile.shape, 0)
    state = jnp.where(row < 6, tile, 0.0)
    grid = jnp.floor(state * 16.0 + 0.5) * 0.0625
    rest = state - grid
    near = rest.astype(BF16).astype(F32)
    far = (rest - near).astype(BF16).astype(F32)
    return grid, near, far


def own_cross(grid, near, far):
    small = near + far
    gp, gv, sp, sv = grid[0:3], grid[3:6], small[0:3], small[3:6]
    cross = jnp.sum(gp * gv, axis=0, keepdims=True)
    rest = jnp.sum(gp * sv + sp * gv + sp * sv, axis=0, keepdims=True)
    return list(pieces(cross)[:2] + pieces(rest))


def slot_rows(tile):
    width = tile.shape[1]
    grid, near, far = split_state(tile)
    none = jnp.zeros((3, width), F32)
    own = jnp.concatenate(own_cross(grid, near, far) + [none], 0)
    other = jnp.concatenate([jnp.ones((5, width), F32), none], 0)
    pad = jnp.zeros((KDIM - STATE_ROW, width), F32)
    return jnp.concatenate([grid] * 3 + [near] * 3 + [far] * 3 + [own, other, pad], 0)


def star_rows(tile):
    width = tile.shape[1]
    grid, near, far = split_state(tile)
    none = jnp.zeros((3, width), F32)
    crossed = [jnp.concatenate([-part[3:6], -part[0:3], part[6:8]], 0) for part in (grid, near, far)]
    other = jnp.concatenate([jnp.ones((5, width), F32), none], 0)
    own = jnp.concatenate(own_cross(grid, near, far) + [none], 0)
    pad = jnp.zeros((KDIM - STATE_ROW - 8, width), F32)
    return jnp.concatenate(crossed * 3 + [other, own, tile, pad], 0)


def source_rows(tile):
    weight = tile[6:7]
    none = jnp.zeros_like(weight)
    sources = jnp.concatenate([weight * tile[0:3], weight, weight * tile[3:6], none], 0)
    return jnp.concatenate(list(pieces(sources)) + [jnp.zeros((SOURCES - 24, tile.shape[1]), F32)], 0)


def kernel(
    lines, planes, pos_hbm, vel_hbm, acc_hbm, jerk_hbm, mass_hbm, level_hbm, index_hbm, result,
    pos, vel, acc, jerk, mass, level, index, stage, fields, actives, arrived, partial,
    spread, left, place_rows, along, moments, cross, high_low, sums,
    load_sem, ready, field_send, field_recv, active_send, active_recv, part_send, part_recv,
):
    group = 2 * planes
    stars, slots = pos.shape[1], index.shape[1]
    tiles = group * slots // TILE
    share = TILE // slots
    wide, s = lax.axis_index("wide"), lax.axis_index("sum")
    z, core = wide // 2, wide % 2
    me = core * planes + s

    def line_peer(k):
        other, bit = z, 1
        while bit < lines:
            other = other + (k // bit) % 2 * bit * (1 - 2 * ((z // bit) % 2))
            bit *= 2
        return other

    def plane_peer(k):
        return (me + 1 + k) % group

    def line_id(other):
        return (other * 2 + core, s)

    def plane_id(other):
        return (z * 2 + other // planes, other % planes)

    loads = [
        pltpu.make_async_copy(source, target, load_sem.at[i])
        for i, (source, target) in enumerate(
            zip((pos_hbm, vel_hbm, acc_hbm, jerk_hbm, mass_hbm, level_hbm, index_hbm), (pos, vel, acc, jerk, mass, level, index))
        )
    ]
    for load in loads:
        load.start()

    barrier = pltpu.get_barrier_semaphore()

    def greet_line(other, carry):
        pl.semaphore_signal(barrier, inc=1, device_id=line_id(other), device_id_type=MESH)
        return carry

    def greet_plane(k, carry):
        pl.semaphore_signal(barrier, inc=1, device_id=plane_id(plane_peer(k)), device_id_type=MESH)
        return carry

    lax.fori_loop(0, group - 1, greet_plane, 0, unroll=True)
    mate = line_peer(1)
    greet_line(mate, 0)
    lax.fori_loop(z // 2 * 2 + 2, lines, greet_line, 0)
    for load in loads:
        load.wait()

    step = step_of(level[...].reshape(1, stars))
    pred_pos, pred_vel = predict(pos[...], vel[...], acc[...], jerk[...], step)
    fields[z, 0:3, :] = pred_pos
    fields[z, 3:6, :] = pred_vel
    fields[z, 6:7, :] = mass[...].reshape(1, stars)
    fields[z, 7:8, :] = jnp.zeros_like(step)

    stage[0:3, :] = pos[...]
    stage[3:6, :] = vel[...]
    stage[6:9, :] = acc[...]
    stage[9:12, :] = jerk[...]
    stage[12:13, :] = step
    stage[13:16, :] = jnp.zeros((3, stars), F32)
    chosen = lax.broadcasted_iota(jnp.int32, (stars, slots), 0) == index[...]
    chosen = chosen.astype(F32).astype(BF16)
    picked = [jnp.dot(part.astype(BF16), chosen, preferred_element_type=F32) for part in pieces(stage[...])]
    picked = (picked[0] + picked[1]) + picked[2]
    result[8:24, :] = picked
    slot_pos, slot_vel = predict(picked[0:3], picked[3:6], picked[6:9], picked[9:12], picked[12:13])
    actives[me] = jnp.zeros((8, LANES), F32)
    actives[me, 0:3, 0:slots] = slot_pos
    actives[me, 3:6, 0:slots] = slot_vel

    pl.semaphore_wait(barrier, group + z // 2 * 2)

    def line_copy(block, other):
        return pltpu.make_async_remote_copy(
            src_ref=fields.at[block], dst_ref=fields.at[block],
            send_sem=field_send.at[other], recv_sem=field_recv.at[block],
            device_id=line_id(other), device_id_type=MESH,
        )

    def plane_copy(block, other, k):
        return pltpu.make_async_remote_copy(
            src_ref=actives.at[block], dst_ref=actives.at[block],
            send_sem=active_send.at[k], recv_sem=active_recv.at[block],
            device_id=plane_id(other), device_id_type=MESH,
        )

    def part_copy(pair, slot, other):
        return pltpu.make_async_remote_copy(
            src_ref=partial.at[pair], dst_ref=arrived.at[slot],
            send_sem=part_send.at[other], recv_sem=part_recv.at[slot],
            device_id=plane_id(other), device_id_type=MESH,
        )

    def send_lower(other, carry):
        pl.semaphore_signal(ready.at[z], inc=1, device_id=line_id(other), device_id_type=MESH)
        line_copy(z, other).start()
        return carry

    def send_higher(other, carry):
        pl.semaphore_wait(ready.at[other], 1)
        line_copy(z, other).start()
        return carry

    def send_plane(k, carry):
        plane_copy(me, plane_peer(k), k).start()
        return carry

    lax.fori_loop(0, group - 1, send_plane, 0, unroll=True)
    line_copy(z, mate).start()
    lax.fori_loop(0, z // 2 * 2, send_lower, 0)

    def take_stars(k, block):
        tile = fields[block]
        at = pl.ds(pl.multiple_of(k * stars, LANES), stars)
        turned = star_rows(tile).T
        left[at, :] = turned.astype(BF16)
        for c in range(3):
            spread[c, at, :] = jnp.broadcast_to(turned[:, STATE_ROW + c:STATE_ROW + c + 1], (stars, LANES))
        moments[:, at] = source_rows(tile).astype(BF16)

    take_stars(0, z)

    def get_plane(k, carry):
        plane_copy(plane_peer(k), plane_peer(k), k).wait_recv()
        return carry

    lax.fori_loop(0, group - 1, get_plane, 0, unroll=True)

    lane = lax.broadcasted_iota(jnp.int32, (8, LANES), 1)

    def take_slots(pair, carry):
        tile = jnp.where(lane < slots, actives[2 * pair], pltpu.roll(actives[2 * pair + 1], slots, 1))
        at = pl.ds(pl.multiple_of(pair * LANES, LANES), LANES)
        place_rows[:, at] = tile
        along[:, at] = slot_rows(tile).astype(BF16)
        return carry

    lax.fori_loop(0, group // 2, take_slots, 0, unroll=True)

    line_copy(mate, mate).wait_recv()
    take_stars(1, mate)

    blocks = 2 * stars // TILE
    rounds = lines // 2

    def stars_of(n, b):
        return pl.ds(pl.multiple_of((n * blocks + b) * TILE, TILE), TILE)

    def slots_of(i):
        return pl.ds(pl.multiple_of(i * TILE, TILE), TILE)

    def get_cross(n, i, b, part):
        half = slice(part * TILE // 2, (part + 1) * TILE // 2)
        rows = pl.ds(pl.multiple_of((n * blocks + b) * TILE + part * TILE // 2, TILE // 2), TILE // 2)
        cross[b, half, :] = jnp.dot(left[rows, :], along[:, slots_of(i)], preferred_element_type=F32)

    def weigh(n, i, b, beside):
        state = [jnp.broadcast_to(place_rows[c:c + 1, slots_of(i)], (ROWS, TILE)) for c in range(3)]
        for sub in range(0, TILE, ROWS):
            rows = pl.ds(pl.multiple_of((n * blocks + b) * TILE + sub, ROWS), ROWS)
            star = [jnp.concatenate([spread[c, rows, :]] * (TILE // LANES), 1) for c in range(3)]
            r = [star[c] - state[c] for c in range(3)]
            q = r[0] * r[0] + r[1] * r[1] + (r[2] * r[2] + SOFT2)
            inverse = lax.rsqrt(q)
            inverse2 = inverse * inverse
            w = inverse2 * inverse
            sw = (w * inverse2) * cross[b, sub:sub + ROWS, :]
            for kind, value in enumerate((w, sw)):
                high = value.astype(BF16)
                high_low[b, kind, sub:sub + ROWS, :] = high
                high_low[b, kind, TILE + sub:TILE + sub + ROWS, :] = (value - high.astype(F32)).astype(BF16)
            if sub // ROWS in beside:
                beside[sub // ROWS]()

    def gain(n, i, b, kind, part):
        piece = high_low[b, kind, part * TILE:(part + 1) * TILE, :]
        sums[i, kind] += jnp.dot(moments[:, stars_of(n, b)], piece, preferred_element_type=F32)

    def finish(i):
        by_w, by_s = sums[i, 0], sums[i, 1]
        by_w = by_w[0:8] + by_w[8:16] + by_w[16:24]
        by_s = by_s[0:8] + by_s[8:16] + by_s[16:24]
        row = lax.broadcasted_iota(jnp.int32, by_s.shape, 0)
        terms = by_w + pltpu.roll(jnp.where(row < 4, -3.0 * by_s, 0.0), 4, 0)
        for pair in range(share // 2):
            place = i * (share // 2) + pair
            partial[place] = terms[:, pair * LANES:(pair + 1) * LANES]
            for half in range(2):
                owner = 2 * place + half

                @pl.when(owner != me)
                def _():
                    part_copy(place, me, owner).start()

    def tile_of(j):
        return (me // share + 1 + j) % tiles

    sums[...] = jnp.zeros_like(sums)

    def pair_round(n, final):
        for part in range(2):
            get_cross(n, tile_of(0), 0, part)

        def slot_tile(j, carry):
            i = tile_of(j)
            before = jnp.where(j > 0, tile_of(j + tiles - 1), tiles)
            for b in range(blocks):
                done = (before, blocks - 1) if b == 0 else (i, b - 1)
                soon = (i, b + 1) if b < blocks - 1 else (tile_of(j + 1), 0)
                beside = {}
                for part in range(2):
                    beside[8 * part + 3] = functools.partial(get_cross, n, *soon, part)
                    for kind in range(2):
                        beside[8 * part + 4 * kind + 1] = functools.partial(gain, n, *done, kind, part)
                weigh(n, i, b, beside)
            if final:

                @pl.when(j > 0)
                def _():
                    finish(before)

            else:

                @pl.when((n == 0) & (j == 1) & (z // 2 % 2 == 0))
                def _():
                    lax.fori_loop(z // 4 * 4 + 2, z // 4 * 4 + 4, send_higher, 0)

            return carry

        lax.fori_loop(0, tiles, slot_tile, 0, unroll=1 if final else 2)
        for kind in range(2):
            for part in range(2):
                gain(n, tile_of(tiles - 1), blocks - 1, kind, part)
        if final:
            finish(tile_of(tiles - 1))

    def early_round(n, carry):
        pair_round(n, False)

        @pl.when(n == 0)
        def _():
            lax.fori_loop(z // 4 * 4 + 4, lines, send_higher, 0)

        for k in (2 * n + 2, 2 * n + 3):
            block = line_peer(k)
            line_copy(block, block).wait_recv()
            take_stars(k, block)
        return carry

    lax.fori_loop(0, rounds - 1, early_round, 0)
    pair_round(rounds - 1, True)

    arrived[me] = partial[me // 2]

    def get_part(k, carry):
        other = plane_peer(k)
        part_copy(other // 2, other, other).wait_recv()
        return carry

    lax.fori_loop(0, group - 1, get_part, 0, unroll=True)
    terms = jnp.sum(arrived[...], axis=0)
    terms = jnp.where(me % 2 == 0, terms, pltpu.roll(terms, slots, 1))
    result[0:8, :] = terms[:, 0:slots]

    def end_line(k, carry):
        line_copy(z, line_peer(k + 1)).wait_send()
        return carry

    def end_plane(k, carry):
        other = plane_peer(k)
        plane_copy(me, other, k).wait_send()
        part_copy(other // 2, me, other).wait_send()
        return carry

    lax.fori_loop(0, lines - 1, end_line, 0, unroll=True)
    lax.fori_loop(0, group - 1, end_plane, 0, unroll=True)


def correct_kernel(result, count, pos_hbm, vel_hbm, acc_hbm, jerk_hbm, pos, vel, acc, jerk, store_sem):
    terms, picked = result[0:8, :], result[8:24, :]
    x0, v0, a0, j0, h = picked[0:3], picked[3:6], picked[6:9], picked[9:12], picked[12:13]
    slot_pos, slot_vel = predict(x0, v0, a0, j0, h)
    new_acc = terms[0:3] - slot_pos * terms[3:4]
    new_jerk = terms[4:7] - slot_vel * terms[3:4] - slot_pos * terms[7:8]
    new_vel = v0 + (a0 + new_acc) * h / 2 + (j0 - new_jerk) * h * h / 12
    new_pos = x0 + (v0 + new_vel) * h / 2 + (a0 - new_acc) * h * h / 12
    live = lax.broadcasted_iota(jnp.int32, new_acc.shape, 1) < count[0]
    stores = []
    for i, (value, held, target) in enumerate(
        ((new_acc, acc, acc_hbm), (new_jerk, jerk, jerk_hbm), (new_vel, vel, vel_hbm), (new_pos, pos, pos_hbm))
    ):
        held[...] = jnp.where(live, value, 0.0)
        stores.append(pltpu.make_async_copy(held, target, store_sem.at[i]))
        stores[-1].start()
    for store in stores:
        store.wait()


def body(lines, planes, pos, vel, acc, jerk, masses, levels, index, count):
    stars, slots, group = pos.shape[1], index.shape[1], 2 * planes
    hbm = pl.BlockSpec(memory_space=pl.ANY)
    tiles, blocks = group * slots // TILE, 2 * stars // TILE
    result = pl.pallas_call(
        functools.partial(kernel, lines, planes),
        out_shape=jax.ShapeDtypeStruct((24, slots), F32),
        in_specs=[hbm] * 7,
        out_specs=pl.BlockSpec(memory_space=pltpu.VMEM),
        scratch_shapes=[
            pltpu.VMEM((3, stars), F32),
            pltpu.VMEM((3, stars), F32),
            pltpu.VMEM((3, stars), F32),
            pltpu.VMEM((3, stars), F32),
            pltpu.VMEM((stars,), F32),
            pltpu.VMEM((stars,), jnp.int32),
            pltpu.VMEM((1, slots), jnp.int32),
            pltpu.VMEM((16, stars), F32),
            pltpu.VMEM((lines, 8, stars), F32),
            pltpu.VMEM((group, 8, LANES), F32),
            pltpu.VMEM((group, 8, LANES), F32),
            pltpu.VMEM((group // 2, 8, LANES), F32),
            pltpu.VMEM((3, lines * stars, LANES), F32),
            pltpu.VMEM((lines * stars, KDIM), BF16),
            pltpu.VMEM((8, group * slots), F32),
            pltpu.VMEM((KDIM, group * slots), BF16),
            pltpu.VMEM((SOURCES, lines * stars), BF16),
            pltpu.VMEM((blocks, TILE, TILE), F32),
            pltpu.VMEM((blocks, 2, 2 * TILE, TILE), BF16),
            pltpu.VMEM((tiles + 1, 2, SOURCES, TILE), F32),
            pltpu.SemaphoreType.DMA((7,)),
            pltpu.SemaphoreType.REGULAR((lines,)),
            pltpu.SemaphoreType.DMA((lines,)),
            pltpu.SemaphoreType.DMA((lines,)),
            pltpu.SemaphoreType.DMA((group,)),
            pltpu.SemaphoreType.DMA((group,)),
            pltpu.SemaphoreType.DMA((group,)),
            pltpu.SemaphoreType.DMA((group,)),
        ],
        compiler_params=pltpu.CompilerParams(collective_id=0, has_side_effects=True, vmem_limit_bytes=VMEM_LIMIT),
        name="forces",
    )(pos, vel, acc, jerk, masses, levels, index)
    three = jax.ShapeDtypeStruct((3, slots), F32)
    return pl.pallas_call(
        correct_kernel,
        out_shape=(three,) * 4,
        in_specs=[pl.BlockSpec(memory_space=pltpu.VMEM), pl.BlockSpec(memory_space=pltpu.SMEM)],
        out_specs=(hbm,) * 4,
        scratch_shapes=[pltpu.VMEM((3, slots), F32)] * 4 + [pltpu.SemaphoreType.DMA((4,))],
        compiler_params=pltpu.CompilerParams(vmem_limit_bytes=VMEM_LIMIT),
        name="correct",
    )(result, count)


def solution(mesh):
    lines, planes = mesh.shape["wide"] // 2, mesh.shape["sum"]
    both = ("wide", "sum")
    in_specs = (P(None, both),) * 4 + (P(both), P(both), P(both, None), P(both))
    return jax.shard_map(
        functools.partial(body, lines, planes), mesh=mesh, in_specs=in_specs,
        out_specs=(P(None, both),) * 4, check_vma=False,
    )
```

```python
import functools

import jax
import jax.numpy as jnp
from jax import lax
from jax.experimental import pallas as pl
from jax.experimental.pallas import tpu as pltpu
from jax.sharding import PartitionSpec as P

SOFT2 = 0.0025
STEP0 = 0.5
MESH = pl.DeviceIdType.MESH
F32 = jnp.float32
BF16 = jnp.bfloat16
LANES = 128
TILE = 256
WIDE = 1024
KDIM = 128
STATE_ROW = 88
ROWS = 16
SOURCES = 32
VMEM_LIMIT = 63 * 1024 * 1024


def step_of(levels):
    low = jnp.where(levels == 0, STEP0, STEP0 / 2)
    high = jnp.where(levels == 2, STEP0 / 4, STEP0 / 8)
    return jnp.where(levels < 2, low, high).astype(F32)


def predict(pos, vel, acc, jerk, step):
    pred_pos = pos + step * (vel + step * (acc / 2 + step * jerk / 6))
    pred_vel = vel + step * (acc + step * jerk / 2)
    return pred_pos, pred_vel


def pieces(value):
    first = value.astype(BF16).astype(F32)
    rest = value - first
    second = rest.astype(BF16).astype(F32)
    third = (rest - second).astype(BF16).astype(F32)
    return first, second, third


def split_state(tile):
    row = lax.broadcasted_iota(jnp.int32, tile.shape, 0)
    state = jnp.where(row < 6, tile, 0.0)
    grid = jnp.floor(state * 16.0 + 0.5) * 0.0625
    rest = state - grid
    near = rest.astype(BF16).astype(F32)
    far = (rest - near).astype(BF16).astype(F32)
    return grid, near, far


def own_cross(grid, near, far):
    small = near + far
    gp, gv, sp, sv = grid[0:3], grid[3:6], small[0:3], small[3:6]
    cross = jnp.sum(gp * gv, axis=0, keepdims=True)
    rest = jnp.sum(gp * sv + sp * gv + sp * sv, axis=0, keepdims=True)
    return list(pieces(cross)[:2] + pieces(rest))


def slot_rows(tile):
    width = tile.shape[1]
    grid, near, far = split_state(tile)
    none = jnp.zeros((3, width), F32)
    own = jnp.concatenate(own_cross(grid, near, far) + [none], 0)
    other = jnp.concatenate([jnp.ones((5, width), F32), none], 0)
    pad = jnp.zeros((KDIM - STATE_ROW, width), F32)
    return jnp.concatenate([grid] * 3 + [near] * 3 + [far] * 3 + [own, other, pad], 0)


def star_rows(tile):
    width = tile.shape[1]
    grid, near, far = split_state(tile)
    none = jnp.zeros((3, width), F32)
    crossed = [jnp.concatenate([-part[3:6], -part[0:3], part[6:8]], 0) for part in (grid, near, far)]
    other = jnp.concatenate([jnp.ones((5, width), F32), none], 0)
    own = jnp.concatenate(own_cross(grid, near, far) + [none], 0)
    pad = jnp.zeros((KDIM - STATE_ROW - 8, width), F32)
    return jnp.concatenate(crossed * 3 + [other, own, tile, pad], 0)


def source_rows(tile):
    weight = tile[6:7]
    none = jnp.zeros_like(weight)
    sources = jnp.concatenate([weight * tile[0:3], weight, weight * tile[3:6], none], 0)
    return jnp.concatenate(list(pieces(sources)) + [jnp.zeros((SOURCES - 24, tile.shape[1]), F32)], 0)


def kernel(
    lines, planes, pos_hbm, vel_hbm, acc_hbm, jerk_hbm, mass_hbm, level_hbm, index_hbm, result,
    pos, vel, acc, jerk, mass, level, index, stage, fields, actives, arrived, partial,
    spread, left, place_rows, along, moments, cross, high_low, sums,
    load_sem, ready, field_send, field_recv, active_send, active_recv, part_send, part_recv,
):
    group = 2 * planes
    stars, slots = pos.shape[1], index.shape[1]
    wide_tile = sums.shape[3]
    tiles = group * slots // wide_tile
    share = wide_tile // slots
    wide, s = lax.axis_index("wide"), lax.axis_index("sum")
    z, core = wide // 2, wide % 2
    me = core * planes + s

    def line_peer(k):
        other, bit = z, 1
        while bit < lines:
            other = other + (k // bit) % 2 * bit * (1 - 2 * ((z // bit) % 2))
            bit *= 2
        return other

    def plane_peer(k):
        return (me + 1 + k) % group

    def line_id(other):
        return (other * 2 + core, s)

    def plane_id(other):
        return (z * 2 + other // planes, other % planes)

    loads = [
        pltpu.make_async_copy(source, target, load_sem.at[i])
        for i, (source, target) in enumerate(
            zip((pos_hbm, vel_hbm, acc_hbm, jerk_hbm, mass_hbm, level_hbm, index_hbm), (pos, vel, acc, jerk, mass, level, index))
        )
    ]
    for load in loads:
        load.start()

    barrier = pltpu.get_barrier_semaphore()

    def greet_line(other, carry):
        pl.semaphore_signal(barrier, inc=1, device_id=line_id(other), device_id_type=MESH)
        return carry

    def greet_plane(k, carry):
        pl.semaphore_signal(barrier, inc=1, device_id=plane_id(plane_peer(k)), device_id_type=MESH)
        return carry

    lax.fori_loop(0, group - 1, greet_plane, 0, unroll=True)
    mate = line_peer(1)
    greet_line(mate, 0)
    lax.fori_loop(z // 2 * 2 + 2, lines, greet_line, 0)
    for load in loads:
        load.wait()

    step = step_of(level[...].reshape(1, stars))
    pred_pos, pred_vel = predict(pos[...], vel[...], acc[...], jerk[...], step)
    fields[z, 0:3, :] = pred_pos
    fields[z, 3:6, :] = pred_vel
    fields[z, 6:7, :] = mass[...].reshape(1, stars)
    fields[z, 7:8, :] = jnp.zeros_like(step)

    stage[0:3, :] = pos[...]
    stage[3:6, :] = vel[...]
    stage[6:9, :] = acc[...]
    stage[9:12, :] = jerk[...]
    stage[12:13, :] = step
    stage[13:16, :] = jnp.zeros((3, stars), F32)
    chosen = lax.broadcasted_iota(jnp.int32, (stars, slots), 0) == index[...]
    chosen = chosen.astype(F32).astype(BF16)
    picked = [jnp.dot(part.astype(BF16), chosen, preferred_element_type=F32) for part in pieces(stage[...])]
    picked = (picked[0] + picked[1]) + picked[2]
    result[8:24, :] = picked
    slot_pos, slot_vel = predict(picked[0:3], picked[3:6], picked[6:9], picked[9:12], picked[12:13])
    actives[me] = jnp.zeros((8, LANES), F32)
    actives[me, 0:3, 0:slots] = slot_pos
    actives[me, 3:6, 0:slots] = slot_vel

    pl.semaphore_wait(barrier, group + z // 2 * 2)

    def line_copy(block, other):
        return pltpu.make_async_remote_copy(
            src_ref=fields.at[block], dst_ref=fields.at[block],
            send_sem=field_send.at[other], recv_sem=field_recv.at[block],
            device_id=line_id(other), device_id_type=MESH,
        )

    def plane_copy(block, other, k):
        return pltpu.make_async_remote_copy(
            src_ref=actives.at[block], dst_ref=actives.at[block],
            send_sem=active_send.at[k], recv_sem=active_recv.at[block],
            device_id=plane_id(other), device_id_type=MESH,
        )

    def part_copy(pair, slot, other):
        return pltpu.make_async_remote_copy(
            src_ref=partial.at[pair], dst_ref=arrived.at[slot],
            send_sem=part_send.at[other], recv_sem=part_recv.at[slot],
            device_id=plane_id(other), device_id_type=MESH,
        )

    def send_lower(other, carry):
        pl.semaphore_signal(ready.at[z], inc=1, device_id=line_id(other), device_id_type=MESH)
        line_copy(z, other).start()
        return carry

    def send_higher(other, carry):
        pl.semaphore_wait(ready.at[other], 1)
        line_copy(z, other).start()
        return carry

    def send_plane(k, carry):
        plane_copy(me, plane_peer(k), k).start()
        return carry

    lax.fori_loop(0, group - 1, send_plane, 0, unroll=True)
    line_copy(z, mate).start()
    lax.fori_loop(0, z // 2 * 2, send_lower, 0)

    def take_stars(k, block):
        tile = fields[block]
        at = pl.ds(pl.multiple_of(k * stars, LANES), stars)
        turned = star_rows(tile).T
        left[at, :] = turned.astype(BF16)
        for c in range(3):
            spread[c, at, :] = jnp.broadcast_to(turned[:, STATE_ROW + c:STATE_ROW + c + 1], (stars, LANES))
        moments[:, at] = source_rows(tile).astype(BF16)

    take_stars(0, z)

    def get_plane(k, carry):
        plane_copy(plane_peer(k), plane_peer(k), k).wait_recv()
        return carry

    lax.fori_loop(0, group - 1, get_plane, 0, unroll=True)

    lane = lax.broadcasted_iota(jnp.int32, (8, LANES), 1)

    def take_slots(pair, carry):
        tile = jnp.where(lane < slots, actives[2 * pair], pltpu.roll(actives[2 * pair + 1], slots, 1))
        at = pl.ds(pl.multiple_of(pair * LANES, LANES), LANES)
        place_rows[:, at] = tile
        along[:, at] = slot_rows(tile).astype(BF16)
        return carry

    lax.fori_loop(0, group // 2, take_slots, 0, unroll=True)

    line_copy(mate, mate).wait_recv()
    take_stars(1, mate)

    blocks = 2 * stars // TILE
    rounds = lines // 2

    def stars_of(n, b):
        return pl.ds(pl.multiple_of((n * blocks + b) * TILE, TILE), TILE)

    def slots_of(i):
        return pl.ds(pl.multiple_of(i * wide_tile, wide_tile), wide_tile)

    def get_cross(n, i, b, part):
        half = slice(part * TILE // 2, (part + 1) * TILE // 2)
        rows = pl.ds(pl.multiple_of((n * blocks + b) * TILE + part * TILE // 2, TILE // 2), TILE // 2)
        cross[b, half, :] = jnp.dot(left[rows, :], along[:, slots_of(i)], preferred_element_type=F32)

    def weigh(n, i, b, beside):
        step = 0
        for lanes in range(0, wide_tile, TILE):
            cols = pl.ds(pl.multiple_of(i * wide_tile + lanes, TILE), TILE)
            state = [jnp.broadcast_to(place_rows[c:c + 1, cols], (ROWS, TILE)) for c in range(3)]
            for sub in range(0, TILE, ROWS):
                rows = pl.ds(pl.multiple_of((n * blocks + b) * TILE + sub, ROWS), ROWS)
                star = [jnp.concatenate([spread[c, rows, :]] * (TILE // LANES), 1) for c in range(3)]
                r = [star[c] - state[c] for c in range(3)]
                q = r[0] * r[0] + r[1] * r[1] + (r[2] * r[2] + SOFT2)
                inverse = lax.rsqrt(q)
                inverse2 = inverse * inverse
                w = inverse2 * inverse
                sw = (w * inverse2) * cross[b, sub:sub + ROWS, lanes:lanes + TILE]
                for kind, value in enumerate((w, sw)):
                    high = value.astype(BF16)
                    low = (value - high.astype(F32)).astype(BF16)
                    high_low[b, kind, sub:sub + ROWS, lanes:lanes + TILE] = high
                    high_low[b, kind, TILE + sub:TILE + sub + ROWS, lanes:lanes + TILE] = low
                if step in beside:
                    beside[step]()
                step += 1

    def gain(n, i, b, kind, part):
        piece = high_low[b, kind, part * TILE:(part + 1) * TILE, :]
        sums[i, kind] += jnp.dot(moments[:, stars_of(n, b)], piece, preferred_element_type=F32)

    def finish(i):
        by_w, by_s = sums[i, 0], sums[i, 1]
        by_w = by_w[0:8] + by_w[8:16] + by_w[16:24]
        by_s = by_s[0:8] + by_s[8:16] + by_s[16:24]
        row = lax.broadcasted_iota(jnp.int32, by_s.shape, 0)
        terms = by_w + pltpu.roll(jnp.where(row < 4, -3.0 * by_s, 0.0), 4, 0)
        for pair in range(share // 2):
            place = i * (share // 2) + pair
            partial[place] = terms[:, pair * LANES:(pair + 1) * LANES]
            for half in range(2):
                owner = 2 * place + half

                @pl.when(owner != me)
                def _():
                    part_copy(place, me, owner).start()

    def tile_of(j):
        return (me // share + 1 + j) % tiles

    sums[...] = jnp.zeros_like(sums)

    def pair_round(n, final):
        for part in range(2):
            get_cross(n, tile_of(0), 0, part)

        def slot_tile(j, carry):
            i = tile_of(j)
            before = jnp.where(j > 0, tile_of(j + tiles - 1), tiles)
            for b in range(blocks):
                done = (before, blocks - 1) if b == 0 else (i, b - 1)
                soon = (i, b + 1) if b < blocks - 1 else (tile_of(j + 1), 0)
                beside = {}
                steps = wide_tile // ROWS
                for part in range(2):
                    beside[part * steps // 2 + steps * 3 // 8] = functools.partial(get_cross, n, *soon, part)
                    for kind in range(2):
                        beside[part * steps // 2 + kind * steps // 4 + steps // 16] = functools.partial(gain, n, *done, kind, part)
                weigh(n, i, b, beside)
            if final:

                @pl.when(j > 0)
                def _():
                    finish(before)

            else:

                @pl.when((n == 0) & (j == 0) & (z // 2 % 2 == 0))
                def _():
                    lax.fori_loop(z // 4 * 4 + 2, z // 4 * 4 + 4, send_higher, 0)

            return carry

        lax.fori_loop(0, tiles, slot_tile, 0)
        for kind in range(2):
            for part in range(2):
                gain(n, tile_of(tiles - 1), blocks - 1, kind, part)
        if final:
            finish(tile_of(tiles - 1))

    def early_round(n, carry):
        pair_round(n, False)

        @pl.when(n == 0)
        def _():
            lax.fori_loop(z // 4 * 4 + 4, lines, send_higher, 0)

        for k in (2 * n + 2, 2 * n + 3):
            block = line_peer(k)
            line_copy(block, block).wait_recv()
            take_stars(k, block)
        return carry

    lax.fori_loop(0, rounds - 1, early_round, 0)
    pair_round(rounds - 1, True)

    arrived[me] = partial[me // 2]

    def get_part(k, carry):
        other = plane_peer(k)
        part_copy(other // 2, other, other).wait_recv()
        return carry

    lax.fori_loop(0, group - 1, get_part, 0, unroll=True)
    terms = jnp.sum(arrived[...], axis=0)
    terms = jnp.where(me % 2 == 0, terms, pltpu.roll(terms, slots, 1))
    result[0:8, :] = terms[:, 0:slots]

    def end_line(k, carry):
        line_copy(z, line_peer(k + 1)).wait_send()
        return carry

    def end_plane(k, carry):
        other = plane_peer(k)
        plane_copy(me, other, k).wait_send()
        part_copy(other // 2, me, other).wait_send()
        return carry

    lax.fori_loop(0, lines - 1, end_line, 0, unroll=True)
    lax.fori_loop(0, group - 1, end_plane, 0, unroll=True)


def correct_kernel(result, count, pos_hbm, vel_hbm, acc_hbm, jerk_hbm, pos, vel, acc, jerk, store_sem):
    terms, picked = result[0:8, :], result[8:24, :]
    x0, v0, a0, j0, h = picked[0:3], picked[3:6], picked[6:9], picked[9:12], picked[12:13]
    slot_pos, slot_vel = predict(x0, v0, a0, j0, h)
    new_acc = terms[0:3] - slot_pos * terms[3:4]
    new_jerk = terms[4:7] - slot_vel * terms[3:4] - slot_pos * terms[7:8]
    new_vel = v0 + (a0 + new_acc) * h / 2 + (j0 - new_jerk) * h * h / 12
    new_pos = x0 + (v0 + new_vel) * h / 2 + (a0 - new_acc) * h * h / 12
    live = lax.broadcasted_iota(jnp.int32, new_acc.shape, 1) < count[0]
    stores = []
    for i, (value, held, target) in enumerate(
        ((new_acc, acc, acc_hbm), (new_jerk, jerk, jerk_hbm), (new_vel, vel, vel_hbm), (new_pos, pos, pos_hbm))
    ):
        held[...] = jnp.where(live, value, 0.0)
        stores.append(pltpu.make_async_copy(held, target, store_sem.at[i]))
        stores[-1].start()
    for store in stores:
        store.wait()


def body(lines, planes, pos, vel, acc, jerk, masses, levels, index, count):
    stars, slots, group = pos.shape[1], index.shape[1], 2 * planes
    hbm = pl.BlockSpec(memory_space=pl.ANY)
    wide_tile, blocks = min(WIDE, group * slots), 2 * stars // TILE
    tiles = group * slots // wide_tile
    result = pl.pallas_call(
        functools.partial(kernel, lines, planes),
        out_shape=jax.ShapeDtypeStruct((24, slots), F32),
        in_specs=[hbm] * 7,
        out_specs=pl.BlockSpec(memory_space=pltpu.VMEM),
        scratch_shapes=[
            pltpu.VMEM((3, stars), F32),
            pltpu.VMEM((3, stars), F32),
            pltpu.VMEM((3, stars), F32),
            pltpu.VMEM((3, stars), F32),
            pltpu.VMEM((stars,), F32),
            pltpu.VMEM((stars,), jnp.int32),
            pltpu.VMEM((1, slots), jnp.int32),
            pltpu.VMEM((16, stars), F32),
            pltpu.VMEM((lines, 8, stars), F32),
            pltpu.VMEM((group, 8, LANES), F32),
            pltpu.VMEM((group, 8, LANES), F32),
            pltpu.VMEM((group // 2, 8, LANES), F32),
            pltpu.VMEM((3, lines * stars, LANES), F32),
            pltpu.VMEM((lines * stars, KDIM), BF16),
            pltpu.VMEM((8, group * slots), F32),
            pltpu.VMEM((KDIM, group * slots), BF16),
            pltpu.VMEM((SOURCES, lines * stars), BF16),
            pltpu.VMEM((blocks, TILE, wide_tile), F32),
            pltpu.VMEM((blocks, 2, 2 * TILE, wide_tile), BF16),
            pltpu.VMEM((tiles + 1, 2, SOURCES, wide_tile), F32),
            pltpu.SemaphoreType.DMA((7,)),
            pltpu.SemaphoreType.REGULAR((lines,)),
            pltpu.SemaphoreType.DMA((lines,)),
            pltpu.SemaphoreType.DMA((lines,)),
            pltpu.SemaphoreType.DMA((group,)),
            pltpu.SemaphoreType.DMA((group,)),
            pltpu.SemaphoreType.DMA((group,)),
            pltpu.SemaphoreType.DMA((group,)),
        ],
        compiler_params=pltpu.CompilerParams(collective_id=0, has_side_effects=True, vmem_limit_bytes=VMEM_LIMIT),
        name="forces",
    )(pos, vel, acc, jerk, masses, levels, index)
    three = jax.ShapeDtypeStruct((3, slots), F32)
    return pl.pallas_call(
        correct_kernel,
        out_shape=(three,) * 4,
        in_specs=[pl.BlockSpec(memory_space=pltpu.VMEM), pl.BlockSpec(memory_space=pltpu.SMEM)],
        out_specs=(hbm,) * 4,
        scratch_shapes=[pltpu.VMEM((3, slots), F32)] * 4 + [pltpu.SemaphoreType.DMA((4,))],
        compiler_params=pltpu.CompilerParams(vmem_limit_bytes=VMEM_LIMIT),
        name="correct",
    )(result, count)


def solution(mesh):
    lines, planes = mesh.shape["wide"] // 2, mesh.shape["sum"]
    both = ("wide", "sum")
    in_specs = (P(None, both),) * 4 + (P(both), P(both), P(both, None), P(both))
    return jax.shard_map(
        functools.partial(body, lines, planes), mesh=mesh, in_specs=in_specs,
        out_specs=(P(None, both),) * 4, check_vma=False,
    )
```

```python
import functools

import jax
import jax.numpy as jnp
from jax import lax
from jax.experimental import pallas as pl
from jax.experimental.pallas import tpu as pltpu
from jax.sharding import PartitionSpec as P

SOFT2 = 0.0025
STEP0 = 0.5
MESH = pl.DeviceIdType.MESH
F32 = jnp.float32
BF16 = jnp.bfloat16
LANES = 128
TILE = 256
KDIM = 128
ROWS = 16
SOURCES = 32
VMEM_LIMIT = 63 * 1024 * 1024


def step_of(levels):
    low = jnp.where(levels == 0, STEP0, STEP0 / 2)
    high = jnp.where(levels == 2, STEP0 / 4, STEP0 / 8)
    return jnp.where(levels < 2, low, high).astype(F32)


def predict(pos, vel, acc, jerk, step):
    pred_pos = pos + step * (vel + step * (acc / 2 + step * jerk / 6))
    pred_vel = vel + step * (acc + step * jerk / 2)
    return pred_pos, pred_vel


def pieces(value):
    first = value.astype(BF16).astype(F32)
    rest = value - first
    second = rest.astype(BF16).astype(F32)
    third = (rest - second).astype(BF16).astype(F32)
    return first, second, third


def split_state(tile):
    row = lax.broadcasted_iota(jnp.int32, tile.shape, 0)
    state = jnp.where(row < 6, tile, 0.0)
    grid = jnp.floor(state * 16.0 + 0.5) * 0.0625
    rest = state - grid
    near = rest.astype(BF16).astype(F32)
    far = (rest - near).astype(BF16).astype(F32)
    return grid, near, far


def own_terms(grid, near, far):
    small = near + far
    gp, gv, sp, sv = grid[0:3], grid[3:6], small[0:3], small[3:6]

    def total(value):
        return jnp.sum(value, axis=0, keepdims=True)

    square, square_rest = total(gp * gp), total(2.0 * gp * sp + sp * sp) + 0.5 * SOFT2
    cross, cross_rest = total(gp * gv), total(gp * sv + sp * gv + sp * sv)
    return list(pieces(square)[:2]), list(pieces(square_rest)), list(pieces(cross)[:2] + pieces(cross_rest))


def star_rows(tile):
    width = tile.shape[1]
    grid, near, far = split_state(tile)
    square, square_rest, cross = own_terms(grid, near, far)

    def ones(count):
        return jnp.ones((count, width), F32)

    first = jnp.concatenate([grid[0:3]] + square + [ones(2), jnp.zeros((1, width), F32)], 0)
    second = jnp.concatenate([grid[3:6]] + cross, 0)
    third = jnp.concatenate([ones(5)] + square_rest, 0)
    pad = jnp.zeros((KDIM - 88, width), F32)
    return jnp.concatenate([first, second, third] + [grid] * 2 + [near] * 3 + [far] * 3 + [pad], 0)


def slot_rows(tile):
    width = tile.shape[1]
    grid, near, far = split_state(tile)
    square, square_rest, cross = own_terms(grid, near, far)
    row = lax.broadcasted_iota(jnp.int32, tile.shape, 0)

    def ones(count):
        return jnp.ones((count, width), F32)

    def none(count):
        return jnp.zeros((count, width), F32)

    def for_square(part):
        return jnp.where(row < 3, -2.0 * part, 0.0)

    def for_cross(part):
        return jnp.concatenate([-part[3:6], -part[0:3], part[6:8]], 0)

    first = jnp.concatenate([-2.0 * grid[0:3], ones(2)] + square + [none(1)], 0)
    third = jnp.concatenate(square_rest + [none(2), ones(3)], 0)
    parts = (near, far) + (grid, near, far) * 2
    pad = none(KDIM - 88)
    in_square = jnp.concatenate([first, none(8), third] + [for_square(part) for part in parts] + [pad], 0)
    first = jnp.concatenate([-grid[3:6], none(5)], 0)
    second = jnp.concatenate([-grid[0:3], ones(5)], 0)
    third = jnp.concatenate(cross + [none(3)], 0)
    in_cross = jnp.concatenate([first, second, third] + [for_cross(part) for part in parts] + [pad], 0)
    return in_square, in_cross


def source_rows(tile):
    weight = tile[6:7]
    none = jnp.zeros_like(weight)
    sources = jnp.concatenate([weight * tile[0:3], weight, weight * tile[3:6], none], 0)
    return jnp.concatenate(list(pieces(sources)) + [jnp.zeros((SOURCES - 24, tile.shape[1]), F32)], 0)


def kernel(
    lines, planes, pos_hbm, vel_hbm, acc_hbm, jerk_hbm, mass_hbm, level_hbm, index_hbm, result,
    pos, vel, acc, jerk, mass, level, index, stage, fields, actives, arrived, partial,
    left, along, moments, both, high_low, sums,
    load_sem, ready, field_send, field_recv, active_send, active_recv, part_send, part_recv,
):
    group = 2 * planes
    stars, slots = pos.shape[1], index.shape[1]
    tiles = group * slots // TILE
    share = TILE // slots
    wide, s = lax.axis_index("wide"), lax.axis_index("sum")
    z, core = wide // 2, wide % 2
    me = core * planes + s

    def line_peer(k):
        other, bit = z, 1
        while bit < lines:
            other = other + (k // bit) % 2 * bit * (1 - 2 * ((z // bit) % 2))
            bit *= 2
        return other

    def plane_peer(k):
        return (me + 1 + k) % group

    def line_id(other):
        return (other * 2 + core, s)

    def plane_id(other):
        return (z * 2 + other // planes, other % planes)

    loads = [
        pltpu.make_async_copy(source, target, load_sem.at[i])
        for i, (source, target) in enumerate(
            zip((pos_hbm, vel_hbm, acc_hbm, jerk_hbm, mass_hbm, level_hbm, index_hbm), (pos, vel, acc, jerk, mass, level, index))
        )
    ]
    for load in loads:
        load.start()

    barrier = pltpu.get_barrier_semaphore()

    def greet_line(other, carry):
        pl.semaphore_signal(barrier, inc=1, device_id=line_id(other), device_id_type=MESH)
        return carry

    def greet_plane(k, carry):
        pl.semaphore_signal(barrier, inc=1, device_id=plane_id(plane_peer(k)), device_id_type=MESH)
        return carry

    lax.fori_loop(0, group - 1, greet_plane, 0, unroll=True)
    mate = line_peer(1)
    greet_line(mate, 0)
    lax.fori_loop(z // 2 * 2 + 2, lines, greet_line, 0)
    for load in loads:
        load.wait()

    step = step_of(level[...].reshape(1, stars))
    pred_pos, pred_vel = predict(pos[...], vel[...], acc[...], jerk[...], step)
    fields[z, 0:3, :] = pred_pos
    fields[z, 3:6, :] = pred_vel
    fields[z, 6:7, :] = mass[...].reshape(1, stars)
    fields[z, 7:8, :] = jnp.zeros_like(step)

    stage[0:3, :] = pos[...]
    stage[3:6, :] = vel[...]
    stage[6:9, :] = acc[...]
    stage[9:12, :] = jerk[...]
    stage[12:13, :] = step
    stage[13:16, :] = jnp.zeros((3, stars), F32)
    chosen = lax.broadcasted_iota(jnp.int32, (stars, slots), 0) == index[...]
    chosen = chosen.astype(F32).astype(BF16)
    picked = [jnp.dot(part.astype(BF16), chosen, preferred_element_type=F32) for part in pieces(stage[...])]
    picked = (picked[0] + picked[1]) + picked[2]
    result[8:24, :] = picked
    slot_pos, slot_vel = predict(picked[0:3], picked[3:6], picked[6:9], picked[9:12], picked[12:13])
    actives[me] = jnp.zeros((8, LANES), F32)
    actives[me, 0:3, 0:slots] = slot_pos
    actives[me, 3:6, 0:slots] = slot_vel

    pl.semaphore_wait(barrier, group + z // 2 * 2)

    def line_copy(block, other):
        return pltpu.make_async_remote_copy(
            src_ref=fields.at[block], dst_ref=fields.at[block],
            send_sem=field_send.at[other], recv_sem=field_recv.at[block],
            device_id=line_id(other), device_id_type=MESH,
        )

    def plane_copy(block, other, k):
        return pltpu.make_async_remote_copy(
            src_ref=actives.at[block], dst_ref=actives.at[block],
            send_sem=active_send.at[k], recv_sem=active_recv.at[block],
            device_id=plane_id(other), device_id_type=MESH,
        )

    def part_copy(pair, slot, other):
        return pltpu.make_async_remote_copy(
            src_ref=partial.at[pair], dst_ref=arrived.at[slot],
            send_sem=part_send.at[other], recv_sem=part_recv.at[slot],
            device_id=plane_id(other), device_id_type=MESH,
        )

    def send_lower(other, carry):
        pl.semaphore_signal(ready.at[z], inc=1, device_id=line_id(other), device_id_type=MESH)
        line_copy(z, other).start()
        return carry

    def send_higher(other, carry):
        pl.semaphore_wait(ready.at[other], 1)
        line_copy(z, other).start()
        return carry

    def send_plane(k, carry):
        plane_copy(me, plane_peer(k), k).start()
        return carry

    lax.fori_loop(0, group - 1, send_plane, 0, unroll=True)
    line_copy(z, mate).start()
    lax.fori_loop(0, z // 2 * 2, send_lower, 0)

    def take_stars(k, block):
        tile = fields[block]
        at = pl.ds(pl.multiple_of(k * stars, LANES), stars)
        left[at, :] = star_rows(tile).T.astype(BF16)
        moments[:, at] = source_rows(tile).astype(BF16)

    take_stars(0, z)

    def get_plane(k, carry):
        plane_copy(plane_peer(k), plane_peer(k), k).wait_recv()
        return carry

    lax.fori_loop(0, group - 1, get_plane, 0, unroll=True)

    lane = lax.broadcasted_iota(jnp.int32, (8, LANES), 1)

    def take_slots(pair, carry):
        tile = jnp.where(lane < slots, actives[2 * pair], pltpu.roll(actives[2 * pair + 1], slots, 1))
        start = pair * LANES // TILE * 2 * TILE + pair * LANES % TILE
        for offset, value in zip((0, TILE), slot_rows(tile)):
            along[:, pl.ds(pl.multiple_of(start + offset, LANES), LANES)] = value.astype(BF16)
        return carry

    lax.fori_loop(0, group // 2, take_slots, 0, unroll=True)

    line_copy(mate, mate).wait_recv()
    take_stars(1, mate)

    blocks = 2 * stars // TILE
    rounds = lines // 2

    def stars_of(n, b):
        return pl.ds(pl.multiple_of((n * blocks + b) * TILE, TILE), TILE)

    def relate(n, i, b, part):
        half = slice(part * TILE // 2, (part + 1) * TILE // 2)
        rows = pl.ds(pl.multiple_of((n * blocks + b) * TILE + part * TILE // 2, TILE // 2), TILE // 2)
        cols = pl.ds(pl.multiple_of(i * 2 * TILE, 2 * TILE), 2 * TILE)
        both[b, half, :] = jnp.dot(left[rows, :], along[:, cols], preferred_element_type=F32)

    def weigh(b, beside):
        for sub in range(0, TILE, ROWS):
            inverse = lax.rsqrt(both[b, sub:sub + ROWS, 0:TILE])
            inverse2 = inverse * inverse
            w = inverse2 * inverse
            sw = (w * inverse2) * both[b, sub:sub + ROWS, TILE:2 * TILE]
            for kind, value in enumerate((w, sw)):
                high = value.astype(BF16)
                high_low[b, kind, sub:sub + ROWS, :] = high
                high_low[b, kind, TILE + sub:TILE + sub + ROWS, :] = (value - high.astype(F32)).astype(BF16)
            if sub // ROWS in beside:
                beside[sub // ROWS]()

    def gain(n, i, b, kind, part):
        piece = high_low[b, kind, part * TILE:(part + 1) * TILE, :]
        sums[i, kind] += jnp.dot(moments[:, stars_of(n, b)], piece, preferred_element_type=F32)

    def finish(i):
        by_w, by_s = sums[i, 0], sums[i, 1]
        by_w = by_w[0:8] + by_w[8:16] + by_w[16:24]
        by_s = by_s[0:8] + by_s[8:16] + by_s[16:24]
        row = lax.broadcasted_iota(jnp.int32, by_s.shape, 0)
        terms = by_w + pltpu.roll(jnp.where(row < 4, -3.0 * by_s, 0.0), 4, 0)
        for pair in range(share // 2):
            place = i * (share // 2) + pair
            partial[place] = terms[:, pair * LANES:(pair + 1) * LANES]
            for half in range(2):
                owner = 2 * place + half

                @pl.when(owner != me)
                def _():
                    part_copy(place, me, owner).start()

    def tile_of(j):
        return (me // share + 1 + j) % tiles

    sums[...] = jnp.zeros_like(sums)

    def pair_round(n, final):
        for part in range(2):
            relate(n, tile_of(0), 0, part)

        def slot_tile(j, carry):
            i = tile_of(j)
            before = jnp.where(j > 0, tile_of(j + tiles - 1), tiles)
            for b in range(blocks):
                done = (before, blocks - 1) if b == 0 else (i, b - 1)
                soon = (i, b + 1) if b < blocks - 1 else (tile_of(j + 1), 0)
                beside = {}
                for part in range(2):
                    beside[8 * part + 3] = functools.partial(relate, n, *soon, part)
                    for kind in range(2):
                        beside[8 * part + 4 * kind + 1] = functools.partial(gain, n, *done, kind, part)
                weigh(b, beside)
            if final:

                @pl.when(j > 0)
                def _():
                    finish(before)

            else:

                @pl.when((n == 0) & (j == 1) & (z // 2 % 2 == 0))
                def _():
                    lax.fori_loop(z // 4 * 4 + 2, z // 4 * 4 + 4, send_higher, 0)

            return carry

        lax.fori_loop(0, tiles, slot_tile, 0, unroll=1 if final else 2)
        for kind in range(2):
            for part in range(2):
                gain(n, tile_of(tiles - 1), blocks - 1, kind, part)
        if final:
            finish(tile_of(tiles - 1))

    def early_round(n, carry):
        pair_round(n, False)

        @pl.when(n == 0)
        def _():
            lax.fori_loop(z // 4 * 4 + 4, lines, send_higher, 0)

        for k in (2 * n + 2, 2 * n + 3):
            block = line_peer(k)
            line_copy(block, block).wait_recv()
            take_stars(k, block)
        return carry

    lax.fori_loop(0, rounds - 1, early_round, 0)
    pair_round(rounds - 1, True)

    arrived[me] = partial[me // 2]

    def get_part(k, carry):
        other = plane_peer(k)
        part_copy(other // 2, other, other).wait_recv()
        return carry

    lax.fori_loop(0, group - 1, get_part, 0, unroll=True)
    terms = jnp.sum(arrived[...], axis=0)
    terms = jnp.where(me % 2 == 0, terms, pltpu.roll(terms, slots, 1))
    result[0:8, :] = terms[:, 0:slots]

    def end_line(k, carry):
        line_copy(z, line_peer(k + 1)).wait_send()
        return carry

    def end_plane(k, carry):
        other = plane_peer(k)
        plane_copy(me, other, k).wait_send()
        part_copy(other // 2, me, other).wait_send()
        return carry

    lax.fori_loop(0, lines - 1, end_line, 0, unroll=True)
    lax.fori_loop(0, group - 1, end_plane, 0, unroll=True)


def correct_kernel(result, count, pos_hbm, vel_hbm, acc_hbm, jerk_hbm, pos, vel, acc, jerk, store_sem):
    terms, picked = result[0:8, :], result[8:24, :]
    x0, v0, a0, j0, h = picked[0:3], picked[3:6], picked[6:9], picked[9:12], picked[12:13]
    slot_pos, slot_vel = predict(x0, v0, a0, j0, h)
    new_acc = terms[0:3] - slot_pos * terms[3:4]
    new_jerk = terms[4:7] - slot_vel * terms[3:4] - slot_pos * terms[7:8]
    new_vel = v0 + (a0 + new_acc) * h / 2 + (j0 - new_jerk) * h * h / 12
    new_pos = x0 + (v0 + new_vel) * h / 2 + (a0 - new_acc) * h * h / 12
    live = lax.broadcasted_iota(jnp.int32, new_acc.shape, 1) < count[0]
    stores = []
    for i, (value, held, target) in enumerate(
        ((new_acc, acc, acc_hbm), (new_jerk, jerk, jerk_hbm), (new_vel, vel, vel_hbm), (new_pos, pos, pos_hbm))
    ):
        held[...] = jnp.where(live, value, 0.0)
        stores.append(pltpu.make_async_copy(held, target, store_sem.at[i]))
        stores[-1].start()
    for store in stores:
        store.wait()


def body(lines, planes, pos, vel, acc, jerk, masses, levels, index, count):
    stars, slots, group = pos.shape[1], index.shape[1], 2 * planes
    hbm = pl.BlockSpec(memory_space=pl.ANY)
    tiles, blocks = group * slots // TILE, 2 * stars // TILE
    result = pl.pallas_call(
        functools.partial(kernel, lines, planes),
        out_shape=jax.ShapeDtypeStruct((24, slots), F32),
        in_specs=[hbm] * 7,
        out_specs=pl.BlockSpec(memory_space=pltpu.VMEM),
        scratch_shapes=[
            pltpu.VMEM((3, stars), F32),
            pltpu.VMEM((3, stars), F32),
            pltpu.VMEM((3, stars), F32),
            pltpu.VMEM((3, stars), F32),
            pltpu.VMEM((stars,), F32),
            pltpu.VMEM((stars,), jnp.int32),
            pltpu.VMEM((1, slots), jnp.int32),
            pltpu.VMEM((16, stars), F32),
            pltpu.VMEM((lines, 8, stars), F32),
            pltpu.VMEM((group, 8, LANES), F32),
            pltpu.VMEM((group, 8, LANES), F32),
            pltpu.VMEM((group // 2, 8, LANES), F32),
            pltpu.VMEM((lines * stars, KDIM), BF16),
            pltpu.VMEM((KDIM, 2 * group * slots), BF16),
            pltpu.VMEM((SOURCES, lines * stars), BF16),
            pltpu.VMEM((blocks, TILE, 2 * TILE), F32),
            pltpu.VMEM((blocks, 2, 2 * TILE, TILE), BF16),
            pltpu.VMEM((tiles + 1, 2, SOURCES, TILE), F32),
            pltpu.SemaphoreType.DMA((7,)),
            pltpu.SemaphoreType.REGULAR((lines,)),
            pltpu.SemaphoreType.DMA((lines,)),
            pltpu.SemaphoreType.DMA((lines,)),
            pltpu.SemaphoreType.DMA((group,)),
            pltpu.SemaphoreType.DMA((group,)),
            pltpu.SemaphoreType.DMA((group,)),
            pltpu.SemaphoreType.DMA((group,)),
        ],
        compiler_params=pltpu.CompilerParams(collective_id=0, has_side_effects=True, vmem_limit_bytes=VMEM_LIMIT),
        name="forces",
    )(pos, vel, acc, jerk, masses, levels, index)
    three = jax.ShapeDtypeStruct((3, slots), F32)
    return pl.pallas_call(
        correct_kernel,
        out_shape=(three,) * 4,
        in_specs=[pl.BlockSpec(memory_space=pltpu.VMEM), pl.BlockSpec(memory_space=pltpu.SMEM)],
        out_specs=(hbm,) * 4,
        scratch_shapes=[pltpu.VMEM((3, slots), F32)] * 4 + [pltpu.SemaphoreType.DMA((4,))],
        compiler_params=pltpu.CompilerParams(vmem_limit_bytes=VMEM_LIMIT),
        name="correct",
    )(result, count)


def solution(mesh):
    lines, planes = mesh.shape["wide"] // 2, mesh.shape["sum"]
    both = ("wide", "sum")
    in_specs = (P(None, both),) * 4 + (P(both), P(both), P(both, None), P(both))
    return jax.shard_map(
        functools.partial(body, lines, planes), mesh=mesh, in_specs=in_specs,
        out_specs=(P(None, both),) * 4, check_vma=False,
    )
```

```python
import functools

import jax
import jax.numpy as jnp
from jax import lax
from jax.experimental import pallas as pl
from jax.experimental.pallas import tpu as pltpu
from jax.sharding import PartitionSpec as P

SOFT2 = 0.0025
STEP0 = 0.5
MESH = pl.DeviceIdType.MESH
F32 = jnp.float32
BF16 = jnp.bfloat16
LANES = 128
TILE = 256
KDIM = 128
ROWS = 16
SOURCES = 32
VMEM_LIMIT = 63 * 1024 * 1024


def step_of(levels):
    low = jnp.where(levels == 0, STEP0, STEP0 / 2)
    high = jnp.where(levels == 2, STEP0 / 4, STEP0 / 8)
    return jnp.where(levels < 2, low, high).astype(F32)


def predict(pos, vel, acc, jerk, step):
    pred_pos = pos + step * (vel + step * (acc / 2 + step * jerk / 6))
    pred_vel = vel + step * (acc + step * jerk / 2)
    return pred_pos, pred_vel


def pieces(value):
    first = value.astype(BF16).astype(F32)
    rest = value - first
    second = rest.astype(BF16).astype(F32)
    third = (rest - second).astype(BF16).astype(F32)
    return first, second, third


def split_state(tile):
    row = lax.broadcasted_iota(jnp.int32, tile.shape, 0)
    state = jnp.where(row < 6, tile, 0.0)
    grid = jnp.floor(state * 16.0 + 0.5) * 0.0625
    rest = state - grid
    near = rest.astype(BF16).astype(F32)
    far = (rest - near).astype(BF16).astype(F32)
    return grid, near, far


def own_terms(grid, near, far):
    small = near + far
    gp, gv, sp, sv = grid[0:3], grid[3:6], small[0:3], small[3:6]

    def total(value):
        return jnp.sum(value, axis=0, keepdims=True)

    square, square_rest = total(gp * gp), total(2.0 * gp * sp + sp * sp) + 0.5 * SOFT2
    cross, cross_rest = total(gp * gv), total(gp * sv + sp * gv + sp * sv)
    return list(pieces(square)[:2]), list(pieces(square_rest)), list(pieces(cross)[:2] + pieces(cross_rest))


def star_rows(tile):
    width = tile.shape[1]
    grid, near, far = split_state(tile)
    square, square_rest, cross = own_terms(grid, near, far)

    def ones(count):
        return jnp.ones((count, width), F32)

    first = jnp.concatenate([grid[0:3]] + square + [ones(2), jnp.zeros((1, width), F32)], 0)
    second = jnp.concatenate([grid[3:6]] + cross, 0)
    third = jnp.concatenate([ones(5)] + square_rest, 0)
    pad = jnp.zeros((KDIM - 88, width), F32)
    return jnp.concatenate([first, second, third] + [grid] * 2 + [near] * 3 + [far] * 3 + [pad], 0)


def slot_rows(tile):
    width = tile.shape[1]
    grid, near, far = split_state(tile)
    square, square_rest, cross = own_terms(grid, near, far)
    row = lax.broadcasted_iota(jnp.int32, tile.shape, 0)

    def ones(count):
        return jnp.ones((count, width), F32)

    def none(count):
        return jnp.zeros((count, width), F32)

    def for_square(part):
        return jnp.where(row < 3, -2.0 * part, 0.0)

    def for_cross(part):
        return jnp.concatenate([-part[3:6], -part[0:3], part[6:8]], 0)

    first = jnp.concatenate([-2.0 * grid[0:3], ones(2)] + square + [none(1)], 0)
    third = jnp.concatenate(square_rest + [none(2), ones(3)], 0)
    parts = (near, far) + (grid, near, far) * 2
    pad = none(KDIM - 88)
    in_square = jnp.concatenate([first, none(8), third] + [for_square(part) for part in parts] + [pad], 0)
    first = jnp.concatenate([-grid[3:6], none(5)], 0)
    second = jnp.concatenate([-grid[0:3], ones(5)], 0)
    third = jnp.concatenate(cross + [none(3)], 0)
    in_cross = jnp.concatenate([first, second, third] + [for_cross(part) for part in parts] + [pad], 0)
    return in_square, in_cross


def source_rows(tile):
    weight = tile[6:7]
    none = jnp.zeros_like(weight)
    sources = jnp.concatenate([weight * tile[0:3], weight, weight * tile[3:6], none], 0)
    return jnp.concatenate(list(pieces(sources)) + [jnp.zeros((SOURCES - 24, tile.shape[1]), F32)], 0)


def kernel(
    lines, planes, pos_hbm, vel_hbm, acc_hbm, jerk_hbm, mass_hbm, level_hbm, index_hbm, result,
    pos, vel, acc, jerk, mass, level, index, stage, fields, actives, arrived, partial,
    left, along, moments, high_low, sums,
    load_sem, ready, field_send, field_recv, active_send, active_recv, part_send, part_recv,
):
    group = 2 * planes
    stars, slots = pos.shape[1], index.shape[1]
    tiles = group * slots // TILE
    share = TILE // slots
    wide, s = lax.axis_index("wide"), lax.axis_index("sum")
    z, core = wide // 2, wide % 2
    me = core * planes + s

    def line_peer(k):
        other, bit = z, 1
        while bit < lines:
            other = other + (k // bit) % 2 * bit * (1 - 2 * ((z // bit) % 2))
            bit *= 2
        return other

    def plane_peer(k):
        return (me + 1 + k) % group

    def line_id(other):
        return (other * 2 + core, s)

    def plane_id(other):
        return (z * 2 + other // planes, other % planes)

    loads = [
        pltpu.make_async_copy(source, target, load_sem.at[i])
        for i, (source, target) in enumerate(
            zip((pos_hbm, vel_hbm, acc_hbm, jerk_hbm, mass_hbm, level_hbm, index_hbm), (pos, vel, acc, jerk, mass, level, index))
        )
    ]
    for load in loads:
        load.start()

    barrier = pltpu.get_barrier_semaphore()

    def greet_line(other, carry):
        pl.semaphore_signal(barrier, inc=1, device_id=line_id(other), device_id_type=MESH)
        return carry

    def greet_plane(k, carry):
        pl.semaphore_signal(barrier, inc=1, device_id=plane_id(plane_peer(k)), device_id_type=MESH)
        return carry

    lax.fori_loop(0, group - 1, greet_plane, 0, unroll=True)
    mate = line_peer(1)
    greet_line(mate, 0)
    lax.fori_loop(z // 2 * 2 + 2, lines, greet_line, 0)
    for load in loads:
        load.wait()

    step = step_of(level[...].reshape(1, stars))
    pred_pos, pred_vel = predict(pos[...], vel[...], acc[...], jerk[...], step)
    fields[z, 0:3, :] = pred_pos
    fields[z, 3:6, :] = pred_vel
    fields[z, 6:7, :] = mass[...].reshape(1, stars)
    fields[z, 7:8, :] = jnp.zeros_like(step)

    stage[0:3, :] = pos[...]
    stage[3:6, :] = vel[...]
    stage[6:9, :] = acc[...]
    stage[9:12, :] = jerk[...]
    stage[12:13, :] = step
    stage[13:16, :] = jnp.zeros((3, stars), F32)
    chosen = lax.broadcasted_iota(jnp.int32, (stars, slots), 0) == index[...]
    chosen = chosen.astype(F32).astype(BF16)
    picked = [jnp.dot(part.astype(BF16), chosen, preferred_element_type=F32) for part in pieces(stage[...])]
    picked = (picked[0] + picked[1]) + picked[2]
    result[8:24, :] = picked
    slot_pos, slot_vel = predict(picked[0:3], picked[3:6], picked[6:9], picked[9:12], picked[12:13])
    actives[me] = jnp.zeros((8, LANES), F32)
    actives[me, 0:3, 0:slots] = slot_pos
    actives[me, 3:6, 0:slots] = slot_vel

    pl.semaphore_wait(barrier, group + z // 2 * 2)

    def line_copy(block, other):
        return pltpu.make_async_remote_copy(
            src_ref=fields.at[block], dst_ref=fields.at[block],
            send_sem=field_send.at[other], recv_sem=field_recv.at[block],
            device_id=line_id(other), device_id_type=MESH,
        )

    def plane_copy(block, other, k):
        return pltpu.make_async_remote_copy(
            src_ref=actives.at[block], dst_ref=actives.at[block],
            send_sem=active_send.at[k], recv_sem=active_recv.at[block],
            device_id=plane_id(other), device_id_type=MESH,
        )

    def part_copy(pair, slot, other):
        return pltpu.make_async_remote_copy(
            src_ref=partial.at[pair], dst_ref=arrived.at[slot],
            send_sem=part_send.at[other], recv_sem=part_recv.at[slot],
            device_id=plane_id(other), device_id_type=MESH,
        )

    def send_lower(other, carry):
        pl.semaphore_signal(ready.at[z], inc=1, device_id=line_id(other), device_id_type=MESH)
        line_copy(z, other).start()
        return carry

    def send_higher(other, carry):
        pl.semaphore_wait(ready.at[other], 1)
        line_copy(z, other).start()
        return carry

    def send_plane(k, carry):
        plane_copy(me, plane_peer(k), k).start()
        return carry

    lax.fori_loop(0, group - 1, send_plane, 0, unroll=True)
    line_copy(z, mate).start()
    lax.fori_loop(0, z // 2 * 2, send_lower, 0)

    def take_stars(k, block):
        tile = fields[block]
        at = pl.ds(pl.multiple_of(k * stars, LANES), stars)
        left[at, :] = star_rows(tile).T.astype(BF16)
        moments[:, at] = source_rows(tile).astype(BF16)

    take_stars(0, z)

    def get_plane(k, carry):
        plane_copy(plane_peer(k), plane_peer(k), k).wait_recv()
        return carry

    lax.fori_loop(0, group - 1, get_plane, 0, unroll=True)

    lane = lax.broadcasted_iota(jnp.int32, (8, LANES), 1)

    def take_slots(pair, carry):
        tile = jnp.where(lane < slots, actives[2 * pair], pltpu.roll(actives[2 * pair + 1], slots, 1))
        start = pair * LANES // TILE * 2 * TILE + pair * LANES % TILE
        for offset, value in zip((0, TILE), slot_rows(tile)):
            along[:, pl.ds(pl.multiple_of(start + offset, LANES), LANES)] = value.astype(BF16)
        return carry

    lax.fori_loop(0, group // 2, take_slots, 0, unroll=True)

    line_copy(mate, mate).wait_recv()
    take_stars(1, mate)

    blocks = 2 * stars // TILE
    rounds = lines // 2

    def stars_of(n, b):
        return pl.ds(pl.multiple_of((n * blocks + b) * TILE, TILE), TILE)

    def weigh(n, i, b, beside):
        cols = pl.ds(pl.multiple_of(i * 2 * TILE, 2 * TILE), 2 * TILE)
        both = jnp.dot(left[stars_of(n, b), :], along[:, cols], preferred_element_type=F32)
        for sub in range(0, TILE, ROWS):
            inverse = lax.rsqrt(both[sub:sub + ROWS, 0:TILE])
            inverse2 = inverse * inverse
            w = inverse2 * inverse
            sw = (w * inverse2) * both[sub:sub + ROWS, TILE:2 * TILE]
            for kind, value in enumerate((w, sw)):
                high = value.astype(BF16)
                high_low[b, kind, sub:sub + ROWS, :] = high
                high_low[b, kind, TILE + sub:TILE + sub + ROWS, :] = (value - high.astype(F32)).astype(BF16)
            if sub // ROWS in beside:
                beside[sub // ROWS]()

    def gain(n, i, b, kind, part):
        piece = high_low[b, kind, part * TILE:(part + 1) * TILE, :]
        sums[i, kind] += jnp.dot(moments[:, stars_of(n, b)], piece, preferred_element_type=F32)

    def finish(i):
        by_w, by_s = sums[i, 0], sums[i, 1]
        by_w = by_w[0:8] + by_w[8:16] + by_w[16:24]
        by_s = by_s[0:8] + by_s[8:16] + by_s[16:24]
        row = lax.broadcasted_iota(jnp.int32, by_s.shape, 0)
        terms = by_w + pltpu.roll(jnp.where(row < 4, -3.0 * by_s, 0.0), 4, 0)
        for pair in range(share // 2):
            place = i * (share // 2) + pair
            partial[place] = terms[:, pair * LANES:(pair + 1) * LANES]
            for half in range(2):
                owner = 2 * place + half

                @pl.when(owner != me)
                def _():
                    part_copy(place, me, owner).start()

    def tile_of(j):
        return (me // share + 1 + j) % tiles

    sums[...] = jnp.zeros_like(sums)

    def pair_round(n, final):

        def slot_tile(j, carry):
            i = tile_of(j)
            before = jnp.where(j > 0, tile_of(j + tiles - 1), tiles)
            for b in range(blocks):
                done = (before, blocks - 1) if b == 0 else (i, b - 1)
                beside = {}
                for part in range(2):
                    for kind in range(2):
                        beside[8 * part + 4 * kind + 1] = functools.partial(gain, n, *done, kind, part)
                weigh(n, i, b, beside)
            if final:

                @pl.when(j > 0)
                def _():
                    finish(before)

            else:

                @pl.when((n == 0) & (j == 1) & (z // 2 % 2 == 0))
                def _():
                    lax.fori_loop(z // 4 * 4 + 2, z // 4 * 4 + 4, send_higher, 0)

            return carry

        lax.fori_loop(0, tiles, slot_tile, 0, unroll=1 if final else 2)
        for kind in range(2):
            for part in range(2):
                gain(n, tile_of(tiles - 1), blocks - 1, kind, part)
        if final:
            finish(tile_of(tiles - 1))

    def early_round(n, carry):
        pair_round(n, False)

        @pl.when(n == 0)
        def _():
            lax.fori_loop(z // 4 * 4 + 4, lines, send_higher, 0)

        for k in (2 * n + 2, 2 * n + 3):
            block = line_peer(k)
            line_copy(block, block).wait_recv()
            take_stars(k, block)
        return carry

    lax.fori_loop(0, rounds - 1, early_round, 0)
    pair_round(rounds - 1, True)

    arrived[me] = partial[me // 2]

    def get_part(k, carry):
        other = plane_peer(k)
        part_copy(other // 2, other, other).wait_recv()
        return carry

    lax.fori_loop(0, group - 1, get_part, 0, unroll=True)
    terms = jnp.sum(arrived[...], axis=0)
    terms = jnp.where(me % 2 == 0, terms, pltpu.roll(terms, slots, 1))
    result[0:8, :] = terms[:, 0:slots]

    def end_line(k, carry):
        line_copy(z, line_peer(k + 1)).wait_send()
        return carry

    def end_plane(k, carry):
        other = plane_peer(k)
        plane_copy(me, other, k).wait_send()
        part_copy(other // 2, me, other).wait_send()
        return carry

    lax.fori_loop(0, lines - 1, end_line, 0, unroll=True)
    lax.fori_loop(0, group - 1, end_plane, 0, unroll=True)


def correct_kernel(result, count, pos_hbm, vel_hbm, acc_hbm, jerk_hbm, pos, vel, acc, jerk, store_sem):
    terms, picked = result[0:8, :], result[8:24, :]
    x0, v0, a0, j0, h = picked[0:3], picked[3:6], picked[6:9], picked[9:12], picked[12:13]
    slot_pos, slot_vel = predict(x0, v0, a0, j0, h)
    new_acc = terms[0:3] - slot_pos * terms[3:4]
    new_jerk = terms[4:7] - slot_vel * terms[3:4] - slot_pos * terms[7:8]
    new_vel = v0 + (a0 + new_acc) * h / 2 + (j0 - new_jerk) * h * h / 12
    new_pos = x0 + (v0 + new_vel) * h / 2 + (a0 - new_acc) * h * h / 12
    live = lax.broadcasted_iota(jnp.int32, new_acc.shape, 1) < count[0]
    stores = []
    for i, (value, held, target) in enumerate(
        ((new_acc, acc, acc_hbm), (new_jerk, jerk, jerk_hbm), (new_vel, vel, vel_hbm), (new_pos, pos, pos_hbm))
    ):
        held[...] = jnp.where(live, value, 0.0)
        stores.append(pltpu.make_async_copy(held, target, store_sem.at[i]))
        stores[-1].start()
    for store in stores:
        store.wait()


def body(lines, planes, pos, vel, acc, jerk, masses, levels, index, count):
    stars, slots, group = pos.shape[1], index.shape[1], 2 * planes
    hbm = pl.BlockSpec(memory_space=pl.ANY)
    tiles, blocks = group * slots // TILE, 2 * stars // TILE
    result = pl.pallas_call(
        functools.partial(kernel, lines, planes),
        out_shape=jax.ShapeDtypeStruct((24, slots), F32),
        in_specs=[hbm] * 7,
        out_specs=pl.BlockSpec(memory_space=pltpu.VMEM),
        scratch_shapes=[
            pltpu.VMEM((3, stars), F32),
            pltpu.VMEM((3, stars), F32),
            pltpu.VMEM((3, stars), F32),
            pltpu.VMEM((3, stars), F32),
            pltpu.VMEM((stars,), F32),
            pltpu.VMEM((stars,), jnp.int32),
            pltpu.VMEM((1, slots), jnp.int32),
            pltpu.VMEM((16, stars), F32),
            pltpu.VMEM((lines, 8, stars), F32),
            pltpu.VMEM((group, 8, LANES), F32),
            pltpu.VMEM((group, 8, LANES), F32),
            pltpu.VMEM((group // 2, 8, LANES), F32),
            pltpu.VMEM((lines * stars, KDIM), BF16),
            pltpu.VMEM((KDIM, 2 * group * slots), BF16),
            pltpu.VMEM((SOURCES, lines * stars), BF16),
            pltpu.VMEM((blocks, 2, 2 * TILE, TILE), BF16),
            pltpu.VMEM((tiles + 1, 2, SOURCES, TILE), F32),
            pltpu.SemaphoreType.DMA((7,)),
            pltpu.SemaphoreType.REGULAR((lines,)),
            pltpu.SemaphoreType.DMA((lines,)),
            pltpu.SemaphoreType.DMA((lines,)),
            pltpu.SemaphoreType.DMA((group,)),
            pltpu.SemaphoreType.DMA((group,)),
            pltpu.SemaphoreType.DMA((group,)),
            pltpu.SemaphoreType.DMA((group,)),
        ],
        compiler_params=pltpu.CompilerParams(collective_id=0, has_side_effects=True, vmem_limit_bytes=VMEM_LIMIT),
        name="forces",
    )(pos, vel, acc, jerk, masses, levels, index)
    three = jax.ShapeDtypeStruct((3, slots), F32)
    return pl.pallas_call(
        correct_kernel,
        out_shape=(three,) * 4,
        in_specs=[pl.BlockSpec(memory_space=pltpu.VMEM), pl.BlockSpec(memory_space=pltpu.SMEM)],
        out_specs=(hbm,) * 4,
        scratch_shapes=[pltpu.VMEM((3, slots), F32)] * 4 + [pltpu.SemaphoreType.DMA((4,))],
        compiler_params=pltpu.CompilerParams(vmem_limit_bytes=VMEM_LIMIT),
        name="correct",
    )(result, count)


def solution(mesh):
    lines, planes = mesh.shape["wide"] // 2, mesh.shape["sum"]
    both = ("wide", "sum")
    in_specs = (P(None, both),) * 4 + (P(both), P(both), P(both, None), P(both))
    return jax.shard_map(
        functools.partial(body, lines, planes), mesh=mesh, in_specs=in_specs,
        out_specs=(P(None, both),) * 4, check_vma=False,
    )
```

```python
import functools

import jax
import jax.numpy as jnp
from jax import lax
from jax.experimental import pallas as pl
from jax.experimental.pallas import tpu as pltpu
from jax.sharding import PartitionSpec as P

SOFT2 = 0.0025
STEP0 = 0.5
MESH = pl.DeviceIdType.MESH
F32 = jnp.float32
BF16 = jnp.bfloat16
LANES = 128
TILE = 256
KDIM = 128
ROWS = 16
SOURCES = 32
VMEM_LIMIT = 63 * 1024 * 1024


def step_of(levels):
    low = jnp.where(levels == 0, STEP0, STEP0 / 2)
    high = jnp.where(levels == 2, STEP0 / 4, STEP0 / 8)
    return jnp.where(levels < 2, low, high).astype(F32)


def predict(pos, vel, acc, jerk, step):
    pred_pos = pos + step * (vel + step * (acc / 2 + step * jerk / 6))
    pred_vel = vel + step * (acc + step * jerk / 2)
    return pred_pos, pred_vel


def pieces(value):
    first = value.astype(BF16).astype(F32)
    rest = value - first
    second = rest.astype(BF16).astype(F32)
    third = (rest - second).astype(BF16).astype(F32)
    return first, second, third


def split_state(tile):
    row = lax.broadcasted_iota(jnp.int32, tile.shape, 0)
    state = jnp.where(row < 6, tile, 0.0)
    grid = jnp.floor(state * 16.0 + 0.5) * 0.0625
    rest = state - grid
    near = rest.astype(BF16).astype(F32)
    far = (rest - near).astype(BF16).astype(F32)
    return grid, near, far


def own_terms(grid, near, far):
    small = near + far
    gp, gv, sp, sv = grid[0:3], grid[3:6], small[0:3], small[3:6]

    def total(value):
        return jnp.sum(value, axis=0, keepdims=True)

    square, square_rest = total(gp * gp), total(2.0 * gp * sp + sp * sp) + 0.5 * SOFT2
    cross, cross_rest = total(gp * gv), total(gp * sv + sp * gv + sp * sv)
    return list(pieces(square)[:2]), list(pieces(square_rest)), list(pieces(cross)[:2] + pieces(cross_rest))


def star_rows(tile):
    width = tile.shape[1]
    grid, near, far = split_state(tile)
    square, square_rest, cross = own_terms(grid, near, far)

    def ones(count):
        return jnp.ones((count, width), F32)

    first = jnp.concatenate([grid[0:3]] + square + [ones(2), jnp.zeros((1, width), F32)], 0)
    second = jnp.concatenate([grid[3:6]] + cross, 0)
    third = jnp.concatenate([ones(5)] + square_rest, 0)
    pad = jnp.zeros((KDIM - 88, width), F32)
    return jnp.concatenate([first, second, third] + [grid] * 2 + [near] * 3 + [far] * 3 + [pad], 0)


def slot_rows(tile):
    width = tile.shape[1]
    grid, near, far = split_state(tile)
    square, square_rest, cross = own_terms(grid, near, far)
    row = lax.broadcasted_iota(jnp.int32, tile.shape, 0)

    def ones(count):
        return jnp.ones((count, width), F32)

    def none(count):
        return jnp.zeros((count, width), F32)

    def for_square(part):
        return jnp.where(row < 3, -2.0 * part, 0.0)

    def for_cross(part):
        return jnp.concatenate([-part[3:6], -part[0:3], part[6:8]], 0)

    first = jnp.concatenate([-2.0 * grid[0:3], ones(2)] + square + [none(1)], 0)
    third = jnp.concatenate(square_rest + [none(2), ones(3)], 0)
    parts = (near, far) + (grid, near, far) * 2
    pad = none(KDIM - 88)
    in_square = jnp.concatenate([first, none(8), third] + [for_square(part) for part in parts] + [pad], 0)
    first = jnp.concatenate([-grid[3:6], none(5)], 0)
    second = jnp.concatenate([-grid[0:3], ones(5)], 0)
    third = jnp.concatenate(cross + [none(3)], 0)
    in_cross = jnp.concatenate([first, second, third] + [for_cross(part) for part in parts] + [pad], 0)
    return in_square, in_cross


def source_rows(tile):
    weight = tile[6:7]
    none = jnp.zeros_like(weight)
    sources = jnp.concatenate([weight * tile[0:3], weight, weight * tile[3:6], none], 0)
    return jnp.concatenate(list(pieces(sources)) + [jnp.zeros((SOURCES - 24, tile.shape[1]), F32)], 0)


def kernel(
    lines, planes, pos_hbm, vel_hbm, acc_hbm, jerk_hbm, mass_hbm, level_hbm, index_hbm, result,
    pos, vel, acc, jerk, mass, level, index, stage, fields, actives, arrived, partial,
    left, along, moments, both, high_low, sums,
    load_sem, ready, field_send, field_recv, active_send, active_recv, part_send, part_recv,
):
    group = 2 * planes
    stars, slots = pos.shape[1], index.shape[1]
    tiles = group * slots // TILE
    share = TILE // slots
    wide, s = lax.axis_index("wide"), lax.axis_index("sum")
    z, core = wide // 2, wide % 2
    me = core * planes + s

    def line_peer(k):
        other, bit = z, 1
        while bit < lines:
            other = other + (k // bit) % 2 * bit * (1 - 2 * ((z // bit) % 2))
            bit *= 2
        return other

    def plane_peer(k):
        return (me + 1 + k) % group

    def line_id(other):
        return (other * 2 + core, s)

    def plane_id(other):
        return (z * 2 + other // planes, other % planes)

    loads = [
        pltpu.make_async_copy(source, target, load_sem.at[i])
        for i, (source, target) in enumerate(
            zip((pos_hbm, vel_hbm, acc_hbm, jerk_hbm, mass_hbm, level_hbm, index_hbm), (pos, vel, acc, jerk, mass, level, index))
        )
    ]
    for load in loads:
        load.start()

    barrier = pltpu.get_barrier_semaphore()

    def greet_line(other, carry):
        pl.semaphore_signal(barrier, inc=1, device_id=line_id(other), device_id_type=MESH)
        return carry

    def greet_plane(k, carry):
        pl.semaphore_signal(barrier, inc=1, device_id=plane_id(plane_peer(k)), device_id_type=MESH)
        return carry

    lax.fori_loop(0, group - 1, greet_plane, 0, unroll=True)
    mate = line_peer(1)
    greet_line(mate, 0)
    lax.fori_loop(z // 2 * 2 + 2, lines, greet_line, 0)
    for load in loads:
        load.wait()

    step = step_of(level[...].reshape(1, stars))
    pred_pos, pred_vel = predict(pos[...], vel[...], acc[...], jerk[...], step)
    fields[z, 0:3, :] = pred_pos
    fields[z, 3:6, :] = pred_vel
    fields[z, 6:7, :] = mass[...].reshape(1, stars)
    fields[z, 7:8, :] = jnp.zeros_like(step)

    stage[0:3, :] = pos[...]
    stage[3:6, :] = vel[...]
    stage[6:9, :] = acc[...]
    stage[9:12, :] = jerk[...]
    stage[12:13, :] = step
    stage[13:16, :] = jnp.zeros((3, stars), F32)
    chosen = lax.broadcasted_iota(jnp.int32, (stars, slots), 0) == index[...]
    chosen = chosen.astype(F32).astype(BF16)
    picked = [jnp.dot(part.astype(BF16), chosen, preferred_element_type=F32) for part in pieces(stage[...])]
    picked = (picked[0] + picked[1]) + picked[2]
    result[8:24, :] = picked
    slot_pos, slot_vel = predict(picked[0:3], picked[3:6], picked[6:9], picked[9:12], picked[12:13])
    actives[me] = jnp.zeros((8, LANES), F32)
    actives[me, 0:3, 0:slots] = slot_pos
    actives[me, 3:6, 0:slots] = slot_vel

    pl.semaphore_wait(barrier, group + z // 2 * 2)

    def line_copy(block, other):
        return pltpu.make_async_remote_copy(
            src_ref=fields.at[block], dst_ref=fields.at[block],
            send_sem=field_send.at[other], recv_sem=field_recv.at[block],
            device_id=line_id(other), device_id_type=MESH,
        )

    def plane_copy(block, other, k):
        return pltpu.make_async_remote_copy(
            src_ref=actives.at[block], dst_ref=actives.at[block],
            send_sem=active_send.at[k], recv_sem=active_recv.at[block],
            device_id=plane_id(other), device_id_type=MESH,
        )

    def part_copy(pair, slot, other):
        return pltpu.make_async_remote_copy(
            src_ref=partial.at[pair], dst_ref=arrived.at[slot],
            send_sem=part_send.at[other], recv_sem=part_recv.at[slot],
            device_id=plane_id(other), device_id_type=MESH,
        )

    def send_lower(other, carry):
        pl.semaphore_signal(ready.at[z], inc=1, device_id=line_id(other), device_id_type=MESH)
        line_copy(z, other).start()
        return carry

    def send_higher(other, carry):
        pl.semaphore_wait(ready.at[other], 1)
        line_copy(z, other).start()
        return carry

    def send_plane(k, carry):
        plane_copy(me, plane_peer(k), k).start()
        return carry

    lax.fori_loop(0, group - 1, send_plane, 0, unroll=True)
    line_copy(z, mate).start()
    lax.fori_loop(0, z // 2 * 2, send_lower, 0)

    def take_stars(k, block):
        tile = fields[block]
        at = pl.ds(pl.multiple_of(k * stars, LANES), stars)
        left[at, :] = star_rows(tile).T.astype(BF16)
        moments[:, at] = source_rows(tile).astype(BF16)

    take_stars(0, z)

    def get_plane(k, carry):
        plane_copy(plane_peer(k), plane_peer(k), k).wait_recv()
        return carry

    lax.fori_loop(0, group - 1, get_plane, 0, unroll=True)

    lane = lax.broadcasted_iota(jnp.int32, (8, LANES), 1)

    def take_slots(pair, carry):
        tile = jnp.where(lane < slots, actives[2 * pair], pltpu.roll(actives[2 * pair + 1], slots, 1))
        start = pair * LANES // TILE * 2 * TILE + pair * LANES % TILE
        for offset, value in zip((0, TILE), slot_rows(tile)):
            along[:, pl.ds(pl.multiple_of(start + offset, LANES), LANES)] = value.astype(BF16)
        return carry

    lax.fori_loop(0, group // 2, take_slots, 0, unroll=True)

    line_copy(mate, mate).wait_recv()
    take_stars(1, mate)

    blocks = 2 * stars // TILE
    rounds = lines // 2

    def stars_of(n, b):
        return pl.ds(pl.multiple_of((n * blocks + b) * TILE, TILE), TILE)

    def relate(n, i, side):
        rows = pl.ds(pl.multiple_of(n * blocks * TILE, TILE), blocks * TILE)
        cols = pl.ds(pl.multiple_of(i * 2 * TILE, 2 * TILE), 2 * TILE)
        both[side] = jnp.dot(left[rows, :], along[:, cols], preferred_element_type=F32)

    def weigh(b, side, beside):
        for sub in range(0, TILE, ROWS):
            at = slice(b * TILE + sub, b * TILE + sub + ROWS)
            inverse = lax.rsqrt(both[side, at, 0:TILE])
            inverse2 = inverse * inverse
            w = inverse2 * inverse
            sw = (w * inverse2) * both[side, at, TILE:2 * TILE]
            for kind, value in enumerate((w, sw)):
                high = value.astype(BF16)
                high_low[b, kind, sub:sub + ROWS, :] = high
                high_low[b, kind, TILE + sub:TILE + sub + ROWS, :] = (value - high.astype(F32)).astype(BF16)
            if sub // ROWS in beside:
                beside[sub // ROWS]()

    def gain(n, i, b, kind, part):
        piece = high_low[b, kind, part * TILE:(part + 1) * TILE, :]
        sums[i, kind] += jnp.dot(moments[:, stars_of(n, b)], piece, preferred_element_type=F32)

    def finish(i):
        by_w, by_s = sums[i, 0], sums[i, 1]
        by_w = by_w[0:8] + by_w[8:16] + by_w[16:24]
        by_s = by_s[0:8] + by_s[8:16] + by_s[16:24]
        row = lax.broadcasted_iota(jnp.int32, by_s.shape, 0)
        terms = by_w + pltpu.roll(jnp.where(row < 4, -3.0 * by_s, 0.0), 4, 0)
        for pair in range(share // 2):
            place = i * (share // 2) + pair
            partial[place] = terms[:, pair * LANES:(pair + 1) * LANES]
            for half in range(2):
                owner = 2 * place + half

                @pl.when(owner != me)
                def _():
                    part_copy(place, me, owner).start()

    def tile_of(j):
        return (me // share + 1 + j) % tiles

    sums[...] = jnp.zeros_like(sums)

    def pair_round(n, final):
        relate(n, tile_of(0), 0)

        def two_tiles(pair, carry):
            for side in range(2):
                j = 2 * pair + side
                i = tile_of(j)
                before = tile_of(j + tiles - 1) if side else jnp.where(j > 0, tile_of(j + tiles - 1), tiles)
                relate(n, tile_of(j + 1), 1 - side)
                for b in range(blocks):
                    done = (before, blocks - 1) if b == 0 else (i, b - 1)
                    beside = {}
                    for kind in range(2):
                        for part in range(2):
                            beside[4 * (2 * kind + part) + 1] = functools.partial(gain, n, *done, kind, part)
                    weigh(b, side, beside)
                if final:

                    @pl.when(j > 0)
                    def _():
                        finish(before)

            if not final:

                @pl.when((n == 0) & (pair == 0) & (z // 2 % 2 == 0))
                def _():
                    lax.fori_loop(z // 4 * 4 + 2, z // 4 * 4 + 4, send_higher, 0)

            return carry

        lax.fori_loop(0, tiles // 2, two_tiles, 0)
        for kind in range(2):
            for part in range(2):
                gain(n, tile_of(tiles - 1), blocks - 1, kind, part)
        if final:
            finish(tile_of(tiles - 1))

    def early_round(n, carry):
        pair_round(n, False)

        @pl.when(n == 0)
        def _():
            lax.fori_loop(z // 4 * 4 + 4, lines, send_higher, 0)

        for k in (2 * n + 2, 2 * n + 3):
            block = line_peer(k)
            line_copy(block, block).wait_recv()
            take_stars(k, block)
        return carry

    lax.fori_loop(0, rounds - 1, early_round, 0)
    pair_round(rounds - 1, True)

    arrived[me] = partial[me // 2]

    def get_part(k, carry):
        other = plane_peer(k)
        part_copy(other // 2, other, other).wait_recv()
        return carry

    lax.fori_loop(0, group - 1, get_part, 0, unroll=True)
    terms = jnp.sum(arrived[...], axis=0)
    terms = jnp.where(me % 2 == 0, terms, pltpu.roll(terms, slots, 1))
    result[0:8, :] = terms[:, 0:slots]

    def end_line(k, carry):
        line_copy(z, line_peer(k + 1)).wait_send()
        return carry

    def end_plane(k, carry):
        other = plane_peer(k)
        plane_copy(me, other, k).wait_send()
        part_copy(other // 2, me, other).wait_send()
        return carry

    lax.fori_loop(0, lines - 1, end_line, 0, unroll=True)
    lax.fori_loop(0, group - 1, end_plane, 0, unroll=True)


def correct_kernel(result, count, pos_hbm, vel_hbm, acc_hbm, jerk_hbm, pos, vel, acc, jerk, store_sem):
    terms, picked = result[0:8, :], result[8:24, :]
    x0, v0, a0, j0, h = picked[0:3], picked[3:6], picked[6:9], picked[9:12], picked[12:13]
    slot_pos, slot_vel = predict(x0, v0, a0, j0, h)
    new_acc = terms[0:3] - slot_pos * terms[3:4]
    new_jerk = terms[4:7] - slot_vel * terms[3:4] - slot_pos * terms[7:8]
    new_vel = v0 + (a0 + new_acc) * h / 2 + (j0 - new_jerk) * h * h / 12
    new_pos = x0 + (v0 + new_vel) * h / 2 + (a0 - new_acc) * h * h / 12
    live = lax.broadcasted_iota(jnp.int32, new_acc.shape, 1) < count[0]
    stores = []
    for i, (value, held, target) in enumerate(
        ((new_acc, acc, acc_hbm), (new_jerk, jerk, jerk_hbm), (new_vel, vel, vel_hbm), (new_pos, pos, pos_hbm))
    ):
        held[...] = jnp.where(live, value, 0.0)
        stores.append(pltpu.make_async_copy(held, target, store_sem.at[i]))
        stores[-1].start()
    for store in stores:
        store.wait()


def body(lines, planes, pos, vel, acc, jerk, masses, levels, index, count):
    stars, slots, group = pos.shape[1], index.shape[1], 2 * planes
    hbm = pl.BlockSpec(memory_space=pl.ANY)
    tiles, blocks = group * slots // TILE, 2 * stars // TILE
    result = pl.pallas_call(
        functools.partial(kernel, lines, planes),
        out_shape=jax.ShapeDtypeStruct((24, slots), F32),
        in_specs=[hbm] * 7,
        out_specs=pl.BlockSpec(memory_space=pltpu.VMEM),
        scratch_shapes=[
            pltpu.VMEM((3, stars), F32),
            pltpu.VMEM((3, stars), F32),
            pltpu.VMEM((3, stars), F32),
            pltpu.VMEM((3, stars), F32),
            pltpu.VMEM((stars,), F32),
            pltpu.VMEM((stars,), jnp.int32),
            pltpu.VMEM((1, slots), jnp.int32),
            pltpu.VMEM((16, stars), F32),
            pltpu.VMEM((lines, 8, stars), F32),
            pltpu.VMEM((group, 8, LANES), F32),
            pltpu.VMEM((group, 8, LANES), F32),
            pltpu.VMEM((group // 2, 8, LANES), F32),
            pltpu.VMEM((lines * stars, KDIM), BF16),
            pltpu.VMEM((KDIM, 2 * group * slots), BF16),
            pltpu.VMEM((SOURCES, lines * stars), BF16),
            pltpu.VMEM((2, 2 * stars, 2 * TILE), F32),
            pltpu.VMEM((blocks, 2, 2 * TILE, TILE), BF16),
            pltpu.VMEM((tiles + 1, 2, SOURCES, TILE), F32),
            pltpu.SemaphoreType.DMA((7,)),
            pltpu.SemaphoreType.REGULAR((lines,)),
            pltpu.SemaphoreType.DMA((lines,)),
            pltpu.SemaphoreType.DMA((lines,)),
            pltpu.SemaphoreType.DMA((group,)),
            pltpu.SemaphoreType.DMA((group,)),
            pltpu.SemaphoreType.DMA((group,)),
            pltpu.SemaphoreType.DMA((group,)),
        ],
        compiler_params=pltpu.CompilerParams(collective_id=0, has_side_effects=True, vmem_limit_bytes=VMEM_LIMIT),
        name="forces",
    )(pos, vel, acc, jerk, masses, levels, index)
    three = jax.ShapeDtypeStruct((3, slots), F32)
    return pl.pallas_call(
        correct_kernel,
        out_shape=(three,) * 4,
        in_specs=[pl.BlockSpec(memory_space=pltpu.VMEM), pl.BlockSpec(memory_space=pltpu.SMEM)],
        out_specs=(hbm,) * 4,
        scratch_shapes=[pltpu.VMEM((3, slots), F32)] * 4 + [pltpu.SemaphoreType.DMA((4,))],
        compiler_params=pltpu.CompilerParams(vmem_limit_bytes=VMEM_LIMIT),
        name="correct",
    )(result, count)


def solution(mesh):
    lines, planes = mesh.shape["wide"] // 2, mesh.shape["sum"]
    both = ("wide", "sum")
    in_specs = (P(None, both),) * 4 + (P(both), P(both), P(both, None), P(both))
    return jax.shard_map(
        functools.partial(body, lines, planes), mesh=mesh, in_specs=in_specs,
        out_specs=(P(None, both),) * 4, check_vma=False,
    )
```

```python
import functools

import jax
import jax.numpy as jnp
from jax import lax
from jax.experimental import pallas as pl
from jax.experimental.pallas import tpu as pltpu
from jax.sharding import PartitionSpec as P

SOFT2 = 0.0025
STEP0 = 0.5
MESH = pl.DeviceIdType.MESH
F32 = jnp.float32
BF16 = jnp.bfloat16
LANES = 128
TILE = 256
QUARTER = 64
KDIM = 128
ROWS = 16
UNROLL = 1
SOURCES = 32
VMEM_LIMIT = 63 * 1024 * 1024


def step_of(levels):
    low = jnp.where(levels == 0, STEP0, STEP0 / 2)
    high = jnp.where(levels == 2, STEP0 / 4, STEP0 / 8)
    return jnp.where(levels < 2, low, high).astype(F32)


def predict(pos, vel, acc, jerk, step):
    pred_pos = pos + step * (vel + step * (acc / 2 + step * jerk / 6))
    pred_vel = vel + step * (acc + step * jerk / 2)
    return pred_pos, pred_vel


def pieces(value):
    first = value.astype(BF16).astype(F32)
    rest = value - first
    second = rest.astype(BF16).astype(F32)
    third = (rest - second).astype(BF16).astype(F32)
    return first, second, third


def split_state(tile):
    row = lax.broadcasted_iota(jnp.int32, tile.shape, 0)
    state = jnp.where(row < 6, tile, 0.0)
    grid = jnp.floor(state * 16.0 + 0.5) * 0.0625
    rest = state - grid
    near = rest.astype(BF16).astype(F32)
    far = (rest - near).astype(BF16).astype(F32)
    return grid, near, far


def own_terms(grid, near, far):
    small = near + far
    gp, gv, sp, sv = grid[0:3], grid[3:6], small[0:3], small[3:6]

    def total(value):
        return jnp.sum(value, axis=0, keepdims=True)

    square, square_rest = total(gp * gp), total(2.0 * gp * sp + sp * sp) + 0.5 * SOFT2
    cross, cross_rest = total(gp * gv), total(gp * sv + sp * gv + sp * sv)
    return list(pieces(square)[:2]), list(pieces(square_rest)), list(pieces(cross)[:2] + pieces(cross_rest))


def star_rows(tile):
    width = tile.shape[1]
    grid, near, far = split_state(tile)
    square, square_rest, cross = own_terms(grid, near, far)

    def ones(count):
        return jnp.ones((count, width), F32)

    first = jnp.concatenate([grid[0:3]] + square + [ones(2), jnp.zeros((1, width), F32)], 0)
    second = jnp.concatenate([grid[3:6]] + cross, 0)
    third = jnp.concatenate([ones(5)] + square_rest, 0)
    pad = jnp.zeros((KDIM - 88, width), F32)
    return jnp.concatenate([first, second, third] + [grid] * 2 + [near] * 3 + [far] * 3 + [pad], 0)


def slot_rows(tile):
    width = tile.shape[1]
    grid, near, far = split_state(tile)
    square, square_rest, cross = own_terms(grid, near, far)
    row = lax.broadcasted_iota(jnp.int32, tile.shape, 0)

    def ones(count):
        return jnp.ones((count, width), F32)

    def none(count):
        return jnp.zeros((count, width), F32)

    def for_square(part):
        return jnp.where(row < 3, -2.0 * part, 0.0)

    def for_cross(part):
        return jnp.concatenate([-part[3:6], -part[0:3], part[6:8]], 0)

    first = jnp.concatenate([-2.0 * grid[0:3], ones(2)] + square + [none(1)], 0)
    third = jnp.concatenate(square_rest + [none(2), ones(3)], 0)
    parts = (near, far) + (grid, near, far) * 2
    pad = none(KDIM - 88)
    in_square = jnp.concatenate([first, none(8), third] + [for_square(part) for part in parts] + [pad], 0)
    first = jnp.concatenate([-grid[3:6], none(5)], 0)
    second = jnp.concatenate([-grid[0:3], ones(5)], 0)
    third = jnp.concatenate(cross + [none(3)], 0)
    in_cross = jnp.concatenate([first, second, third] + [for_cross(part) for part in parts] + [pad], 0)
    return in_square, in_cross


def source_rows(tile):
    weight = tile[6:7]
    none = jnp.zeros_like(weight)
    sources = jnp.concatenate([weight * tile[0:3], weight, weight * tile[3:6], none], 0)
    return jnp.concatenate(list(pieces(sources)) + [jnp.zeros((SOURCES - 24, tile.shape[1]), F32)], 0)


def kernel(
    lines, planes, pos_hbm, vel_hbm, acc_hbm, jerk_hbm, mass_hbm, level_hbm, index_hbm, result,
    pos, vel, acc, jerk, mass, level, index, stage, fields, actives, arrived, partial,
    left, along, moments, both, high_low, sums,
    load_sem, ready, field_send, field_recv, active_send, active_recv, part_send, part_recv,
):
    group = 2 * planes
    stars, slots = pos.shape[1], index.shape[1]
    tiles = group * slots // TILE
    share = TILE // slots
    wide, s = lax.axis_index("wide"), lax.axis_index("sum")
    z, core = wide // 2, wide % 2
    me = core * planes + s

    def line_peer(k):
        other, bit = z, 1
        while bit < lines:
            other = other + (k // bit) % 2 * bit * (1 - 2 * ((z // bit) % 2))
            bit *= 2
        return other

    def plane_peer(k):
        return (me + 1 + k) % group

    def line_id(other):
        return (other * 2 + core, s)

    def plane_id(other):
        return (z * 2 + other // planes, other % planes)

    loads = [
        pltpu.make_async_copy(source, target, load_sem.at[i])
        for i, (source, target) in enumerate(
            zip((pos_hbm, vel_hbm, acc_hbm, jerk_hbm, mass_hbm, level_hbm, index_hbm), (pos, vel, acc, jerk, mass, level, index))
        )
    ]
    for load in loads:
        load.start()

    barrier = pltpu.get_barrier_semaphore()

    def greet_line(other, carry):
        pl.semaphore_signal(barrier, inc=1, device_id=line_id(other), device_id_type=MESH)
        return carry

    def greet_plane(k, carry):
        pl.semaphore_signal(barrier, inc=1, device_id=plane_id(plane_peer(k)), device_id_type=MESH)
        return carry

    lax.fori_loop(0, group - 1, greet_plane, 0, unroll=True)
    mate = line_peer(1)
    greet_line(mate, 0)
    lax.fori_loop(z // 2 * 2 + 2, lines, greet_line, 0)
    for load in loads:
        load.wait()

    step = step_of(level[...].reshape(1, stars))
    pred_pos, pred_vel = predict(pos[...], vel[...], acc[...], jerk[...], step)
    fields[z, 0:3, :] = pred_pos
    fields[z, 3:6, :] = pred_vel
    fields[z, 6:7, :] = mass[...].reshape(1, stars)
    fields[z, 7:8, :] = jnp.zeros_like(step)

    stage[0:3, :] = pos[...]
    stage[3:6, :] = vel[...]
    stage[6:9, :] = acc[...]
    stage[9:12, :] = jerk[...]
    stage[12:13, :] = step
    stage[13:16, :] = jnp.zeros((3, stars), F32)
    chosen = lax.broadcasted_iota(jnp.int32, (stars, slots), 0) == index[...]
    chosen = chosen.astype(F32).astype(BF16)
    picked = [jnp.dot(part.astype(BF16), chosen, preferred_element_type=F32) for part in pieces(stage[...])]
    picked = (picked[0] + picked[1]) + picked[2]
    result[8:24, :] = picked
    slot_pos, slot_vel = predict(picked[0:3], picked[3:6], picked[6:9], picked[9:12], picked[12:13])
    actives[me] = jnp.zeros((8, LANES), F32)
    actives[me, 0:3, 0:slots] = slot_pos
    actives[me, 3:6, 0:slots] = slot_vel

    pl.semaphore_wait(barrier, group + z // 2 * 2)

    def line_copy(block, other):
        return pltpu.make_async_remote_copy(
            src_ref=fields.at[block], dst_ref=fields.at[block],
            send_sem=field_send.at[other], recv_sem=field_recv.at[block],
            device_id=line_id(other), device_id_type=MESH,
        )

    def plane_copy(block, other, k):
        return pltpu.make_async_remote_copy(
            src_ref=actives.at[block], dst_ref=actives.at[block],
            send_sem=active_send.at[k], recv_sem=active_recv.at[block],
            device_id=plane_id(other), device_id_type=MESH,
        )

    def part_copy(pair, slot, other):
        return pltpu.make_async_remote_copy(
            src_ref=partial.at[pair], dst_ref=arrived.at[slot],
            send_sem=part_send.at[other], recv_sem=part_recv.at[slot],
            device_id=plane_id(other), device_id_type=MESH,
        )

    def send_lower(other, carry):
        pl.semaphore_signal(ready.at[z], inc=1, device_id=line_id(other), device_id_type=MESH)
        line_copy(z, other).start()
        return carry

    def send_higher(other, carry):
        pl.semaphore_wait(ready.at[other], 1)
        line_copy(z, other).start()
        return carry

    def send_plane(k, carry):
        plane_copy(me, plane_peer(k), k).start()
        return carry

    lax.fori_loop(0, group - 1, send_plane, 0, unroll=True)
    line_copy(z, mate).start()
    lax.fori_loop(0, z // 2 * 2, send_lower, 0)

    def take_stars(k, block):
        tile = fields[block]
        at = pl.ds(pl.multiple_of(k * stars, LANES), stars)
        left[at, :] = star_rows(tile).T.astype(BF16)
        moments[:, at] = source_rows(tile).astype(BF16)

    take_stars(0, z)

    def get_plane(k, carry):
        plane_copy(plane_peer(k), plane_peer(k), k).wait_recv()
        return carry

    lax.fori_loop(0, group - 1, get_plane, 0, unroll=True)

    lane = lax.broadcasted_iota(jnp.int32, (8, LANES), 1)

    def take_slots(pair, carry):
        tile = jnp.where(lane < slots, actives[2 * pair], pltpu.roll(actives[2 * pair + 1], slots, 1))
        start = pair * LANES // TILE * 2 * TILE + pair * LANES % TILE
        for offset, value in zip((0, TILE), slot_rows(tile)):
            along[:, pl.ds(pl.multiple_of(start + offset, LANES), LANES)] = value.astype(BF16)
        return carry

    lax.fori_loop(0, group // 2, take_slots, 0, unroll=True)

    line_copy(mate, mate).wait_recv()
    take_stars(1, mate)

    blocks = 2 * stars // TILE
    rounds = lines // 2

    def stars_of(n, b):
        return pl.ds(pl.multiple_of((n * blocks + b) * TILE, TILE), TILE)

    def relate(n, i, b, part):
        rows = pl.ds(pl.multiple_of((n * blocks + b) * TILE + part * QUARTER, QUARTER), QUARTER)
        cols = pl.ds(pl.multiple_of(i * 2 * TILE, 2 * TILE), 2 * TILE)
        return jnp.dot(left[rows, :], along[:, cols], preferred_element_type=F32)

    def keep(b, part, value):
        both[b, part * QUARTER:(part + 1) * QUARTER, :] = value

    def weigh(b, beside):
        for sub in range(0, TILE, ROWS):
            inverse = lax.rsqrt(both[b, sub:sub + ROWS, 0:TILE])
            inverse2 = inverse * inverse
            w = inverse2 * inverse
            sw = (w * inverse2) * both[b, sub:sub + ROWS, TILE:2 * TILE]
            for kind, value in enumerate((w, sw)):
                high = value.astype(BF16)
                high_low[b, kind, sub:sub + ROWS, :] = high
                high_low[b, kind, TILE + sub:TILE + sub + ROWS, :] = (value - high.astype(F32)).astype(BF16)
            beside(sub // ROWS)

    def gain(n, b, kind, part):
        piece = high_low[b, kind, part * TILE:(part + 1) * TILE, :]
        return jnp.dot(moments[:, stars_of(n, b)], piece, preferred_element_type=F32)

    def finish(i):
        by_w, by_s = sums[i, 0], sums[i, 1]
        by_w = by_w[0:8] + by_w[8:16] + by_w[16:24]
        by_s = by_s[0:8] + by_s[8:16] + by_s[16:24]
        row = lax.broadcasted_iota(jnp.int32, by_s.shape, 0)
        terms = by_w + pltpu.roll(jnp.where(row < 4, -3.0 * by_s, 0.0), 4, 0)
        for pair in range(share // 2):
            place = i * (share // 2) + pair
            partial[place] = terms[:, pair * LANES:(pair + 1) * LANES]
            for half in range(2):
                owner = 2 * place + half

                @pl.when(owner != me)
                def _():
                    part_copy(place, me, owner).start()

    def tile_of(j):
        return (me // share + 1 + j) % tiles

    sums[...] = jnp.zeros_like(sums)

    steps = TILE // ROWS
    pieces_of = TILE // QUARTER

    def locate(k):
        return k // tiles, tile_of(k % tiles)

    for part in range(pieces_of):
        keep(0, part, relate(0, tile_of(0), 0, part))

    def slot_tile(k, carry):
        n, i = locate(k)
        j = k % tiles
        last_n, last_i = locate(jnp.where(k > 0, k - 1, 0))
        last_i = jnp.where(k > 0, last_i, tiles)
        next_n, next_i = locate(jnp.where(k < rounds * tiles - 1, k + 1, k))
        for b in range(blocks):
            done_n, done_i, done_b = (last_n, last_i, blocks - 1) if b == 0 else (n, i, b - 1)
            soon_n, soon_i, soon_b = (n, i, b + 1) if b < blocks - 1 else (next_n, next_i, 0)
            related, gained = {}, {}

            def beside(step):
                part, phase = step // (steps // pieces_of), step % (steps // pieces_of)
                if phase == 0:
                    related[part] = relate(soon_n, soon_i, soon_b, part)
                if phase == 1:
                    gained[part] = gain(done_n, done_b, part // 2, part % 2)
                if phase == 2:
                    keep(soon_b, part, related[part])
                if phase == 3:
                    sums[done_i, part // 2] += gained[part]

            weigh(b, beside)

        @pl.when((n == rounds - 1) & (j > 0))
        def _():
            finish(last_i)

        @pl.when((n == 0) & (j == 1) & (z // 2 % 2 == 0) & (rounds > 1))
        def _():
            lax.fori_loop(z // 4 * 4 + 2, z // 4 * 4 + 4, send_higher, 0)

        @pl.when((n < rounds - 1) & (j == tiles - 2))
        def _():
            @pl.when(n == 0)
            def _():
                lax.fori_loop(z // 4 * 4 + 4, lines, send_higher, 0)

            for later in (2 * n + 2, 2 * n + 3):
                block = line_peer(later)
                line_copy(block, block).wait_recv()
                take_stars(later, block)

        return carry

    lax.fori_loop(0, rounds * tiles, slot_tile, 0, unroll=UNROLL)
    for part in range(4):
        sums[tile_of(tiles - 1), part // 2] += gain(rounds - 1, blocks - 1, part // 2, part % 2)
    finish(tile_of(tiles - 1))

    arrived[me] = partial[me // 2]

    def get_part(k, carry):
        other = plane_peer(k)
        part_copy(other // 2, other, other).wait_recv()
        return carry

    lax.fori_loop(0, group - 1, get_part, 0, unroll=True)
    terms = jnp.sum(arrived[...], axis=0)
    terms = jnp.where(me % 2 == 0, terms, pltpu.roll(terms, slots, 1))
    result[0:8, :] = terms[:, 0:slots]

    def end_line(k, carry):
        line_copy(z, line_peer(k + 1)).wait_send()
        return carry

    def end_plane(k, carry):
        other = plane_peer(k)
        plane_copy(me, other, k).wait_send()
        part_copy(other // 2, me, other).wait_send()
        return carry

    lax.fori_loop(0, lines - 1, end_line, 0, unroll=True)
    lax.fori_loop(0, group - 1, end_plane, 0, unroll=True)


def correct_kernel(result, count, pos_hbm, vel_hbm, acc_hbm, jerk_hbm, pos, vel, acc, jerk, store_sem):
    terms, picked = result[0:8, :], result[8:24, :]
    x0, v0, a0, j0, h = picked[0:3], picked[3:6], picked[6:9], picked[9:12], picked[12:13]
    slot_pos, slot_vel = predict(x0, v0, a0, j0, h)
    new_acc = terms[0:3] - slot_pos * terms[3:4]
    new_jerk = terms[4:7] - slot_vel * terms[3:4] - slot_pos * terms[7:8]
    new_vel = v0 + (a0 + new_acc) * h / 2 + (j0 - new_jerk) * h * h / 12
    new_pos = x0 + (v0 + new_vel) * h / 2 + (a0 - new_acc) * h * h / 12
    live = lax.broadcasted_iota(jnp.int32, new_acc.shape, 1) < count[0]
    stores = []
    for i, (value, held, target) in enumerate(
        ((new_acc, acc, acc_hbm), (new_jerk, jerk, jerk_hbm), (new_vel, vel, vel_hbm), (new_pos, pos, pos_hbm))
    ):
        held[...] = jnp.where(live, value, 0.0)
        stores.append(pltpu.make_async_copy(held, target, store_sem.at[i]))
        stores[-1].start()
    for store in stores:
        store.wait()


def body(lines, planes, pos, vel, acc, jerk, masses, levels, index, count):
    stars, slots, group = pos.shape[1], index.shape[1], 2 * planes
    hbm = pl.BlockSpec(memory_space=pl.ANY)
    tiles, blocks = group * slots // TILE, 2 * stars // TILE
    result = pl.pallas_call(
        functools.partial(kernel, lines, planes),
        out_shape=jax.ShapeDtypeStruct((24, slots), F32),
        in_specs=[hbm] * 7,
        out_specs=pl.BlockSpec(memory_space=pltpu.VMEM),
        scratch_shapes=[
            pltpu.VMEM((3, stars), F32),
            pltpu.VMEM((3, stars), F32),
            pltpu.VMEM((3, stars), F32),
            pltpu.VMEM((3, stars), F32),
            pltpu.VMEM((stars,), F32),
            pltpu.VMEM((stars,), jnp.int32),
            pltpu.VMEM((1, slots), jnp.int32),
            pltpu.VMEM((16, stars), F32),
            pltpu.VMEM((lines, 8, stars), F32),
            pltpu.VMEM((group, 8, LANES), F32),
            pltpu.VMEM((group, 8, LANES), F32),
            pltpu.VMEM((group // 2, 8, LANES), F32),
            pltpu.VMEM((lines * stars, KDIM), BF16),
            pltpu.VMEM((KDIM, 2 * group * slots), BF16),
            pltpu.VMEM((SOURCES, lines * stars), BF16),
            pltpu.VMEM((blocks, TILE, 2 * TILE), F32),
            pltpu.VMEM((blocks, 2, 2 * TILE, TILE), BF16),
            pltpu.VMEM((tiles + 1, 2, SOURCES, TILE), F32),
            pltpu.SemaphoreType.DMA((7,)),
            pltpu.SemaphoreType.REGULAR((lines,)),
            pltpu.SemaphoreType.DMA((lines,)),
            pltpu.SemaphoreType.DMA((lines,)),
            pltpu.SemaphoreType.DMA((group,)),
            pltpu.SemaphoreType.DMA((group,)),
            pltpu.SemaphoreType.DMA((group,)),
            pltpu.SemaphoreType.DMA((group,)),
        ],
        compiler_params=pltpu.CompilerParams(collective_id=0, has_side_effects=True, vmem_limit_bytes=VMEM_LIMIT),
        name="forces",
    )(pos, vel, acc, jerk, masses, levels, index)
    three = jax.ShapeDtypeStruct((3, slots), F32)
    return pl.pallas_call(
        correct_kernel,
        out_shape=(three,) * 4,
        in_specs=[pl.BlockSpec(memory_space=pltpu.VMEM), pl.BlockSpec(memory_space=pltpu.SMEM)],
        out_specs=(hbm,) * 4,
        scratch_shapes=[pltpu.VMEM((3, slots), F32)] * 4 + [pltpu.SemaphoreType.DMA((4,))],
        compiler_params=pltpu.CompilerParams(vmem_limit_bytes=VMEM_LIMIT),
        name="correct",
    )(result, count)


def solution(mesh):
    lines, planes = mesh.shape["wide"] // 2, mesh.shape["sum"]
    both = ("wide", "sum")
    in_specs = (P(None, both),) * 4 + (P(both), P(both), P(both, None), P(both))
    return jax.shard_map(
        functools.partial(body, lines, planes), mesh=mesh, in_specs=in_specs,
        out_specs=(P(None, both),) * 4, check_vma=False,
    )
```

```python
import functools

import jax
import jax.numpy as jnp
from jax import lax
from jax.experimental import pallas as pl
from jax.experimental.pallas import tpu as pltpu
from jax.sharding import PartitionSpec as P

SOFT2 = 0.0025
STEP0 = 0.5
MESH = pl.DeviceIdType.MESH
F32 = jnp.float32
BF16 = jnp.bfloat16
LANES = 128
TILE = 256
PART = 128
KDIM = 128
ROWS = 16
SOURCES = 32
VMEM_LIMIT = 63 * 1024 * 1024


def step_of(levels):
    low = jnp.where(levels == 0, STEP0, STEP0 / 2)
    high = jnp.where(levels == 2, STEP0 / 4, STEP0 / 8)
    return jnp.where(levels < 2, low, high).astype(F32)


def predict(pos, vel, acc, jerk, step):
    pred_pos = pos + step * (vel + step * (acc / 2 + step * jerk / 6))
    pred_vel = vel + step * (acc + step * jerk / 2)
    return pred_pos, pred_vel


def pieces(value):
    first = value.astype(BF16).astype(F32)
    rest = value - first
    second = rest.astype(BF16).astype(F32)
    third = (rest - second).astype(BF16).astype(F32)
    return first, second, third


def split_state(tile):
    row = lax.broadcasted_iota(jnp.int32, tile.shape, 0)
    state = jnp.where(row < 6, tile, 0.0)
    grid = jnp.floor(state * 16.0 + 0.5) * 0.0625
    rest = state - grid
    near = rest.astype(BF16).astype(F32)
    far = (rest - near).astype(BF16).astype(F32)
    return grid, near, far


def own_terms(grid, near, far):
    small = near + far
    gp, gv, sp, sv = grid[0:3], grid[3:6], small[0:3], small[3:6]

    def total(value):
        return jnp.sum(value, axis=0, keepdims=True)

    square, square_rest = total(gp * gp), total(2.0 * gp * sp + sp * sp) + 0.5 * SOFT2
    cross, cross_rest = total(gp * gv), total(gp * sv + sp * gv + sp * sv)
    return list(pieces(square)[:2]), list(pieces(square_rest)), list(pieces(cross)[:2] + pieces(cross_rest))


def star_rows(tile):
    width = tile.shape[1]
    grid, near, far = split_state(tile)
    square, square_rest, cross = own_terms(grid, near, far)

    def ones(count):
        return jnp.ones((count, width), F32)

    first = jnp.concatenate([grid[0:3]] + square + [ones(2), jnp.zeros((1, width), F32)], 0)
    second = jnp.concatenate([grid[3:6]] + cross, 0)
    third = jnp.concatenate([ones(5)] + square_rest, 0)
    pad = jnp.zeros((KDIM - 88, width), F32)
    return jnp.concatenate([first, second, third] + [grid] * 2 + [near] * 3 + [far] * 3 + [pad], 0)


def slot_rows(tile):
    width = tile.shape[1]
    grid, near, far = split_state(tile)
    square, square_rest, cross = own_terms(grid, near, far)
    row = lax.broadcasted_iota(jnp.int32, tile.shape, 0)

    def ones(count):
        return jnp.ones((count, width), F32)

    def none(count):
        return jnp.zeros((count, width), F32)

    def for_square(part):
        return jnp.where(row < 3, -2.0 * part, 0.0)

    def for_cross(part):
        return jnp.concatenate([-part[3:6], -part[0:3], part[6:8]], 0)

    first = jnp.concatenate([-2.0 * grid[0:3], ones(2)] + square + [none(1)], 0)
    third = jnp.concatenate(square_rest + [none(2), ones(3)], 0)
    parts = (near, far) + (grid, near, far) * 2
    pad = none(KDIM - 88)
    in_square = jnp.concatenate([first, none(8), third] + [for_square(part) for part in parts] + [pad], 0)
    first = jnp.concatenate([-grid[3:6], none(5)], 0)
    second = jnp.concatenate([-grid[0:3], ones(5)], 0)
    third = jnp.concatenate(cross + [none(3)], 0)
    in_cross = jnp.concatenate([first, second, third] + [for_cross(part) for part in parts] + [pad], 0)
    return in_square, in_cross


def source_rows(tile):
    weight = tile[6:7]
    none = jnp.zeros_like(weight)
    sources = jnp.concatenate([weight * tile[0:3], weight, weight * tile[3:6], none], 0)
    return jnp.concatenate(list(pieces(sources)) + [jnp.zeros((SOURCES - 24, tile.shape[1]), F32)], 0)


def kernel(
    lines, planes, pos_hbm, vel_hbm, acc_hbm, jerk_hbm, mass_hbm, level_hbm, index_hbm, result,
    pos, vel, acc, jerk, mass, level, index, stage, fields, actives, arrived, partial,
    left, along, moments, both, high_low, sums,
    load_sem, ready, field_send, field_recv, active_send, active_recv, part_send, part_recv,
):
    group = 2 * planes
    stars, slots = pos.shape[1], index.shape[1]
    tiles = group * slots // TILE
    share = TILE // slots
    wide, s = lax.axis_index("wide"), lax.axis_index("sum")
    z, core = wide // 2, wide % 2
    me = core * planes + s

    def line_peer(k):
        other, bit = z, 1
        while bit < lines:
            other = other + (k // bit) % 2 * bit * (1 - 2 * ((z // bit) % 2))
            bit *= 2
        return other

    def plane_peer(k):
        return (me + 1 + k) % group

    def line_id(other):
        return (other * 2 + core, s)

    def plane_id(other):
        return (z * 2 + other // planes, other % planes)

    loads = [
        pltpu.make_async_copy(source, target, load_sem.at[i])
        for i, (source, target) in enumerate(
            zip((pos_hbm, vel_hbm, acc_hbm, jerk_hbm, mass_hbm, level_hbm, index_hbm), (pos, vel, acc, jerk, mass, level, index))
        )
    ]
    for load in loads:
        load.start()

    barrier = pltpu.get_barrier_semaphore()

    def greet_line(other, carry):
        pl.semaphore_signal(barrier, inc=1, device_id=line_id(other), device_id_type=MESH)
        return carry

    def greet_plane(k, carry):
        pl.semaphore_signal(barrier, inc=1, device_id=plane_id(plane_peer(k)), device_id_type=MESH)
        return carry

    lax.fori_loop(0, group - 1, greet_plane, 0, unroll=True)
    mate = line_peer(1)
    greet_line(mate, 0)
    lax.fori_loop(z // 2 * 2 + 2, lines, greet_line, 0)
    for load in loads:
        load.wait()

    step = step_of(level[...].reshape(1, stars))
    pred_pos, pred_vel = predict(pos[...], vel[...], acc[...], jerk[...], step)
    fields[z, 0:3, :] = pred_pos
    fields[z, 3:6, :] = pred_vel
    fields[z, 6:7, :] = mass[...].reshape(1, stars)
    fields[z, 7:8, :] = jnp.zeros_like(step)

    stage[0:3, :] = pos[...]
    stage[3:6, :] = vel[...]
    stage[6:9, :] = acc[...]
    stage[9:12, :] = jerk[...]
    stage[12:13, :] = step
    stage[13:16, :] = jnp.zeros((3, stars), F32)
    chosen = lax.broadcasted_iota(jnp.int32, (stars, slots), 0) == index[...]
    chosen = chosen.astype(F32).astype(BF16)
    picked = [jnp.dot(part.astype(BF16), chosen, preferred_element_type=F32) for part in pieces(stage[...])]
    picked = (picked[0] + picked[1]) + picked[2]
    result[8:24, :] = picked
    slot_pos, slot_vel = predict(picked[0:3], picked[3:6], picked[6:9], picked[9:12], picked[12:13])
    actives[me] = jnp.zeros((8, LANES), F32)
    actives[me, 0:3, 0:slots] = slot_pos
    actives[me, 3:6, 0:slots] = slot_vel

    pl.semaphore_wait(barrier, group + z // 2 * 2)

    def line_copy(block, other):
        return pltpu.make_async_remote_copy(
            src_ref=fields.at[block], dst_ref=fields.at[block],
            send_sem=field_send.at[other], recv_sem=field_recv.at[block],
            device_id=line_id(other), device_id_type=MESH,
        )

    def plane_copy(block, other, k):
        return pltpu.make_async_remote_copy(
            src_ref=actives.at[block], dst_ref=actives.at[block],
            send_sem=active_send.at[k], recv_sem=active_recv.at[block],
            device_id=plane_id(other), device_id_type=MESH,
        )

    def part_copy(pair, slot, other):
        return pltpu.make_async_remote_copy(
            src_ref=partial.at[pair], dst_ref=arrived.at[slot],
            send_sem=part_send.at[other], recv_sem=part_recv.at[slot],
            device_id=plane_id(other), device_id_type=MESH,
        )

    def send_lower(other, carry):
        pl.semaphore_signal(ready.at[z], inc=1, device_id=line_id(other), device_id_type=MESH)
        line_copy(z, other).start()
        return carry

    def send_higher(other, carry):
        pl.semaphore_wait(ready.at[other], 1)
        line_copy(z, other).start()
        return carry

    def send_plane(k, carry):
        plane_copy(me, plane_peer(k), k).start()
        return carry

    lax.fori_loop(0, group - 1, send_plane, 0, unroll=True)
    line_copy(z, mate).start()
    lax.fori_loop(0, z // 2 * 2, send_lower, 0)

    def take_stars(k, block):
        tile = fields[block]
        at = pl.ds(pl.multiple_of(k * stars, LANES), stars)
        left[at, :] = star_rows(tile).T.astype(BF16)
        moments[:, at] = source_rows(tile).astype(BF16)

    take_stars(0, z)

    def get_plane(k, carry):
        plane_copy(plane_peer(k), plane_peer(k), k).wait_recv()
        return carry

    lax.fori_loop(0, group - 1, get_plane, 0, unroll=True)

    lane = lax.broadcasted_iota(jnp.int32, (8, LANES), 1)

    def take_slots(pair, carry):
        tile = jnp.where(lane < slots, actives[2 * pair], pltpu.roll(actives[2 * pair + 1], slots, 1))
        start = pair * LANES // TILE * 2 * TILE + pair * LANES % TILE
        for offset, value in zip((0, TILE), slot_rows(tile)):
            along[:, pl.ds(pl.multiple_of(start + offset, LANES), LANES)] = value.astype(BF16)
        return carry

    lax.fori_loop(0, group // 2, take_slots, 0, unroll=True)

    line_copy(mate, mate).wait_recv()
    take_stars(1, mate)

    blocks = 2 * stars // TILE
    rounds = lines // 2

    def stars_of(n, b):
        return pl.ds(pl.multiple_of((n * blocks + b) * TILE, TILE), TILE)

    def relate(n, i, b, part):
        rows = pl.ds(pl.multiple_of((n * blocks + b) * TILE + part * PART, PART), PART)
        cols = pl.ds(pl.multiple_of(i * 2 * TILE, 2 * TILE), 2 * TILE)
        return jnp.dot(left[rows, :], along[:, cols], preferred_element_type=F32)

    def keep(b, part, value):
        both[b, part * PART:(part + 1) * PART, :] = value

    def weigh(b, beside):
        for sub in range(0, TILE, ROWS):
            inverse = lax.rsqrt(both[b, sub:sub + ROWS, 0:TILE])
            inverse2 = inverse * inverse
            w = inverse2 * inverse
            sw = (w * inverse2) * both[b, sub:sub + ROWS, TILE:2 * TILE]
            for kind, value in enumerate((w, sw)):
                high = value.astype(BF16)
                high_low[b, kind, sub:sub + ROWS, :] = high
                high_low[b, kind, TILE + sub:TILE + sub + ROWS, :] = (value - high.astype(F32)).astype(BF16)
            beside(sub // ROWS)

    def gain(n, b, kind, part):
        piece = high_low[b, kind, part * TILE:(part + 1) * TILE, :]
        return jnp.dot(moments[:, stars_of(n, b)], piece, preferred_element_type=F32)

    def finish(i):
        by_w, by_s = sums[i, 0], sums[i, 1]
        by_w = by_w[0:8] + by_w[8:16] + by_w[16:24]
        by_s = by_s[0:8] + by_s[8:16] + by_s[16:24]
        row = lax.broadcasted_iota(jnp.int32, by_s.shape, 0)
        terms = by_w + pltpu.roll(jnp.where(row < 4, -3.0 * by_s, 0.0), 4, 0)
        for pair in range(share // 2):
            place = i * (share // 2) + pair
            partial[place] = terms[:, pair * LANES:(pair + 1) * LANES]
            for half in range(2):
                owner = 2 * place + half

                @pl.when(owner != me)
                def _():
                    part_copy(place, me, owner).start()

    def tile_of(j):
        return (me // share + 1 + j) % tiles

    sums[...] = jnp.zeros_like(sums)

    steps = TILE // ROWS
    pieces_of = TILE // PART

    def locate(k):
        return k // tiles, tile_of(k % tiles)

    for part in range(pieces_of):
        keep(0, part, relate(0, tile_of(0), 0, part))

    def two_tiles(pair, carry):
        for k in (2 * pair, 2 * pair + 1):
            n, i = locate(k)
            last_n, last_i = locate(jnp.where(k > 0, k - 1, 0))
            last_i = jnp.where(k > 0, last_i, tiles)
            next_n, next_i = locate(jnp.where(k < rounds * tiles - 1, k + 1, k))
            for b in range(blocks):
                done_n, done_i, done_b = (last_n, last_i, blocks - 1) if b == 0 else (n, i, b - 1)
                soon_n, soon_i, soon_b = (n, i, b + 1) if b < blocks - 1 else (next_n, next_i, 0)

                def beside(step):
                    part, phase = step // (steps // 4), step % (steps // 4)
                    if phase == 1:
                        sums[done_i, part // 2] += gain(done_n, done_b, part // 2, part % 2)
                    if phase == 3 and part % (4 // pieces_of) == 0:
                        keep(soon_b, part * pieces_of // 4, relate(soon_n, soon_i, soon_b, part * pieces_of // 4))

                weigh(b, beside)

        n, j = 2 * pair // tiles, 2 * pair % tiles

        @pl.when(n == rounds - 1)
        def _():
            @pl.when(j > 0)
            def _():
                finish(tile_of(j + tiles - 1))

            finish(tile_of(j))

        @pl.when((n == 0) & (j == 0) & (z // 2 % 2 == 0) & (rounds > 1))
        def _():
            lax.fori_loop(z // 4 * 4 + 2, z // 4 * 4 + 4, send_higher, 0)

        @pl.when((n < rounds - 1) & (j == tiles - 4))
        def _():
            @pl.when(n == 0)
            def _():
                lax.fori_loop(z // 4 * 4 + 4, lines, send_higher, 0)

            for later in (2 * n + 2, 2 * n + 3):
                block = line_peer(later)
                line_copy(block, block).wait_recv()
                take_stars(later, block)

        return carry

    lax.fori_loop(0, rounds * tiles // 2, two_tiles, 0)
    for part in range(4):
        sums[tile_of(tiles - 1), part // 2] += gain(rounds - 1, blocks - 1, part // 2, part % 2)
    finish(tile_of(tiles - 1))

    arrived[me] = partial[me // 2]

    def get_part(k, carry):
        other = plane_peer(k)
        part_copy(other // 2, other, other).wait_recv()
        return carry

    lax.fori_loop(0, group - 1, get_part, 0, unroll=True)
    terms = jnp.sum(arrived[...], axis=0)
    terms = jnp.where(me % 2 == 0, terms, pltpu.roll(terms, slots, 1))
    result[0:8, :] = terms[:, 0:slots]

    def end_line(k, carry):
        line_copy(z, line_peer(k + 1)).wait_send()
        return carry

    def end_plane(k, carry):
        other = plane_peer(k)
        plane_copy(me, other, k).wait_send()
        part_copy(other // 2, me, other).wait_send()
        return carry

    lax.fori_loop(0, lines - 1, end_line, 0, unroll=True)
    lax.fori_loop(0, group - 1, end_plane, 0, unroll=True)


def correct_kernel(result, count, pos_hbm, vel_hbm, acc_hbm, jerk_hbm, pos, vel, acc, jerk, store_sem):
    terms, picked = result[0:8, :], result[8:24, :]
    x0, v0, a0, j0, h = picked[0:3], picked[3:6], picked[6:9], picked[9:12], picked[12:13]
    slot_pos, slot_vel = predict(x0, v0, a0, j0, h)
    new_acc = terms[0:3] - slot_pos * terms[3:4]
    new_jerk = terms[4:7] - slot_vel * terms[3:4] - slot_pos * terms[7:8]
    new_vel = v0 + (a0 + new_acc) * h / 2 + (j0 - new_jerk) * h * h / 12
    new_pos = x0 + (v0 + new_vel) * h / 2 + (a0 - new_acc) * h * h / 12
    live = lax.broadcasted_iota(jnp.int32, new_acc.shape, 1) < count[0]
    stores = []
    for i, (value, held, target) in enumerate(
        ((new_acc, acc, acc_hbm), (new_jerk, jerk, jerk_hbm), (new_vel, vel, vel_hbm), (new_pos, pos, pos_hbm))
    ):
        held[...] = jnp.where(live, value, 0.0)
        stores.append(pltpu.make_async_copy(held, target, store_sem.at[i]))
        stores[-1].start()
    for store in stores:
        store.wait()


def body(lines, planes, pos, vel, acc, jerk, masses, levels, index, count):
    stars, slots, group = pos.shape[1], index.shape[1], 2 * planes
    hbm = pl.BlockSpec(memory_space=pl.ANY)
    tiles, blocks = group * slots // TILE, 2 * stars // TILE
    result = pl.pallas_call(
        functools.partial(kernel, lines, planes),
        out_shape=jax.ShapeDtypeStruct((24, slots), F32),
        in_specs=[hbm] * 7,
        out_specs=pl.BlockSpec(memory_space=pltpu.VMEM),
        scratch_shapes=[
            pltpu.VMEM((3, stars), F32),
            pltpu.VMEM((3, stars), F32),
            pltpu.VMEM((3, stars), F32),
            pltpu.VMEM((3, stars), F32),
            pltpu.VMEM((stars,), F32),
            pltpu.VMEM((stars,), jnp.int32),
            pltpu.VMEM((1, slots), jnp.int32),
            pltpu.VMEM((16, stars), F32),
            pltpu.VMEM((lines, 8, stars), F32),
            pltpu.VMEM((group, 8, LANES), F32),
            pltpu.VMEM((group, 8, LANES), F32),
            pltpu.VMEM((group // 2, 8, LANES), F32),
            pltpu.VMEM((lines * stars, KDIM), BF16),
            pltpu.VMEM((KDIM, 2 * group * slots), BF16),
            pltpu.VMEM((SOURCES, lines * stars), BF16),
            pltpu.VMEM((blocks, TILE, 2 * TILE), F32),
            pltpu.VMEM((blocks, 2, 2 * TILE, TILE), BF16),
            pltpu.VMEM((tiles + 1, 2, SOURCES, TILE), F32),
            pltpu.SemaphoreType.DMA((7,)),
            pltpu.SemaphoreType.REGULAR((lines,)),
            pltpu.SemaphoreType.DMA((lines,)),
            pltpu.SemaphoreType.DMA((lines,)),
            pltpu.SemaphoreType.DMA((group,)),
            pltpu.SemaphoreType.DMA((group,)),
            pltpu.SemaphoreType.DMA((group,)),
            pltpu.SemaphoreType.DMA((group,)),
        ],
        compiler_params=pltpu.CompilerParams(collective_id=0, has_side_effects=True, vmem_limit_bytes=VMEM_LIMIT),
        name="forces",
    )(pos, vel, acc, jerk, masses, levels, index)
    three = jax.ShapeDtypeStruct((3, slots), F32)
    return pl.pallas_call(
        correct_kernel,
        out_shape=(three,) * 4,
        in_specs=[pl.BlockSpec(memory_space=pltpu.VMEM), pl.BlockSpec(memory_space=pltpu.SMEM)],
        out_specs=(hbm,) * 4,
        scratch_shapes=[pltpu.VMEM((3, slots), F32)] * 4 + [pltpu.SemaphoreType.DMA((4,))],
        compiler_params=pltpu.CompilerParams(vmem_limit_bytes=VMEM_LIMIT),
        name="correct",
    )(result, count)


def solution(mesh):
    lines, planes = mesh.shape["wide"] // 2, mesh.shape["sum"]
    both = ("wide", "sum")
    in_specs = (P(None, both),) * 4 + (P(both), P(both), P(both, None), P(both))
    return jax.shard_map(
        functools.partial(body, lines, planes), mesh=mesh, in_specs=in_specs,
        out_specs=(P(None, both),) * 4, check_vma=False,
    )
```

```python
import functools

import jax
import jax.numpy as jnp
from jax import lax
from jax.experimental import pallas as pl
from jax.experimental.pallas import tpu as pltpu
from jax.sharding import PartitionSpec as P

SOFT2 = 0.0025
STEP0 = 0.5
MESH = pl.DeviceIdType.MESH
F32 = jnp.float32
BF16 = jnp.bfloat16
LANES = 128
TILE = 256
PART = 256
KDIM = 128
ROWS = 16
SOURCES = 32
VMEM_LIMIT = 63 * 1024 * 1024


def step_of(levels):
    low = jnp.where(levels == 0, STEP0, STEP0 / 2)
    high = jnp.where(levels == 2, STEP0 / 4, STEP0 / 8)
    return jnp.where(levels < 2, low, high).astype(F32)


def predict(pos, vel, acc, jerk, step):
    pred_pos = pos + step * (vel + step * (acc / 2 + step * jerk / 6))
    pred_vel = vel + step * (acc + step * jerk / 2)
    return pred_pos, pred_vel


def pieces(value):
    first = value.astype(BF16).astype(F32)
    rest = value - first
    second = rest.astype(BF16).astype(F32)
    third = (rest - second).astype(BF16).astype(F32)
    return first, second, third


def split_state(tile):
    row = lax.broadcasted_iota(jnp.int32, tile.shape, 0)
    state = jnp.where(row < 6, tile, 0.0)
    grid = jnp.floor(state * 16.0 + 0.5) * 0.0625
    rest = state - grid
    near = rest.astype(BF16).astype(F32)
    far = (rest - near).astype(BF16).astype(F32)
    return grid, near, far


def own_terms(grid, near, far):
    small = near + far
    gp, gv, sp, sv = grid[0:3], grid[3:6], small[0:3], small[3:6]

    def total(value):
        return jnp.sum(value, axis=0, keepdims=True)

    square, square_rest = total(gp * gp), total(2.0 * gp * sp + sp * sp) + 0.5 * SOFT2
    cross, cross_rest = total(gp * gv), total(gp * sv + sp * gv + sp * sv)
    return list(pieces(square)[:2]), list(pieces(square_rest)), list(pieces(cross)[:2] + pieces(cross_rest))


def star_rows(tile):
    width = tile.shape[1]
    grid, near, far = split_state(tile)
    square, square_rest, cross = own_terms(grid, near, far)

    def ones(count):
        return jnp.ones((count, width), F32)

    first = jnp.concatenate([grid[0:3]] + square + [ones(2), jnp.zeros((1, width), F32)], 0)
    second = jnp.concatenate([grid[3:6]] + cross, 0)
    third = jnp.concatenate([ones(5)] + square_rest, 0)
    pad = jnp.zeros((KDIM - 88, width), F32)
    return jnp.concatenate([first, second, third] + [grid] * 2 + [near] * 3 + [far] * 3 + [pad], 0)


def slot_rows(tile):
    width = tile.shape[1]
    grid, near, far = split_state(tile)
    square, square_rest, cross = own_terms(grid, near, far)
    row = lax.broadcasted_iota(jnp.int32, tile.shape, 0)

    def ones(count):
        return jnp.ones((count, width), F32)

    def none(count):
        return jnp.zeros((count, width), F32)

    def for_square(part):
        return jnp.where(row < 3, -2.0 * part, 0.0)

    def for_cross(part):
        return jnp.concatenate([-part[3:6], -part[0:3], part[6:8]], 0)

    first = jnp.concatenate([-2.0 * grid[0:3], ones(2)] + square + [none(1)], 0)
    third = jnp.concatenate(square_rest + [none(2), ones(3)], 0)
    parts = (near, far) + (grid, near, far) * 2
    pad = none(KDIM - 88)
    in_square = jnp.concatenate([first, none(8), third] + [for_square(part) for part in parts] + [pad], 0)
    first = jnp.concatenate([-grid[3:6], none(5)], 0)
    second = jnp.concatenate([-grid[0:3], ones(5)], 0)
    third = jnp.concatenate(cross + [none(3)], 0)
    in_cross = jnp.concatenate([first, second, third] + [for_cross(part) for part in parts] + [pad], 0)
    return in_square, in_cross


def source_rows(tile):
    weight = tile[6:7]
    none = jnp.zeros_like(weight)
    sources = jnp.concatenate([weight * tile[0:3], weight, weight * tile[3:6], none], 0)
    return jnp.concatenate(list(pieces(sources)) + [jnp.zeros((SOURCES - 24, tile.shape[1]), F32)], 0)


def kernel(
    lines, planes, pos_hbm, vel_hbm, acc_hbm, jerk_hbm, mass_hbm, level_hbm, index_hbm, result,
    pos, vel, acc, jerk, mass, level, index, stage, fields, actives, arrived, partial,
    left, along, moments, both, high_low, sums,
    load_sem, ready, field_send, field_recv, active_send, active_recv, part_send, part_recv,
):
    group = 2 * planes
    stars, slots = pos.shape[1], index.shape[1]
    tiles = group * slots // TILE
    share = TILE // slots
    wide, s = lax.axis_index("wide"), lax.axis_index("sum")
    z, core = wide // 2, wide % 2
    me = core * planes + s

    def line_peer(k):
        other, bit = z, 1
        while bit < lines:
            other = other + (k // bit) % 2 * bit * (1 - 2 * ((z // bit) % 2))
            bit *= 2
        return other

    def plane_peer(k):
        return (me + 1 + k) % group

    def line_id(other):
        return (other * 2 + core, s)

    def plane_id(other):
        return (z * 2 + other // planes, other % planes)

    loads = [
        pltpu.make_async_copy(source, target, load_sem.at[i])
        for i, (source, target) in enumerate(
            zip((pos_hbm, vel_hbm, acc_hbm, jerk_hbm, mass_hbm, level_hbm, index_hbm), (pos, vel, acc, jerk, mass, level, index))
        )
    ]
    for load in loads:
        load.start()

    barrier = pltpu.get_barrier_semaphore()

    def greet_line(other, carry):
        pl.semaphore_signal(barrier, inc=1, device_id=line_id(other), device_id_type=MESH)
        return carry

    def greet_plane(k, carry):
        pl.semaphore_signal(barrier, inc=1, device_id=plane_id(plane_peer(k)), device_id_type=MESH)
        return carry

    lax.fori_loop(0, group - 1, greet_plane, 0, unroll=True)
    mate = line_peer(1)
    greet_line(mate, 0)
    lax.fori_loop(z // 2 * 2 + 2, lines, greet_line, 0)
    for load in loads:
        load.wait()

    step = step_of(level[...].reshape(1, stars))
    pred_pos, pred_vel = predict(pos[...], vel[...], acc[...], jerk[...], step)
    fields[z, 0:3, :] = pred_pos
    fields[z, 3:6, :] = pred_vel
    fields[z, 6:7, :] = mass[...].reshape(1, stars)
    fields[z, 7:8, :] = jnp.zeros_like(step)

    stage[0:3, :] = pos[...]
    stage[3:6, :] = vel[...]
    stage[6:9, :] = acc[...]
    stage[9:12, :] = jerk[...]
    stage[12:13, :] = step
    stage[13:16, :] = jnp.zeros((3, stars), F32)
    chosen = lax.broadcasted_iota(jnp.int32, (stars, slots), 0) == index[...]
    chosen = chosen.astype(F32).astype(BF16)
    picked = [jnp.dot(part.astype(BF16), chosen, preferred_element_type=F32) for part in pieces(stage[...])]
    picked = (picked[0] + picked[1]) + picked[2]
    result[8:24, :] = picked
    slot_pos, slot_vel = predict(picked[0:3], picked[3:6], picked[6:9], picked[9:12], picked[12:13])
    actives[me] = jnp.zeros((8, LANES), F32)
    actives[me, 0:3, 0:slots] = slot_pos
    actives[me, 3:6, 0:slots] = slot_vel

    pl.semaphore_wait(barrier, group + z // 2 * 2)

    def line_copy(block, other):
        return pltpu.make_async_remote_copy(
            src_ref=fields.at[block], dst_ref=fields.at[block],
            send_sem=field_send.at[other], recv_sem=field_recv.at[block],
            device_id=line_id(other), device_id_type=MESH,
        )

    def plane_copy(block, other, k):
        return pltpu.make_async_remote_copy(
            src_ref=actives.at[block], dst_ref=actives.at[block],
            send_sem=active_send.at[k], recv_sem=active_recv.at[block],
            device_id=plane_id(other), device_id_type=MESH,
        )

    def part_copy(pair, slot, other):
        return pltpu.make_async_remote_copy(
            src_ref=partial.at[pair], dst_ref=arrived.at[slot],
            send_sem=part_send.at[other], recv_sem=part_recv.at[slot],
            device_id=plane_id(other), device_id_type=MESH,
        )

    def send_lower(other, carry):
        pl.semaphore_signal(ready.at[z], inc=1, device_id=line_id(other), device_id_type=MESH)
        line_copy(z, other).start()
        return carry

    def send_higher(other, carry):
        pl.semaphore_wait(ready.at[other], 1)
        line_copy(z, other).start()
        return carry

    def send_plane(k, carry):
        plane_copy(me, plane_peer(k), k).start()
        return carry

    lax.fori_loop(0, group - 1, send_plane, 0, unroll=True)
    line_copy(z, mate).start()
    lax.fori_loop(0, z // 2 * 2, send_lower, 0)

    def take_stars(k, block):
        tile = fields[block]
        at = pl.ds(pl.multiple_of(k * stars, LANES), stars)
        left[at, :] = star_rows(tile).T.astype(BF16)
        moments[:, at] = source_rows(tile).astype(BF16)

    take_stars(0, z)

    def get_plane(k, carry):
        plane_copy(plane_peer(k), plane_peer(k), k).wait_recv()
        return carry

    lax.fori_loop(0, group - 1, get_plane, 0, unroll=True)

    lane = lax.broadcasted_iota(jnp.int32, (8, LANES), 1)

    def take_slots(pair, carry):
        tile = jnp.where(lane < slots, actives[2 * pair], pltpu.roll(actives[2 * pair + 1], slots, 1))
        start = pair * LANES // TILE * 2 * TILE + pair * LANES % TILE
        for offset, value in zip((0, TILE), slot_rows(tile)):
            along[:, pl.ds(pl.multiple_of(start + offset, LANES), LANES)] = value.astype(BF16)
        return carry

    lax.fori_loop(0, group // 2, take_slots, 0, unroll=True)

    line_copy(mate, mate).wait_recv()
    take_stars(1, mate)

    blocks = 2 * stars // TILE
    rounds = lines // 2

    def stars_of(n, b):
        return pl.ds(pl.multiple_of((n * blocks + b) * TILE, TILE), TILE)

    def relate(n, i, b, part):
        rows = pl.ds(pl.multiple_of((n * blocks + b) * TILE + part * PART, PART), PART)
        cols = pl.ds(pl.multiple_of(i * 2 * TILE, 2 * TILE), 2 * TILE)
        return jnp.dot(left[rows, :], along[:, cols], preferred_element_type=F32)

    def keep(b, part, value):
        both[b, part * PART:(part + 1) * PART, :] = value

    def weigh(b, beside):
        for sub in range(0, TILE, ROWS):
            inverse = lax.rsqrt(both[b, sub:sub + ROWS, 0:TILE])
            inverse2 = inverse * inverse
            w = inverse2 * inverse
            sw = (w * inverse2) * both[b, sub:sub + ROWS, TILE:2 * TILE]
            for kind, value in enumerate((w, sw)):
                high = value.astype(BF16)
                high_low[b, kind, sub:sub + ROWS, :] = high
                high_low[b, kind, TILE + sub:TILE + sub + ROWS, :] = (value - high.astype(F32)).astype(BF16)
            beside(sub // ROWS)

    def gain(n, b, kind, part):
        piece = high_low[b, kind, part * TILE:(part + 1) * TILE, :]
        return jnp.dot(moments[:, stars_of(n, b)], piece, preferred_element_type=F32)

    def finish(i):
        by_w, by_s = sums[i, 0], sums[i, 1]
        by_w = by_w[0:8] + by_w[8:16] + by_w[16:24]
        by_s = by_s[0:8] + by_s[8:16] + by_s[16:24]
        row = lax.broadcasted_iota(jnp.int32, by_s.shape, 0)
        terms = by_w + pltpu.roll(jnp.where(row < 4, -3.0 * by_s, 0.0), 4, 0)
        for pair in range(share // 2):
            place = i * (share // 2) + pair
            partial[place] = terms[:, pair * LANES:(pair + 1) * LANES]
            for half in range(2):
                owner = 2 * place + half

                @pl.when(owner != me)
                def _():
                    part_copy(place, me, owner).start()

    def tile_of(j):
        return (me // share + 1 + j) % tiles

    sums[...] = jnp.zeros_like(sums)

    steps = TILE // ROWS
    pieces_of = TILE // PART

    def locate(k):
        return k // tiles, tile_of(k % tiles)

    for part in range(pieces_of):
        keep(0, part, relate(0, tile_of(0), 0, part))

    def two_tiles(pair, carry):
        for k in (2 * pair, 2 * pair + 1):
            n, i = locate(k)
            last_n, last_i = locate(jnp.where(k > 0, k - 1, 0))
            last_i = jnp.where(k > 0, last_i, tiles)
            next_n, next_i = locate(jnp.where(k < rounds * tiles - 1, k + 1, k))
            for b in range(blocks):
                done_n, done_i, done_b = (last_n, last_i, blocks - 1) if b == 0 else (n, i, b - 1)
                soon_n, soon_i, soon_b = (n, i, b + 1) if b < blocks - 1 else (next_n, next_i, 0)

                def beside(step):
                    part, phase = step // (steps // 4), step % (steps // 4)
                    if phase == 1:
                        sums[done_i, part // 2] += gain(done_n, done_b, part // 2, part % 2)
                    if phase == 3 and part % (4 // pieces_of) == 0:
                        keep(soon_b, part * pieces_of // 4, relate(soon_n, soon_i, soon_b, part * pieces_of // 4))

                weigh(b, beside)

        n, j = 2 * pair // tiles, 2 * pair % tiles

        @pl.when(n == rounds - 1)
        def _():
            @pl.when(j > 0)
            def _():
                finish(tile_of(j + tiles - 1))

            finish(tile_of(j))

        @pl.when((n == 0) & (j == 0) & (z // 2 % 2 == 0) & (rounds > 1))
        def _():
            lax.fori_loop(z // 4 * 4 + 2, z // 4 * 4 + 4, send_higher, 0)

        @pl.when((n < rounds - 1) & (j == tiles - 4))
        def _():
            @pl.when(n == 0)
            def _():
                lax.fori_loop(z // 4 * 4 + 4, lines, send_higher, 0)

            for later in (2 * n + 2, 2 * n + 3):
                block = line_peer(later)
                line_copy(block, block).wait_recv()
                take_stars(later, block)

        return carry

    lax.fori_loop(0, rounds * tiles // 2, two_tiles, 0)
    for part in range(4):
        sums[tile_of(tiles - 1), part // 2] += gain(rounds - 1, blocks - 1, part // 2, part % 2)
    finish(tile_of(tiles - 1))

    arrived[me] = partial[me // 2]

    def get_part(k, carry):
        other = plane_peer(k)
        part_copy(other // 2, other, other).wait_recv()
        return carry

    lax.fori_loop(0, group - 1, get_part, 0, unroll=True)
    terms = jnp.sum(arrived[...], axis=0)
    terms = jnp.where(me % 2 == 0, terms, pltpu.roll(terms, slots, 1))
    result[0:8, :] = terms[:, 0:slots]

    def end_line(k, carry):
        line_copy(z, line_peer(k + 1)).wait_send()
        return carry

    def end_plane(k, carry):
        other = plane_peer(k)
        plane_copy(me, other, k).wait_send()
        part_copy(other // 2, me, other).wait_send()
        return carry

    lax.fori_loop(0, lines - 1, end_line, 0, unroll=True)
    lax.fori_loop(0, group - 1, end_plane, 0, unroll=True)


def correct_kernel(result, count, pos_hbm, vel_hbm, acc_hbm, jerk_hbm, pos, vel, acc, jerk, store_sem):
    terms, picked = result[0:8, :], result[8:24, :]
    x0, v0, a0, j0, h = picked[0:3], picked[3:6], picked[6:9], picked[9:12], picked[12:13]
    slot_pos, slot_vel = predict(x0, v0, a0, j0, h)
    new_acc = terms[0:3] - slot_pos * terms[3:4]
    new_jerk = terms[4:7] - slot_vel * terms[3:4] - slot_pos * terms[7:8]
    new_vel = v0 + (a0 + new_acc) * h / 2 + (j0 - new_jerk) * h * h / 12
    new_pos = x0 + (v0 + new_vel) * h / 2 + (a0 - new_acc) * h * h / 12
    live = lax.broadcasted_iota(jnp.int32, new_acc.shape, 1) < count[0]
    stores = []
    for i, (value, held, target) in enumerate(
        ((new_acc, acc, acc_hbm), (new_jerk, jerk, jerk_hbm), (new_vel, vel, vel_hbm), (new_pos, pos, pos_hbm))
    ):
        held[...] = jnp.where(live, value, 0.0)
        stores.append(pltpu.make_async_copy(held, target, store_sem.at[i]))
        stores[-1].start()
    for store in stores:
        store.wait()


def body(lines, planes, pos, vel, acc, jerk, masses, levels, index, count):
    stars, slots, group = pos.shape[1], index.shape[1], 2 * planes
    hbm = pl.BlockSpec(memory_space=pl.ANY)
    tiles, blocks = group * slots // TILE, 2 * stars // TILE
    result = pl.pallas_call(
        functools.partial(kernel, lines, planes),
        out_shape=jax.ShapeDtypeStruct((24, slots), F32),
        in_specs=[hbm] * 7,
        out_specs=pl.BlockSpec(memory_space=pltpu.VMEM),
        scratch_shapes=[
            pltpu.VMEM((3, stars), F32),
            pltpu.VMEM((3, stars), F32),
            pltpu.VMEM((3, stars), F32),
            pltpu.VMEM((3, stars), F32),
            pltpu.VMEM((stars,), F32),
            pltpu.VMEM((stars,), jnp.int32),
            pltpu.VMEM((1, slots), jnp.int32),
            pltpu.VMEM((16, stars), F32),
            pltpu.VMEM((lines, 8, stars), F32),
            pltpu.VMEM((group, 8, LANES), F32),
            pltpu.VMEM((group, 8, LANES), F32),
            pltpu.VMEM((group // 2, 8, LANES), F32),
            pltpu.VMEM((lines * stars, KDIM), BF16),
            pltpu.VMEM((KDIM, 2 * group * slots), BF16),
            pltpu.VMEM((SOURCES, lines * stars), BF16),
            pltpu.VMEM((blocks, TILE, 2 * TILE), F32),
            pltpu.VMEM((blocks, 2, 2 * TILE, TILE), BF16),
            pltpu.VMEM((tiles + 1, 2, SOURCES, TILE), F32),
            pltpu.SemaphoreType.DMA((7,)),
            pltpu.SemaphoreType.REGULAR((lines,)),
            pltpu.SemaphoreType.DMA((lines,)),
            pltpu.SemaphoreType.DMA((lines,)),
            pltpu.SemaphoreType.DMA((group,)),
            pltpu.SemaphoreType.DMA((group,)),
            pltpu.SemaphoreType.DMA((group,)),
            pltpu.SemaphoreType.DMA((group,)),
        ],
        compiler_params=pltpu.CompilerParams(collective_id=0, has_side_effects=True, vmem_limit_bytes=VMEM_LIMIT),
        name="forces",
    )(pos, vel, acc, jerk, masses, levels, index)
    three = jax.ShapeDtypeStruct((3, slots), F32)
    return pl.pallas_call(
        correct_kernel,
        out_shape=(three,) * 4,
        in_specs=[pl.BlockSpec(memory_space=pltpu.VMEM), pl.BlockSpec(memory_space=pltpu.SMEM)],
        out_specs=(hbm,) * 4,
        scratch_shapes=[pltpu.VMEM((3, slots), F32)] * 4 + [pltpu.SemaphoreType.DMA((4,))],
        compiler_params=pltpu.CompilerParams(vmem_limit_bytes=VMEM_LIMIT),
        name="correct",
    )(result, count)


def solution(mesh):
    lines, planes = mesh.shape["wide"] // 2, mesh.shape["sum"]
    both = ("wide", "sum")
    in_specs = (P(None, both),) * 4 + (P(both), P(both), P(both, None), P(both))
    return jax.shard_map(
        functools.partial(body, lines, planes), mesh=mesh, in_specs=in_specs,
        out_specs=(P(None, both),) * 4, check_vma=False,
    )
```

```python
import functools

import jax
import jax.numpy as jnp
from jax import lax
from jax.experimental import pallas as pl
from jax.experimental.pallas import tpu as pltpu
from jax.sharding import PartitionSpec as P

SOFT2 = 0.0025
STEP0 = 0.5
MESH = pl.DeviceIdType.MESH
F32 = jnp.float32
BF16 = jnp.bfloat16
LANES = 128
TILE = 256
PART = 256
KDIM = 128
ROWS = 32
SOURCES = 32
VMEM_LIMIT = 63 * 1024 * 1024


def step_of(levels):
    low = jnp.where(levels == 0, STEP0, STEP0 / 2)
    high = jnp.where(levels == 2, STEP0 / 4, STEP0 / 8)
    return jnp.where(levels < 2, low, high).astype(F32)


def predict(pos, vel, acc, jerk, step):
    pred_pos = pos + step * (vel + step * (acc / 2 + step * jerk / 6))
    pred_vel = vel + step * (acc + step * jerk / 2)
    return pred_pos, pred_vel


def pieces(value):
    first = value.astype(BF16).astype(F32)
    rest = value - first
    second = rest.astype(BF16).astype(F32)
    third = (rest - second).astype(BF16).astype(F32)
    return first, second, third


def split_state(tile):
    row = lax.broadcasted_iota(jnp.int32, tile.shape, 0)
    state = jnp.where(row < 6, tile, 0.0)
    grid = jnp.floor(state * 16.0 + 0.5) * 0.0625
    rest = state - grid
    near = rest.astype(BF16).astype(F32)
    far = (rest - near).astype(BF16).astype(F32)
    return grid, near, far


def own_terms(grid, near, far):
    small = near + far
    gp, gv, sp, sv = grid[0:3], grid[3:6], small[0:3], small[3:6]

    def total(value):
        return jnp.sum(value, axis=0, keepdims=True)

    square, square_rest = total(gp * gp), total(2.0 * gp * sp + sp * sp) + 0.5 * SOFT2
    cross, cross_rest = total(gp * gv), total(gp * sv + sp * gv + sp * sv)
    return list(pieces(square)[:2]), list(pieces(square_rest)), list(pieces(cross)[:2] + pieces(cross_rest))


def star_rows(tile):
    width = tile.shape[1]
    grid, near, far = split_state(tile)
    square, square_rest, cross = own_terms(grid, near, far)

    def ones(count):
        return jnp.ones((count, width), F32)

    first = jnp.concatenate([grid[0:3]] + square + [ones(2), jnp.zeros((1, width), F32)], 0)
    second = jnp.concatenate([grid[3:6]] + cross, 0)
    third = jnp.concatenate([ones(5)] + square_rest, 0)
    pad = jnp.zeros((KDIM - 88, width), F32)
    return jnp.concatenate([first, second, third] + [grid] * 2 + [near] * 3 + [far] * 3 + [pad], 0)


def slot_rows(tile):
    width = tile.shape[1]
    grid, near, far = split_state(tile)
    square, square_rest, cross = own_terms(grid, near, far)
    row = lax.broadcasted_iota(jnp.int32, tile.shape, 0)

    def ones(count):
        return jnp.ones((count, width), F32)

    def none(count):
        return jnp.zeros((count, width), F32)

    def for_square(part):
        return jnp.where(row < 3, -2.0 * part, 0.0)

    def for_cross(part):
        return jnp.concatenate([-part[3:6], -part[0:3], part[6:8]], 0)

    first = jnp.concatenate([-2.0 * grid[0:3], ones(2)] + square + [none(1)], 0)
    third = jnp.concatenate(square_rest + [none(2), ones(3)], 0)
    parts = (near, far) + (grid, near, far) * 2
    pad = none(KDIM - 88)
    in_square = jnp.concatenate([first, none(8), third] + [for_square(part) for part in parts] + [pad], 0)
    first = jnp.concatenate([-grid[3:6], none(5)], 0)
    second = jnp.concatenate([-grid[0:3], ones(5)], 0)
    third = jnp.concatenate(cross + [none(3)], 0)
    in_cross = jnp.concatenate([first, second, third] + [for_cross(part) for part in parts] + [pad], 0)
    return in_square, in_cross


def source_rows(tile):
    weight = tile[6:7]
    none = jnp.zeros_like(weight)
    sources = jnp.concatenate([weight * tile[0:3], weight, weight * tile[3:6], none], 0)
    return jnp.concatenate(list(pieces(sources)) + [jnp.zeros((SOURCES - 24, tile.shape[1]), F32)], 0)


def kernel(
    lines, planes, pos_hbm, vel_hbm, acc_hbm, jerk_hbm, mass_hbm, level_hbm, index_hbm, result,
    pos, vel, acc, jerk, mass, level, index, stage, fields, actives, arrived, partial,
    left, along, moments, both, high_low, sums,
    load_sem, ready, field_send, field_recv, active_send, active_recv, part_send, part_recv,
):
    group = 2 * planes
    stars, slots = pos.shape[1], index.shape[1]
    tiles = group * slots // TILE
    share = TILE // slots
    wide, s = lax.axis_index("wide"), lax.axis_index("sum")
    z, core = wide // 2, wide % 2
    me = core * planes + s

    def line_peer(k):
        other, bit = z, 1
        while bit < lines:
            other = other + (k // bit) % 2 * bit * (1 - 2 * ((z // bit) % 2))
            bit *= 2
        return other

    def plane_peer(k):
        return (me + 1 + k) % group

    def line_id(other):
        return (other * 2 + core, s)

    def plane_id(other):
        return (z * 2 + other // planes, other % planes)

    loads = [
        pltpu.make_async_copy(source, target, load_sem.at[i])
        for i, (source, target) in enumerate(
            zip((pos_hbm, vel_hbm, acc_hbm, jerk_hbm, mass_hbm, level_hbm, index_hbm), (pos, vel, acc, jerk, mass, level, index))
        )
    ]
    for load in loads:
        load.start()

    barrier = pltpu.get_barrier_semaphore()

    def greet_line(other, carry):
        pl.semaphore_signal(barrier, inc=1, device_id=line_id(other), device_id_type=MESH)
        return carry

    def greet_plane(k, carry):
        pl.semaphore_signal(barrier, inc=1, device_id=plane_id(plane_peer(k)), device_id_type=MESH)
        return carry

    lax.fori_loop(0, group - 1, greet_plane, 0, unroll=True)
    mate = line_peer(1)
    greet_line(mate, 0)
    lax.fori_loop(z // 2 * 2 + 2, lines, greet_line, 0)
    for load in loads:
        load.wait()

    step = step_of(level[...].reshape(1, stars))
    pred_pos, pred_vel = predict(pos[...], vel[...], acc[...], jerk[...], step)
    fields[z, 0:3, :] = pred_pos
    fields[z, 3:6, :] = pred_vel
    fields[z, 6:7, :] = mass[...].reshape(1, stars)
    fields[z, 7:8, :] = jnp.zeros_like(step)

    stage[0:3, :] = pos[...]
    stage[3:6, :] = vel[...]
    stage[6:9, :] = acc[...]
    stage[9:12, :] = jerk[...]
    stage[12:13, :] = step
    stage[13:16, :] = jnp.zeros((3, stars), F32)
    chosen = lax.broadcasted_iota(jnp.int32, (stars, slots), 0) == index[...]
    chosen = chosen.astype(F32).astype(BF16)
    picked = [jnp.dot(part.astype(BF16), chosen, preferred_element_type=F32) for part in pieces(stage[...])]
    picked = (picked[0] + picked[1]) + picked[2]
    result[8:24, :] = picked
    slot_pos, slot_vel = predict(picked[0:3], picked[3:6], picked[6:9], picked[9:12], picked[12:13])
    actives[me] = jnp.zeros((8, LANES), F32)
    actives[me, 0:3, 0:slots] = slot_pos
    actives[me, 3:6, 0:slots] = slot_vel

    pl.semaphore_wait(barrier, group + z // 2 * 2)

    def line_copy(block, other):
        return pltpu.make_async_remote_copy(
            src_ref=fields.at[block], dst_ref=fields.at[block],
            send_sem=field_send.at[other], recv_sem=field_recv.at[block],
            device_id=line_id(other), device_id_type=MESH,
        )

    def plane_copy(block, other, k):
        return pltpu.make_async_remote_copy(
            src_ref=actives.at[block], dst_ref=actives.at[block],
            send_sem=active_send.at[k], recv_sem=active_recv.at[block],
            device_id=plane_id(other), device_id_type=MESH,
        )

    def part_copy(pair, slot, other):
        return pltpu.make_async_remote_copy(
            src_ref=partial.at[pair], dst_ref=arrived.at[slot],
            send_sem=part_send.at[other], recv_sem=part_recv.at[slot],
            device_id=plane_id(other), device_id_type=MESH,
        )

    def send_lower(other, carry):
        pl.semaphore_signal(ready.at[z], inc=1, device_id=line_id(other), device_id_type=MESH)
        line_copy(z, other).start()
        return carry

    def send_higher(other, carry):
        pl.semaphore_wait(ready.at[other], 1)
        line_copy(z, other).start()
        return carry

    def send_plane(k, carry):
        plane_copy(me, plane_peer(k), k).start()
        return carry

    lax.fori_loop(0, group - 1, send_plane, 0, unroll=True)
    line_copy(z, mate).start()
    lax.fori_loop(0, z // 2 * 2, send_lower, 0)

    def take_stars(k, block):
        tile = fields[block]
        at = pl.ds(pl.multiple_of(k * stars, LANES), stars)
        left[at, :] = star_rows(tile).T.astype(BF16)
        moments[:, at] = source_rows(tile).astype(BF16)

    take_stars(0, z)

    def get_plane(k, carry):
        plane_copy(plane_peer(k), plane_peer(k), k).wait_recv()
        return carry

    lax.fori_loop(0, group - 1, get_plane, 0, unroll=True)

    lane = lax.broadcasted_iota(jnp.int32, (8, LANES), 1)

    def take_slots(pair, carry):
        tile = jnp.where(lane < slots, actives[2 * pair], pltpu.roll(actives[2 * pair + 1], slots, 1))
        start = pair * LANES // TILE * 2 * TILE + pair * LANES % TILE
        for offset, value in zip((0, TILE), slot_rows(tile)):
            along[:, pl.ds(pl.multiple_of(start + offset, LANES), LANES)] = value.astype(BF16)
        return carry

    lax.fori_loop(0, group // 2, take_slots, 0, unroll=True)

    line_copy(mate, mate).wait_recv()
    take_stars(1, mate)

    blocks = 2 * stars // TILE
    rounds = lines // 2

    def stars_of(n, b):
        return pl.ds(pl.multiple_of((n * blocks + b) * TILE, TILE), TILE)

    def relate(n, i, b, part):
        rows = pl.ds(pl.multiple_of((n * blocks + b) * TILE + part * PART, PART), PART)
        cols = pl.ds(pl.multiple_of(i * 2 * TILE, 2 * TILE), 2 * TILE)
        return jnp.dot(left[rows, :], along[:, cols], preferred_element_type=F32)

    def keep(b, part, value):
        both[b, part * PART:(part + 1) * PART, :] = value

    def weigh(b, beside):
        for sub in range(0, TILE, ROWS):
            inverse = lax.rsqrt(both[b, sub:sub + ROWS, 0:TILE])
            inverse2 = inverse * inverse
            w = inverse2 * inverse
            sw = (w * inverse2) * both[b, sub:sub + ROWS, TILE:2 * TILE]
            for kind, value in enumerate((w, sw)):
                high = value.astype(BF16)
                high_low[b, kind, sub:sub + ROWS, :] = high
                high_low[b, kind, TILE + sub:TILE + sub + ROWS, :] = (value - high.astype(F32)).astype(BF16)
            beside(sub // ROWS)

    def gain(n, b, kind, part):
        piece = high_low[b, kind, part * TILE:(part + 1) * TILE, :]
        return jnp.dot(moments[:, stars_of(n, b)], piece, preferred_element_type=F32)

    def finish(i):
        by_w, by_s = sums[i, 0], sums[i, 1]
        by_w = by_w[0:8] + by_w[8:16] + by_w[16:24]
        by_s = by_s[0:8] + by_s[8:16] + by_s[16:24]
        row = lax.broadcasted_iota(jnp.int32, by_s.shape, 0)
        terms = by_w + pltpu.roll(jnp.where(row < 4, -3.0 * by_s, 0.0), 4, 0)
        for pair in range(share // 2):
            place = i * (share // 2) + pair
            partial[place] = terms[:, pair * LANES:(pair + 1) * LANES]
            for half in range(2):
                owner = 2 * place + half

                @pl.when(owner != me)
                def _():
                    part_copy(place, me, owner).start()

    def tile_of(j):
        return (me // share + 1 + j) % tiles

    sums[...] = jnp.zeros_like(sums)

    steps = TILE // ROWS
    pieces_of = TILE // PART

    def locate(k):
        return k // tiles, tile_of(k % tiles)

    for part in range(pieces_of):
        keep(0, part, relate(0, tile_of(0), 0, part))

    def two_tiles(pair, carry):
        for k in (2 * pair, 2 * pair + 1):
            n, i = locate(k)
            last_n, last_i = locate(jnp.where(k > 0, k - 1, 0))
            last_i = jnp.where(k > 0, last_i, tiles)
            next_n, next_i = locate(jnp.where(k < rounds * tiles - 1, k + 1, k))
            for b in range(blocks):
                done_n, done_i, done_b = (last_n, last_i, blocks - 1) if b == 0 else (n, i, b - 1)
                soon_n, soon_i, soon_b = (n, i, b + 1) if b < blocks - 1 else (next_n, next_i, 0)

                def beside(step):
                    part, phase = step // (steps // 4), step % (steps // 4)
                    if phase == 1:
                        sums[done_i, part // 2] += gain(done_n, done_b, part // 2, part % 2)
                    if phase == steps // 4 - 1 and part % (4 // pieces_of) == 0:
                        keep(soon_b, part * pieces_of // 4, relate(soon_n, soon_i, soon_b, part * pieces_of // 4))

                weigh(b, beside)

        n, j = 2 * pair // tiles, 2 * pair % tiles

        @pl.when(n == rounds - 1)
        def _():
            @pl.when(j > 0)
            def _():
                finish(tile_of(j + tiles - 1))

            finish(tile_of(j))

        @pl.when((n == 0) & (j == 0) & (z // 2 % 2 == 0) & (rounds > 1))
        def _():
            lax.fori_loop(z // 4 * 4 + 2, z // 4 * 4 + 4, send_higher, 0)

        @pl.when((n < rounds - 1) & (j == tiles - 4))
        def _():
            @pl.when(n == 0)
            def _():
                lax.fori_loop(z // 4 * 4 + 4, lines, send_higher, 0)

            for later in (2 * n + 2, 2 * n + 3):
                block = line_peer(later)
                line_copy(block, block).wait_recv()
                take_stars(later, block)

        return carry

    lax.fori_loop(0, rounds * tiles // 2, two_tiles, 0)
    for part in range(4):
        sums[tile_of(tiles - 1), part // 2] += gain(rounds - 1, blocks - 1, part // 2, part % 2)
    finish(tile_of(tiles - 1))

    arrived[me] = partial[me // 2]

    def get_part(k, carry):
        other = plane_peer(k)
        part_copy(other // 2, other, other).wait_recv()
        return carry

    lax.fori_loop(0, group - 1, get_part, 0, unroll=True)
    terms = jnp.sum(arrived[...], axis=0)
    terms = jnp.where(me % 2 == 0, terms, pltpu.roll(terms, slots, 1))
    result[0:8, :] = terms[:, 0:slots]

    def end_line(k, carry):
        line_copy(z, line_peer(k + 1)).wait_send()
        return carry

    def end_plane(k, carry):
        other = plane_peer(k)
        plane_copy(me, other, k).wait_send()
        part_copy(other // 2, me, other).wait_send()
        return carry

    lax.fori_loop(0, lines - 1, end_line, 0, unroll=True)
    lax.fori_loop(0, group - 1, end_plane, 0, unroll=True)


def correct_kernel(result, count, pos_hbm, vel_hbm, acc_hbm, jerk_hbm, pos, vel, acc, jerk, store_sem):
    terms, picked = result[0:8, :], result[8:24, :]
    x0, v0, a0, j0, h = picked[0:3], picked[3:6], picked[6:9], picked[9:12], picked[12:13]
    slot_pos, slot_vel = predict(x0, v0, a0, j0, h)
    new_acc = terms[0:3] - slot_pos * terms[3:4]
    new_jerk = terms[4:7] - slot_vel * terms[3:4] - slot_pos * terms[7:8]
    new_vel = v0 + (a0 + new_acc) * h / 2 + (j0 - new_jerk) * h * h / 12
    new_pos = x0 + (v0 + new_vel) * h / 2 + (a0 - new_acc) * h * h / 12
    live = lax.broadcasted_iota(jnp.int32, new_acc.shape, 1) < count[0]
    stores = []
    for i, (value, held, target) in enumerate(
        ((new_acc, acc, acc_hbm), (new_jerk, jerk, jerk_hbm), (new_vel, vel, vel_hbm), (new_pos, pos, pos_hbm))
    ):
        held[...] = jnp.where(live, value, 0.0)
        stores.append(pltpu.make_async_copy(held, target, store_sem.at[i]))
        stores[-1].start()
    for store in stores:
        store.wait()


def body(lines, planes, pos, vel, acc, jerk, masses, levels, index, count):
    stars, slots, group = pos.shape[1], index.shape[1], 2 * planes
    hbm = pl.BlockSpec(memory_space=pl.ANY)
    tiles, blocks = group * slots // TILE, 2 * stars // TILE
    result = pl.pallas_call(
        functools.partial(kernel, lines, planes),
        out_shape=jax.ShapeDtypeStruct((24, slots), F32),
        in_specs=[hbm] * 7,
        out_specs=pl.BlockSpec(memory_space=pltpu.VMEM),
        scratch_shapes=[
            pltpu.VMEM((3, stars), F32),
            pltpu.VMEM((3, stars), F32),
            pltpu.VMEM((3, stars), F32),
            pltpu.VMEM((3, stars), F32),
            pltpu.VMEM((stars,), F32),
            pltpu.VMEM((stars,), jnp.int32),
            pltpu.VMEM((1, slots), jnp.int32),
            pltpu.VMEM((16, stars), F32),
            pltpu.VMEM((lines, 8, stars), F32),
            pltpu.VMEM((group, 8, LANES), F32),
            pltpu.VMEM((group, 8, LANES), F32),
            pltpu.VMEM((group // 2, 8, LANES), F32),
            pltpu.VMEM((lines * stars, KDIM), BF16),
            pltpu.VMEM((KDIM, 2 * group * slots), BF16),
            pltpu.VMEM((SOURCES, lines * stars), BF16),
            pltpu.VMEM((blocks, TILE, 2 * TILE), F32),
            pltpu.VMEM((blocks, 2, 2 * TILE, TILE), BF16),
            pltpu.VMEM((tiles + 1, 2, SOURCES, TILE), F32),
            pltpu.SemaphoreType.DMA((7,)),
            pltpu.SemaphoreType.REGULAR((lines,)),
            pltpu.SemaphoreType.DMA((lines,)),
            pltpu.SemaphoreType.DMA((lines,)),
            pltpu.SemaphoreType.DMA((group,)),
            pltpu.SemaphoreType.DMA((group,)),
            pltpu.SemaphoreType.DMA((group,)),
            pltpu.SemaphoreType.DMA((group,)),
        ],
        compiler_params=pltpu.CompilerParams(collective_id=0, has_side_effects=True, vmem_limit_bytes=VMEM_LIMIT),
        name="forces",
    )(pos, vel, acc, jerk, masses, levels, index)
    three = jax.ShapeDtypeStruct((3, slots), F32)
    return pl.pallas_call(
        correct_kernel,
        out_shape=(three,) * 4,
        in_specs=[pl.BlockSpec(memory_space=pltpu.VMEM), pl.BlockSpec(memory_space=pltpu.SMEM)],
        out_specs=(hbm,) * 4,
        scratch_shapes=[pltpu.VMEM((3, slots), F32)] * 4 + [pltpu.SemaphoreType.DMA((4,))],
        compiler_params=pltpu.CompilerParams(vmem_limit_bytes=VMEM_LIMIT),
        name="correct",
    )(result, count)


def solution(mesh):
    lines, planes = mesh.shape["wide"] // 2, mesh.shape["sum"]
    both = ("wide", "sum")
    in_specs = (P(None, both),) * 4 + (P(both), P(both), P(both, None), P(both))
    return jax.shard_map(
        functools.partial(body, lines, planes), mesh=mesh, in_specs=in_specs,
        out_specs=(P(None, both),) * 4, check_vma=False,
    )
```
